32 devices in a mesh: rep: 4 (over z), fsdp: 8 (over y, x, core).
Axes of the slice: x: 2, y: 2, z: 4, core: 2. Of those that a mesh axis runs over, the one named last changes fastest.
Arguments:
- tokens: bfloat16 [32768, 768], P(('rep', 'fsdp')), may hold values from -6 to 6
- cotangent: bfloat16 [32768, 768], P(('rep', 'fsdp')), may hold values from -6 to 6
- lengths: int32 [256], P(('rep', 'fsdp')), may hold values from 32 to 128, as said below
- w_attn: float32 [768, 3072], P('fsdp')
- w_in: float32 [768, 3072], P('fsdp'), may hold values from -0.21875 to 0.21875
- w_out: float32 [3072, 768], P('fsdp'), may hold values from -0.109375 to 0.109375
- b_in: float32 [3072], P('fsdp'), may hold values from -1.8 to 1.8
- vecs: float32 [8, 768], P(None, 'fsdp')
- m_attn: float32 [768, 3072], P('fsdp'), may hold values from -6 to 6
- m_in: float32 [768, 3072], P('fsdp'), may hold values from -6 to 6
- m_out: float32 [3072, 768], P('fsdp'), may hold values from -6 to 6
- m_bin: float32 [3072], P('fsdp'), may hold values from -6 to 6
- m_vecs: float32 [8, 768], P(None, 'fsdp'), may hold values from -6 to 6
- v_attn: float32 [768, 3072], P('fsdp'), may hold values from 1 to 100
- v_in: float32 [768, 3072], P('fsdp'), may hold values from 1 to 100
- v_out: float32 [3072, 768], P('fsdp'), may hold values from 1 to 100
- v_bin: float32 [3072], P('fsdp'), may hold values from 1 to 100
- v_vecs: float32 [8, 768], P(None, 'fsdp'), may hold values from 1 to 100
Outputs:
- output: bfloat16 [32768, 768], P(('rep', 'fsdp'))
- grad_tokens: bfloat16 [32768, 768], P(('rep', 'fsdp'))
- grad_attn: float32 [768, 3072], P('fsdp')
- grad_in: float32 [768, 3072], P('fsdp')
- grad_out: float32 [3072, 768], P('fsdp')
- grad_bin: float32 [3072], P('fsdp')
- grad_vecs: float32 [8, 768], P(None, 'fsdp')
- step_attn: float32 [768, 3072], P('fsdp')
- step_in: float32 [768, 3072], P('fsdp')
- step_out: float32 [3072, 768], P('fsdp')
- step_bin: float32 [3072], P('fsdp')
- step_vecs: float32 [8, 768], P(None, 'fsdp')
- mom_attn: float32 [768, 3072], P('fsdp')
- mom_in: float32 [768, 3072], P('fsdp')
- mom_out: float32 [3072, 768], P('fsdp')
- mom_bin: float32 [3072], P('fsdp')
- mom_vecs: float32 [8, 768], P(None, 'fsdp')
- sq_attn: float32 [768, 3072], P('fsdp')
- sq_in: float32 [768, 3072], P('fsdp')
- sq_out: float32 [3072, 768], P('fsdp')
- sq_bin: float32 [3072], P('fsdp')
- sq_vecs: float32 [8, 768], P(None, 'fsdp')
The draws below stay inside these ranges and needn't reach their ends.
Inputs may be any that keep to these rules, and one draw needn't show every extreme that they name: `lengths`: each pair has at least 32 valid rows; on every device one of its 8 pairs fills all 128 rows.
All inputs are finite; a program needn't handle non-finite values.
Results may differ from the reference program's by a relative error of at most 0.017.
The reference program's roundings to bfloat16 on the way count: a program that leaves them out, or rounds other values in their place, can miss the bound.
Values may be sent and summed in bfloat16 or wider, within the bound.
No kernel may reach another device: no remote copies, remote signals or barrier semaphores. Data moves between devices by JAX's collectives and lax.ppermute only.
A program may use at most 192 MiB of HBM per device.

```python
import math
import jax
import jax.numpy as jnp
from jax import lax

D = 768
HEADS = 12
HDIM = 64
FF = 3072
SEQ = 128
STEP = 5
SEQ_DEV = 8
SEQS = 256
TOKENS = 32768


def draw_lengths(key, part):
    key = jax.random.fold_in(key, 11)
    drawn = jax.random.randint(key, (SEQS,), SEQ // 4, SEQ + 1)
    picked = jax.random.randint(jax.random.fold_in(key, 5), (SEQS // SEQ_DEV,), 0, SEQ_DEV)
    position = jnp.arange(SEQS)
    full_slot = jnp.repeat(picked, SEQ_DEV, total_repeat_length=SEQS)
    return jnp.where(position % SEQ_DEV == full_slot, SEQ, drawn).astype(jnp.int32)


def draw_w_attn(key, part):
    key = jax.random.fold_in(key, 12)
    noise = jax.random.normal(key, (D, 4 * D), jnp.float32)
    column = jnp.arange(4 * D)[None, :]
    factor = jnp.where(column >= 3 * D, 4.0, 1.0)
    return noise * factor * D ** (-0.5)


def draw_vecs(key, part):
    key = jax.random.fold_in(key, 13)
    noise = jax.random.normal(key, (8, D), jnp.float32)
    row_index = jnp.arange(8)[:, None]
    is_gain = (row_index == 3) | (row_index == 6)
    return jnp.where(is_gain, 1.0 + 0.1 * noise, 0.3 * noise)


def block_levels(own_key, extent, pieces, least, largest):
    loudness, own = 1.0, jax.random.fold_in(own_key, 6)
    for dim, parts in pieces:
        steps = jnp.exp(jax.random.uniform(jax.random.fold_in(own, dim), (parts,), jnp.float32, least / len(pieces), largest / len(pieces)))
        loudness = loudness * jnp.repeat(steps, extent[dim] // parts).reshape([-1 if axis == dim else 1 for axis in range(len(extent))])
    return loudness


def scatter_about(stream_key, extent, spread, reach, shards=(), kind=jnp.bfloat16):
    values = spread * jax.random.normal(stream_key, extent, jnp.float32)
    if shards:
        values = values * block_levels(stream_key, extent, shards, -0.22, 0.18)
    return jnp.clip(values, -reach, reach).astype(kind)


def setup_inputs(seed: int = 0) -> dict:
    arg_keys = jax.random.split(jax.random.key(seed), 19)
    return {
        "tokens": scatter_about(arg_keys[0], (TOKENS, D), 1.0, 6.0, ((0, 32),)),
        "cotangent": scatter_about(arg_keys[1], (TOKENS, D), 1.0, 6.0, ((0, 32),)),
        "lengths": draw_lengths(jax.random.fold_in(arg_keys[18], 71), 0),
        "w_attn": draw_w_attn(jax.random.fold_in(arg_keys[18], 71), 0),
        "w_in": scatter_about(arg_keys[4], (D, FF), D ** -0.5, 0.21875, ((0, 8),), jnp.float32),
        "w_out": scatter_about(arg_keys[5], (FF, D), FF ** -0.5, 0.109375, ((0, 8),), jnp.float32),
        "b_in": scatter_about(arg_keys[6], (FF,), 0.3, 1.8, ((0, 8),), jnp.float32),
        "vecs": draw_vecs(jax.random.fold_in(arg_keys[18], 71), 0),
        "m_attn": scatter_about(arg_keys[8], (D, 4 * D), 1.0, 6.0, ((0, 8),), jnp.float32),
        "m_in": scatter_about(arg_keys[9], (D, FF), 1.0, 6.0, ((0, 8),), jnp.float32),
        "m_out": scatter_about(arg_keys[10], (FF, D), 1.0, 6.0, ((0, 8),), jnp.float32),
        "m_bin": scatter_about(arg_keys[11], (FF,), 1.0, 6.0, ((0, 8),), jnp.float32),
        "m_vecs": scatter_about(arg_keys[12], (8, D), 1.0, 6.0, ((1, 8),), jnp.float32),
        "v_attn": jnp.clip(jnp.exp(math.log(100.0) - 4.6051702 * jax.random.uniform(arg_keys[13], (D, 4 * D), jnp.float32) ** block_levels(arg_keys[13], (D, 4 * D), ((0, 8),), -0.2, 0.2)), 1.0, 100.0),
        "v_in": jnp.clip(jnp.exp(math.log(100.0) - 4.6051702 * jax.random.uniform(arg_keys[14], (D, FF), jnp.float32) ** block_levels(arg_keys[14], (D, FF), ((0, 8),), -0.2, 0.2)), 1.0, 100.0),
        "v_out": jnp.clip(jnp.exp(math.log(100.0) - 4.6051702 * jax.random.uniform(arg_keys[15], (FF, D), jnp.float32) ** block_levels(arg_keys[15], (FF, D), ((0, 8),), -0.2, 0.2)), 1.0, 100.0),
        "v_bin": jnp.clip(jnp.exp(math.log(100.0) - 4.6051702 * jax.random.uniform(arg_keys[16], (FF,), jnp.float32) ** block_levels(arg_keys[16], (FF,), ((0, 8),), -0.2, 0.2)), 1.0, 100.0),
        "v_vecs": jnp.clip(jnp.exp(math.log(100.0) - 4.6051702 * jax.random.uniform(arg_keys[17], (8, D), jnp.float32) ** block_levels(arg_keys[17], (8, D), ((1, 8),), -0.2, 0.2)), 1.0, 100.0),
    }


@jax.custom_vjp
def low(v):
    return lax.optimization_barrier(v.astype(jnp.bfloat16)).astype(jnp.float32)

@jax.custom_vjp
def low_back(v):
    return v

def low_keep(v):
    return (low(v), None)

def low_pass(kept, grad):
    return (grad,)

def back_keep(v):
    return (v, None)

def back_low(kept, grad):
    return (low(grad),)
low.defvjp(low_keep, low_pass)
low_back.defvjp(back_keep, back_low)
beta_one = 0.9
beta_two = 0.999
adam_epsilon = 1e-06
norm_epsilon = 1e-05
masked_score = -1000000000.0

def normalize(residual):
    centre = residual - lax.optimization_barrier(jnp.mean(residual, axis=-1, keepdims=True))
    variance = lax.optimization_barrier(jnp.mean(centre * centre, axis=-1, keepdims=True))
    return centre * lax.rsqrt(variance + norm_epsilon)

def matmul(left, right):
    return jnp.dot(left, right, precision=lax.Precision.HIGHEST, preferred_element_type=jnp.float32)

def forward(source, lengths, params):
    attn_mat, in_mat, out_mat, in_bias, vectors = [low(entry) for entry in params]
    row_count = source.shape[0]
    seq_count = lengths.shape[0]
    head_shape = (seq_count, SEQ, HEADS, HDIM)
    projected = matmul(source, attn_mat[:, :3 * D])
    queries = low(low_back(projected[:, :D] + vectors[0])).reshape(head_shape)
    key_rows = low(low_back(projected[:, D:2 * D])).reshape(head_shape)
    value_rows = low(low_back(projected[:, 2 * D:] + vectors[1])).reshape(head_shape)
    scores = jnp.einsum('bqhd,bkhd->bhqk', queries, key_rows, precision=lax.Precision.HIGHEST) * HDIM ** (-0.5)
    valid_keys = jnp.arange(SEQ)[None, :] < lengths[:, None]
    scores = low_back(jnp.where(valid_keys[:, None, None, :], scores, masked_score))
    attn_weights = jax.nn.softmax(scores, axis=-1)
    attended = jnp.einsum('bhqk,bkhd->bqhd', low(attn_weights), value_rows, precision=lax.Precision.HIGHEST)
    attended = low(low_back(attended.reshape(row_count, D)))
    branch = low_back(matmul(attended, attn_mat[:, 3 * D:]) + vectors[2])
    hidden = normalize(source + branch) * vectors[3] + vectors[4]
    pre_act = low_back(matmul(low(hidden), in_mat) + in_bias)
    activated = low(jax.nn.gelu(pre_act, approximate=False))
    ffn_out = low_back(matmul(activated, out_mat) + vectors[5])
    return normalize(hidden + ffn_out) * vectors[6] + vectors[7]

def adamw(moment, square, gradient, first_fix, second_fix):
    moment = beta_one * moment + (1.0 - beta_one) * gradient
    square = beta_two * square + (1.0 - beta_two) * gradient * gradient
    update = moment / first_fix / (jnp.sqrt(square / second_fix) + adam_epsilon)
    return (update, moment, square)

def reference(tokens, cotangent, lengths, w_attn, w_in, w_out, b_in, vecs, m_attn, m_in, m_out, m_bin, m_vecs, v_attn, v_in, v_out, v_bin, v_vecs):
    params = (w_attn, w_in, w_out, b_in, vecs)
    block_rows = SEQ_DEV * SEQ
    blocks = tokens.shape[0] // block_rows
    sources = tokens.astype(jnp.float32).reshape(blocks, block_rows, D)
    cot_blocks = cotangent.astype(jnp.float32).reshape(blocks, block_rows, D)
    length_blocks = lengths.reshape(blocks, SEQ_DEV)

    def one_block(totals, block_items):
        source, block_lengths, cot_block = block_items

        def run_block(values_in, weights):
            return forward(values_in, block_lengths, weights)
        result, pullback = jax.vjp(run_block, source, params)
        grad_source, grad_params = pullback(cot_block)
        totals = jax.tree.map(lambda a, b: a + b, totals, grad_params)
        return (totals, (result, grad_source))
    empty_grads = tuple((jnp.zeros_like(entry) for entry in params))
    gradients, (results, grad_sources) = lax.scan(one_block, empty_grads, (sources, length_blocks, cot_blocks))
    first_fix = 1.0 - beta_one ** STEP
    second_fix = 1.0 - beta_two ** STEP
    step_attn, mom_attn, sq_attn = adamw(m_attn, v_attn, gradients[0], first_fix, second_fix)
    step_in, mom_in, sq_in = adamw(m_in, v_in, gradients[1], first_fix, second_fix)
    step_out, mom_out, sq_out = adamw(m_out, v_out, gradients[2], first_fix, second_fix)
    step_bin, mom_bin, sq_bin = adamw(m_bin, v_bin, gradients[3], first_fix, second_fix)
    step_vecs, mom_vecs, sq_vecs = adamw(m_vecs, v_vecs, gradients[4], first_fix, second_fix)
    output = results.reshape(-1, D).astype(jnp.bfloat16)
    grad_tokens = grad_sources.reshape(-1, D).astype(jnp.bfloat16)
    return (output, grad_tokens, gradients[0], gradients[1], gradients[2], gradients[3], gradients[4], step_attn, step_in, step_out, step_bin, step_vecs, mom_attn, mom_in, mom_out, mom_bin, mom_vecs, sq_attn, sq_in, sq_out, sq_bin, sq_vecs)
```

```python
import functools

import jax
import jax.numpy as jnp
from jax import lax
from jax.experimental import pallas as pl
from jax.experimental.pallas import tpu as pltpu
from jax.sharding import PartitionSpec as P

D = 768
HEADS = 12
HDIM = 64
FF = 3072
SEQ = 128
STEP = 5

RANKS = 8
SHARD = D // RANKS
SHARD_FF = FF // RANKS

beta_one = 0.9
beta_two = 0.999
adam_epsilon = 1e-06
norm_epsilon = 1e-05
masked_score = -1000000000.0

bf16 = jnp.bfloat16
f32 = jnp.float32
NN = (((1,), (0,)), ((), ()))
NT = (((1,), (1,)), ((), ()))
TN = (((0,), (0,)), ((), ()))
VMEM_BYTES = 56 * 1024 * 1024
TILE = 256


def dot(left, right, dims):
    return lax.dot_general(left, right, dims, preferred_element_type=f32)


def call(kernel, grid, in_specs, out_specs, out_shape, scratch=(), flops=0, bytes_accessed=0, name=None):
    return pl.pallas_call(
        kernel,
        grid_spec=pltpu.PrefetchScalarGridSpec(
            num_scalar_prefetch=1,
            grid=grid,
            in_specs=in_specs,
            out_specs=out_specs,
            scratch_shapes=list(scratch),
        ),
        out_shape=out_shape,
        compiler_params=pltpu.CompilerParams(
            vmem_limit_bytes=VMEM_BYTES, dimension_semantics=("arbitrary",) * len(grid)
        ),
        cost_estimate=pl.CostEstimate(
            flops=int(flops), bytes_accessed=int(bytes_accessed), transcendentals=0
        ),
        name=name,
    )


def rows_of(width, tile=TILE):
    return pl.BlockSpec((tile, width), lambda i, s: (i, 0))


def whole(shape):
    return pl.BlockSpec(shape, lambda i, s: (0,) * len(shape))


ANY = pl.BlockSpec(memory_space=pl.ANY)


class Pieces:
    def __init__(self, arrays, places):
        self.arrays = list(arrays)
        self.places = places

    def __len__(self):
        return len(self.arrays)


def load_weight(pieces, me, refs, scratch, sem):
    copies = []
    for ref, place in zip(refs, pieces.places):
        if place is None:
            target = scratch
        else:
            mask, first, count = place
            target = scratch.at[me ^ mask, pl.ds(first, count)]
        copies.append(pltpu.make_async_copy(ref, target, sem))
    for copy in copies:
        copy.start()
    for copy in copies:
        copy.wait()


def lane_sum(value):
    return jnp.sum(value, axis=-1, keepdims=True)


def normalize(residual):
    centre = residual - lane_sum(residual) * (1.0 / D)
    variance = lane_sum(centre * centre) * (1.0 / D)
    inv_std = lax.rsqrt(variance + norm_epsilon)
    return (centre * inv_std, inv_std)


def norm_back(grad_normed, normed, inv_std):
    first_mean = lane_sum(grad_normed) * (1.0 / D)
    second_mean = lane_sum(grad_normed * normed) * (1.0 / D)
    return inv_std * (grad_normed - first_mean - normed * second_mean)


def gelu_and_slope(pre_act):
    cumulative = 0.5 * (1.0 + lax.erf(pre_act * 0.7071067811865476))
    density = jnp.exp(-0.5 * pre_act * pre_act) * 0.3989422804014327
    return (pre_act * cumulative, cumulative + pre_act * density)


def project_qkv(me, tokens, weight, bias):
    rows = tokens.shape[0]
    count = len(weight)

    def kernel(s, x_ref, b_ref, *rest):
        refs, (out_ref, w_ref, sem) = rest[:count], rest[count:]

        @pl.when(pl.program_id(0) == 0)
        def _():
            load_weight(weight, s[0], refs, w_ref, sem)

        j = pl.multiple_of(pl.program_id(0) * 256, 256)
        w = w_ref[:, :, pl.ds(j, 256)].reshape(D, 256)
        out_ref[...] = (dot(x_ref[...], w, NN) + b_ref[...]).astype(bf16)

    return call(
        kernel,
        (3 * D // 256,),
        [whole((rows, D)), pl.BlockSpec((1, 256), lambda j, s: (0, j))] + [ANY] * count,
        pl.BlockSpec((rows, 256), lambda j, s: (0, j)),
        jax.ShapeDtypeStruct((rows, 3 * D), bf16),
        [pltpu.VMEM((RANKS, SHARD, 3 * D), bf16), pltpu.SemaphoreType.DMA],
        flops=2 * rows * D * 3 * D,
        bytes_accessed=2 * (rows * D * 4 + 3 * D * D),
        name="qkv",
    )(me, tokens, bias, *weight.arrays)


def head_masks():
    lane = lax.broadcasted_iota(jnp.int32, (SEQ, 2 * HDIM), 1)
    return lane < HDIM


def stack_heads(value, first):
    zero = jnp.zeros_like(value)
    return jnp.concatenate([jnp.where(first, value, zero), jnp.where(first, zero, value)], axis=0)


def attention(lengths, qkv):
    rows = qkv.shape[0]
    pairs = rows // SEQ
    scale = HDIM ** (-0.5)

    def kernel(s, qkv_ref, out_ref, p_ref):
        length = s[pl.program_id(0)]
        first = head_masks()
        valid = lax.broadcasted_iota(jnp.int32, (SEQ, SEQ), 1) < length
        for h in range(HEADS // 2):
            lanes = slice(h * 2 * HDIM, (h + 1) * 2 * HDIM)
            q = qkv_ref[:, lanes]
            k = qkv_ref[:, D + h * 2 * HDIM : D + (h + 1) * 2 * HDIM]
            v = qkv_ref[:, 2 * D + h * 2 * HDIM : 2 * D + (h + 1) * 2 * HDIM]
            scores = dot(q, stack_heads(k, first), NT) * scale
            halves = []
            for part in range(2):
                one = jnp.where(valid, scores[:, part * SEQ : (part + 1) * SEQ], masked_score)
                top = jnp.max(one, axis=-1, keepdims=True)
                raised = jnp.exp(one - top)
                halves.append(raised / lane_sum(raised))
            weights = jnp.concatenate(halves, axis=1)
            p_ref[:, h * 2 * SEQ : (h + 1) * 2 * SEQ] = weights
            out_ref[:, lanes] = dot(weights.astype(bf16), stack_heads(v, first), NN).astype(bf16)

    return call(
        kernel,
        (pairs,),
        [rows_of(3 * D, SEQ)],
        [rows_of(D, SEQ), rows_of(HEADS * SEQ, SEQ)],
        [
            jax.ShapeDtypeStruct((rows, D), bf16),
            jax.ShapeDtypeStruct((rows, HEADS * SEQ), f32),
        ],
        flops=8e9,
        bytes_accessed=rows * (3 * D * 2 + D * 2 + HEADS * SEQ * 4),
        name="attention",
    )(lengths, qkv)


def feed_in(me, attended, tokens, weight, vectors, in_bias):
    rows = tokens.shape[0]
    count = len(weight)
    tile = 512

    def kernel(s, o_ref, x_ref, v_ref, b_ref, *rest):
        refs = rest[:count]
        n1_ref, inv_ref, hb_ref, f_ref, sl_ref, w_ref, sem = rest[count:]

        @pl.when(pl.program_id(0) == 0)
        def _():
            load_weight(weight, s[0], refs, w_ref, sem)

        w_proj = w_ref[:, :, :D].reshape(D, D)
        branch = dot(o_ref[...], w_proj, NN) + v_ref[2:3, :]
        normed, inv_std = normalize(x_ref[...].astype(f32) + branch)
        n1_ref[...] = normed
        inv_ref[...] = inv_std
        low = (normed * v_ref[3:4, :] + v_ref[4:5, :]).astype(bf16)
        hb_ref[...] = low
        for j in range(FF // tile):
            w = w_ref[:, :, D + j * tile : D + (j + 1) * tile].reshape(D, tile)
            pre_act = dot(low, w, NN) + b_ref[:, j * tile : (j + 1) * tile]
            act, slope = gelu_and_slope(pre_act)
            f_ref[:, j * tile : (j + 1) * tile] = act.astype(bf16)
            sl_ref[:, j * tile : (j + 1) * tile] = slope.astype(bf16)

    return call(
        kernel,
        (rows // TILE,),
        [rows_of(D), rows_of(D), whole((8, D)), whole((1, FF))] + [ANY] * count,
        [rows_of(D), rows_of(1), rows_of(D), rows_of(FF), rows_of(FF)],
        [
            jax.ShapeDtypeStruct((rows, D), f32),
            jax.ShapeDtypeStruct((rows, 1), f32),
            jax.ShapeDtypeStruct((rows, D), bf16),
            jax.ShapeDtypeStruct((rows, FF), bf16),
            jax.ShapeDtypeStruct((rows, FF), bf16),
        ],
        [pltpu.VMEM((RANKS, SHARD, D + FF), bf16), pltpu.SemaphoreType.DMA],
        flops=2 * rows * D * (D + FF),
        bytes_accessed=rows * (D * 10 + FF * 4) + 2 * D * (D + FF),
        name="feed_in",
    )(me, attended, tokens, vectors, in_bias, *weight.arrays)


def feed_out(me, activated, normed_one, cotangent, weight, vectors):
    rows = activated.shape[0]
    count = len(weight)

    def kernel(s, f_ref, n1_ref, g_ref, v_ref, *rest):
        refs = rest[:count]
        y_ref, dr_ref, dz_ref, sums_ref, w_ref, sem = rest[count:]

        @pl.when(pl.program_id(0) == 0)
        def _():
            load_weight(weight, s[0], refs, w_ref, sem)
            sums_ref[...] = jnp.zeros_like(sums_ref)

        branch = dot(f_ref[...], w_ref[...].reshape(FF, D), NN) + v_ref[5:6, :]
        hidden = n1_ref[...] * v_ref[3:4, :] + v_ref[4:5, :]
        normed, inv_std = normalize(hidden + branch)
        y_ref[...] = (normed * v_ref[6:7, :] + v_ref[7:8, :]).astype(bf16)
        grad_y = g_ref[...].astype(f32)
        sums_ref[1:2, :] += jnp.sum(grad_y * normed, axis=0, keepdims=True)
        sums_ref[2:3, :] += jnp.sum(grad_y, axis=0, keepdims=True)
        grad_res = norm_back(grad_y * v_ref[6:7, :], normed, inv_std)
        dr_ref[...] = grad_res
        low = grad_res.astype(bf16)
        dz_ref[...] = low
        sums_ref[0:1, :] += jnp.sum(low.astype(f32), axis=0, keepdims=True)

    return call(
        kernel,
        (rows // TILE,),
        [rows_of(FF), rows_of(D), rows_of(D), whole((8, D))] + [ANY] * count,
        [rows_of(D), rows_of(D), rows_of(D), whole((8, D))],
        [
            jax.ShapeDtypeStruct((rows, D), bf16),
            jax.ShapeDtypeStruct((rows, D), f32),
            jax.ShapeDtypeStruct((rows, D), bf16),
            jax.ShapeDtypeStruct((8, D), f32),
        ],
        [pltpu.VMEM((RANKS, SHARD_FF, D), bf16), pltpu.SemaphoreType.DMA],
        flops=2 * rows * D * FF,
        bytes_accessed=rows * (D * 14 + FF * 2) + 2 * D * FF,
        name="feed_out",
    )(me, activated, normed_one, cotangent, vectors, *weight.arrays)


def grad_w_out(me, activated, grad_ffn):
    rows = activated.shape[0]
    half = RANKS // 2

    def rank(step, s):
        core = s[0] & 1
        slot = jnp.where(step < half, step, step - half)
        chip = (s[0] >> 1) ^ slot
        return chip * 2 + jnp.where(step < half, 1 - core, core)

    def kernel(s, f_ref, dz_ref, t_ref, m_ref):
        step = pl.program_id(0)
        block = dot(f_ref[...], dz_ref[...], TN).astype(bf16)

        @pl.when(step < half)
        def _():
            t_ref[0] = block

        @pl.when(step >= half)
        def _():
            m_ref[0] = block

    shape = jax.ShapeDtypeStruct((half, SHARD_FF, D), bf16)
    return call(
        kernel,
        (RANKS,),
        [pl.BlockSpec((rows, SHARD_FF), lambda i, s: (0, rank(i, s))), whole((rows, D))],
        [
            pl.BlockSpec((1, SHARD_FF, D), lambda i, s: (jnp.minimum(i, half - 1), 0, 0)),
            pl.BlockSpec((1, SHARD_FF, D), lambda i, s: (jnp.maximum(i - half, 0), 0, 0)),
        ],
        [shape, shape],
        flops=2 * rows * D * FF,
        bytes_accessed=rows * (D * 2 + FF * 2) + 2 * D * FF,
        name="grad_w_out",
    )(me, activated, grad_ffn)


def back_out(me, grad_ffn, slope, weight):
    rows = grad_ffn.shape[0]
    count = len(weight)

    def kernel(s, dz_ref, sl_ref, *rest):
        refs = rest[:count]
        du_ref, sums_ref, w_ref, sem = rest[count:]

        @pl.when(pl.program_id(0) == 0)
        def _():
            load_weight(weight, s[0], refs, w_ref, sem)
            sums_ref[...] = jnp.zeros_like(sums_ref)

        dz = dz_ref[...]
        for r in range(RANKS):
            lanes = slice(r * SHARD_FF, (r + 1) * SHARD_FF)
            grad = dot(dz, w_ref[r], NT) * sl_ref[:, lanes].astype(f32)
            low = grad.astype(bf16)
            du_ref[:, lanes] = low
            sums_ref[:, lanes] += jnp.sum(low.astype(f32), axis=0, keepdims=True)

    return call(
        kernel,
        (rows // TILE,),
        [rows_of(D), rows_of(FF)] + [ANY] * count,
        [rows_of(FF), whole((1, FF))],
        [jax.ShapeDtypeStruct((rows, FF), bf16), jax.ShapeDtypeStruct((1, FF), f32)],
        [pltpu.VMEM((RANKS, SHARD_FF, D), bf16), pltpu.SemaphoreType.DMA],
        flops=2 * rows * D * FF,
        bytes_accessed=rows * (D * 2 + FF * 4) + 2 * D * FF,
        name="back_out",
    )(me, grad_ffn, slope, *weight.arrays)


def back_in(me, grad_pre, grad_res_two, normed_one, inv_one, weight, vectors):
    rows = grad_pre.shape[0]
    count = len(weight)

    def kernel(s, du_ref, dr2_ref, n1_ref, inv_ref, v_ref, *rest):
        refs = rest[:count]
        dr1_ref, da_ref, do_ref, sums_ref, w_ref, sem = rest[count:]

        @pl.when(pl.program_id(0) == 0)
        def _():
            load_weight(weight, s[0], refs, w_ref, sem)
            sums_ref[...] = jnp.zeros_like(sums_ref)

        w_in = w_ref[:, :, D:].reshape(D, FF)
        grad_hidden = dot(du_ref[...], w_in, NT) + dr2_ref[...]
        normed = n1_ref[...]
        sums_ref[1:2, :] += jnp.sum(grad_hidden * normed, axis=0, keepdims=True)
        sums_ref[2:3, :] += jnp.sum(grad_hidden, axis=0, keepdims=True)
        grad_res = norm_back(grad_hidden * v_ref[3:4, :], normed, inv_ref[...])
        dr1_ref[...] = grad_res
        low = grad_res.astype(bf16)
        da_ref[...] = low
        sums_ref[0:1, :] += jnp.sum(low.astype(f32), axis=0, keepdims=True)
        w_proj = w_ref[:, :, :D].reshape(D, D)
        do_ref[...] = dot(low, w_proj, NT).astype(bf16)

    return call(
        kernel,
        (rows // TILE,),
        [rows_of(FF), rows_of(D), rows_of(D), rows_of(1), whole((8, D))] + [ANY] * count,
        [rows_of(D), rows_of(D), rows_of(D), whole((8, D))],
        [
            jax.ShapeDtypeStruct((rows, D), f32),
            jax.ShapeDtypeStruct((rows, D), bf16),
            jax.ShapeDtypeStruct((rows, D), bf16),
            jax.ShapeDtypeStruct((8, D), f32),
        ],
        [pltpu.VMEM((RANKS, SHARD, D + FF), bf16), pltpu.SemaphoreType.DMA],
        flops=2 * rows * D * (D + FF),
        bytes_accessed=rows * (D * 16 + FF * 2) + 2 * D * (D + FF),
        name="back_in",
    )(me, grad_pre, grad_res_two, normed_one, inv_one, vectors, *weight.arrays)


def store_by_rank(s, block, t_ref, m_ref):
    core, chip = s[0] & 1, s[0] >> 1
    for r in range(RANKS):
        part = block[r * SHARD : (r + 1) * SHARD]
        slot = chip ^ (r >> 1)

        @pl.when(core == (r & 1))
        def _():
            m_ref[slot] = part

        @pl.when(core != (r & 1))
        def _():
            t_ref[slot] = part


def grad_w_in(me, attended, grad_branch, hidden_low, grad_pre):
    rows = attended.shape[0]
    half = RANKS // 2
    tile = 384
    lead = D // tile

    def kernel(s, o_ref, da_ref, h_ref, du_ref, t_ref, m_ref, left_ref):
        step = pl.program_id(0)

        @pl.when(step == 0)
        def _():
            left_ref[...] = o_ref[...].T

        @pl.when(step == lead)
        def _():
            left_ref[...] = h_ref[...].T

        right = jnp.where(step < lead, da_ref[...], du_ref[...])
        store_by_rank(s, dot(left_ref[...], right, NN).astype(bf16), t_ref, m_ref)

    shape = jax.ShapeDtypeStruct((half, SHARD, D + FF), bf16)
    out = pl.BlockSpec((half, SHARD, tile), lambda i, s: (0, 0, i))
    return call(
        kernel,
        ((D + FF) // tile,),
        [
            whole((rows, D)),
            pl.BlockSpec((rows, tile), lambda i, s: (0, jnp.minimum(i, lead - 1))),
            whole((rows, D)),
            pl.BlockSpec((rows, tile), lambda i, s: (0, jnp.maximum(i - lead, 0))),
        ],
        [out, out],
        [shape, shape],
        [pltpu.VMEM((D, rows), bf16)],
        flops=2 * rows * D * (D + FF),
        bytes_accessed=rows * (D * 4 + FF * 2) + 2 * D * (D + FF),
        name="grad_w_in",
    )(me, attended, grad_branch, hidden_low, grad_pre)


def attention_back(lengths, qkv, weights, grad_attended):
    rows = qkv.shape[0]
    pairs = rows // SEQ
    scale = HDIM ** (-0.5)

    def kernel(s, qkv_ref, p_ref, do_ref, out_ref, sums_ref):
        @pl.when(pl.program_id(0) == 0)
        def _():
            sums_ref[...] = jnp.zeros_like(sums_ref)

        first = head_masks()
        for h in range(HEADS // 2):
            lanes = slice(h * 2 * HDIM, (h + 1) * 2 * HDIM)
            k_lanes = slice(D + h * 2 * HDIM, D + (h + 1) * 2 * HDIM)
            v_lanes = slice(2 * D + h * 2 * HDIM, 2 * D + (h + 1) * 2 * HDIM)
            q, k, v = qkv_ref[:, lanes], qkv_ref[:, k_lanes], qkv_ref[:, v_lanes]
            grad_out = do_ref[:, lanes]
            p = p_ref[:, h * 2 * SEQ : (h + 1) * 2 * SEQ]
            grad_p = dot(grad_out, stack_heads(v, first), NT)
            both = grad_p * p
            halves = []
            for part in range(2):
                cut = slice(part * SEQ, (part + 1) * SEQ)
                halves.append((p[:, cut] * (grad_p[:, cut] - lane_sum(both[:, cut]))).astype(bf16))
            grad_s = jnp.concatenate(halves, axis=1)
            grad_v = dot(p.astype(bf16), grad_out, TN)
            grad_v = jnp.where(first, grad_v[:SEQ], grad_v[SEQ:]).astype(bf16)
            grad_q = (dot(grad_s, stack_heads(k, first), NN) * scale).astype(bf16)
            grad_k = dot(grad_s, q, TN)
            grad_k = (jnp.where(first, grad_k[:SEQ], grad_k[SEQ:]) * scale).astype(bf16)
            out_ref[:, lanes] = grad_q
            out_ref[:, k_lanes] = grad_k
            out_ref[:, v_lanes] = grad_v
            sums_ref[0:1, lanes] += jnp.sum(grad_q.astype(f32), axis=0, keepdims=True)
            sums_ref[1:2, lanes] += jnp.sum(grad_v.astype(f32), axis=0, keepdims=True)

    return call(
        kernel,
        (pairs,),
        [rows_of(3 * D, SEQ), rows_of(HEADS * SEQ, SEQ), rows_of(D, SEQ)],
        [rows_of(3 * D, SEQ), whole((8, D))],
        [jax.ShapeDtypeStruct((rows, 3 * D), bf16), jax.ShapeDtypeStruct((8, D), f32)],
        flops=14e9,
        bytes_accessed=rows * (3 * D * 4 + D * 2 + HEADS * SEQ * 4),
        name="attention_back",
    )(lengths, qkv, weights, grad_attended)


def grad_w_qkv(me, tokens, grad_mixed):
    rows = tokens.shape[0]
    half = RANKS // 2
    tile = 384

    def kernel(s, x_ref, g_ref, t_ref, m_ref, left_ref):
        @pl.when(pl.program_id(0) == 0)
        def _():
            left_ref[...] = x_ref[...].T

        store_by_rank(s, dot(left_ref[...], g_ref[...], NN).astype(bf16), t_ref, m_ref)

    shape = jax.ShapeDtypeStruct((half, SHARD, 3 * D), bf16)
    out = pl.BlockSpec((half, SHARD, tile), lambda i, s: (0, 0, i))
    return call(
        kernel,
        (3 * D // tile,),
        [whole((rows, D)), pl.BlockSpec((rows, tile), lambda i, s: (0, i))],
        [out, out],
        [shape, shape],
        [pltpu.VMEM((D, rows), bf16)],
        flops=2 * rows * D * 3 * D,
        bytes_accessed=rows * (D * 8) + 2 * D * 3 * D,
        name="grad_w_qkv",
    )(me, tokens, grad_mixed)


def back_qkv(me, grad_mixed, grad_res_one, weight):
    rows = grad_mixed.shape[0]
    count = len(weight)

    def kernel(s, g_ref, dr_ref, *rest):
        refs = rest[:count]
        out_ref, w_ref, sem = rest[count:]

        @pl.when(pl.program_id(0) == 0)
        def _():
            load_weight(weight, s[0], refs, w_ref, sem)

        w = w_ref[...].reshape(D, 3 * D)
        out_ref[...] = (dot(g_ref[...], w, NT) + dr_ref[...]).astype(bf16)

    return call(
        kernel,
        (rows // TILE,),
        [rows_of(3 * D), rows_of(D)] + [ANY] * count,
        rows_of(D),
        jax.ShapeDtypeStruct((rows, D), bf16),
        [pltpu.VMEM((RANKS, SHARD, 3 * D), bf16), pltpu.SemaphoreType.DMA],
        flops=2 * rows * D * 3 * D,
        bytes_accessed=rows * D * 12 + 2 * D * 3 * D,
        name="back_qkv",
    )(me, grad_mixed, grad_res_one, *weight.arrays)


def adamw_math(moment, square, gradient):
    first_fix = 1.0 - beta_one**STEP
    second_fix = 1.0 - beta_two**STEP
    moment = beta_one * moment + (1.0 - beta_one) * gradient
    square = beta_two * square + (1.0 - beta_two) * gradient * gradient
    update = moment / first_fix / (jnp.sqrt(square / second_fix) + adam_epsilon)
    return (update, moment, square)


def adamw(moment, square, gradient):
    gradient = gradient.astype(f32)
    return (gradient,) + adamw_math(moment, square, gradient)


def flip(bit):
    return [(i, i ^ bit) for i in range(RANKS)]


def swap(value, bit):
    return lax.ppermute(value, "fsdp", flip(bit))


def gather_chunk(shard):
    half = shard.shape[0] // 2
    from_x = swap(shard, 2)
    from_y = swap(shard, 4)
    far_a = swap(from_x[:half], 4)
    far_b = swap(from_y[half:], 2)
    mine = [shard, from_x, from_y, far_a, far_b]
    places = [
        (0, 0, 2 * half),
        (2, 0, 2 * half),
        (4, 0, 2 * half),
        (6, 0, half),
        (6, half, half),
    ]
    other = [swap(piece, 1) for piece in mine]
    return Pieces(mine + other, places + [(m ^ 1, first, count) for m, first, count in places])


def low_sum(*values):
    total = values[0].astype(f32)
    for value in values[1:]:
        total = total + value.astype(f32)
    return total.astype(bf16)


def scatter_chunk(theirs, mine):
    half = mine.shape[1] // 2
    got = swap(theirs, 1)
    send_x = low_sum(mine[1::2, :half], got[1::2, :half])
    send_y = low_sum(mine[2:, half:], got[2:, half:])
    got_x = swap(send_x, 2)
    got_y = swap(send_y, 4)
    last_y = swap(low_sum(mine[2, :half], got[2, :half], got_x[1]), 4)
    last_x = swap(low_sum(mine[1, half:], got[1, half:], got_y[1]), 2)
    return jnp.concatenate(
        [
            low_sum(mine[0, :half], got[0, :half], got_x[0], last_y),
            low_sum(mine[0, half:], got[0, half:], got_y[0], last_x),
        ],
        axis=0,
    )


def sum_over_copies(owned, rep_index):
    near = low_sum(owned, lax.ppermute(owned, "rep", [(0, 1), (3, 2)]))
    total = low_sum(near, lax.ppermute(near, "rep", [(1, 2), (2, 1)]))
    back = lax.ppermute(total, "rep", [(1, 0), (2, 3)])
    inner = (rep_index == 1) | (rep_index == 2)
    return jnp.where(inner, total, back)


def gather_small(value, me):
    for position, bit in enumerate((1, 2, 4)):
        got = swap(value, bit)
        low_first = ((me >> position) & 1) == 0
        value = jnp.where(
            low_first, jnp.concatenate([value, got]), jnp.concatenate([got, value])
        )
    return value


def local(
    fsdp,
    rep,
    tokens,
    cotangent,
    lengths,
    w_attn,
    w_in,
    w_out,
    b_in,
    vecs,
    m_attn,
    m_in,
    m_out,
    m_bin,
    m_vecs,
    v_attn,
    v_in,
    v_out,
    v_bin,
    v_vecs,
):
    direct = fsdp == RANKS and rep == 4
    position = lax.axis_index("fsdp")
    rep_index = lax.axis_index("rep")
    part = D // fsdp
    low_qkv = w_attn[:, : 3 * D].astype(bf16)
    low_in = jnp.concatenate([w_attn[:, 3 * D :], w_in], axis=1).astype(bf16)
    low_out = w_out.astype(bf16)
    small = jnp.concatenate([vecs.reshape(1, -1), b_in.reshape(1, -1)], axis=1).astype(bf16)
    if direct:
        me = position.reshape(1)
        pieces_qkv = gather_chunk(low_qkv)
        small_all = gather_small(small, position)
        pieces_in = gather_chunk(low_in)
        pieces_out = gather_chunk(low_out)
    else:
        me = jnp.zeros((1,), jnp.int32)

        def gather(shard):
            full = lax.all_gather(shard, "fsdp", axis=0, tiled=True)
            return Pieces([full.reshape(RANKS, -1, full.shape[1])], [None])

        pieces_qkv, pieces_in, pieces_out = gather(low_qkv), gather(low_in), gather(low_out)
        small_all = lax.all_gather(small, "fsdp", axis=0, tiled=True)
    small_all = small_all.astype(f32)
    vectors = small_all[:, : 8 * part].reshape(fsdp, 8, part).transpose(1, 0, 2).reshape(8, D)
    in_bias = small_all[:, 8 * part :].reshape(1, FF)
    mixed_bias = jnp.concatenate([vectors[0:1], jnp.zeros((1, D), f32), vectors[1:2]], axis=1)

    qkv = project_qkv(me, tokens, pieces_qkv, mixed_bias)
    attended, weights = attention(lengths, qkv)
    normed_one, inv_one, hidden_low, activated, slope = feed_in(
        me, attended, tokens, pieces_in, vectors, in_bias
    )
    output, grad_res_two, grad_ffn, sums_two = feed_out(
        me, activated, normed_one, cotangent, pieces_out, vectors
    )
    parts_out = grad_w_out(me, activated, grad_ffn)
    grad_pre, sums_in = back_out(me, grad_ffn, slope, pieces_out)
    grad_res_one, grad_branch, grad_attended, sums_one = back_in(
        me, grad_pre, grad_res_two, normed_one, inv_one, pieces_in, vectors
    )
    parts_in = grad_w_in(me, attended, grad_branch, hidden_low, grad_pre)
    grad_mixed, sums_qkv = attention_back(lengths, qkv, weights, grad_attended)
    parts_qkv = grad_w_qkv(me, tokens, grad_mixed)
    grad_tokens = back_qkv(me, grad_mixed, grad_res_one, pieces_qkv)

    local_vecs = jnp.concatenate(
        [sums_qkv[0:2], sums_one[0:3], sums_two[0:3], sums_in.reshape(FF // D, D)], axis=0
    )
    if direct:
        for bit in (1, 2, 4):
            local_vecs = local_vecs + swap(local_vecs, bit)
        for bit in (1, 2):
            local_vecs = local_vecs + lax.ppermute(
                local_vecs, "rep", [(i, i ^ bit) for i in range(4)]
            )
        sum_out = sum_over_copies(scatter_chunk(*parts_out), rep_index)
        sum_in = sum_over_copies(scatter_chunk(*parts_in), rep_index)
        sum_qkv = sum_over_copies(scatter_chunk(*parts_qkv), rep_index)
    else:
        local_vecs = lax.psum(local_vecs, ("fsdp", "rep"))

        def reduce(theirs, mine):
            full = jnp.stack([mine, theirs], axis=1)
            full = full.reshape(-1, full.shape[-1])
            owned = lax.psum_scatter(full, "fsdp", scatter_dimension=0, tiled=True)
            return lax.psum(owned, "rep")

        sum_out, sum_in, sum_qkv = reduce(*parts_out), reduce(*parts_in), reduce(*parts_qkv)
    sum_vecs = lax.dynamic_slice(local_vecs, (0, position * part), (8, part))
    sum_bin = lax.dynamic_slice(local_vecs[8:].reshape(FF), (position * (FF // fsdp),), (FF // fsdp,))

    grad_out, step_out, mom_out, sq_out = adamw(m_out, v_out, sum_out)
    grad_in, step_in, mom_in, sq_in = adamw(m_in, v_in, sum_in[:, D:])
    sum_attn = jnp.concatenate([sum_qkv, sum_in[:, :D]], axis=1)
    grad_attn, step_attn, mom_attn, sq_attn = adamw(m_attn, v_attn, sum_attn)
    grad_bin, step_bin, mom_bin, sq_bin = adamw(m_bin, v_bin, sum_bin)
    grad_vecs, step_vecs, mom_vecs, sq_vecs = adamw(m_vecs, v_vecs, sum_vecs)
    return (
        output,
        grad_tokens,
        grad_attn,
        grad_in,
        grad_out,
        grad_bin,
        grad_vecs,
        step_attn,
        step_in,
        step_out,
        step_bin,
        step_vecs,
        mom_attn,
        mom_in,
        mom_out,
        mom_bin,
        mom_vecs,
        sq_attn,
        sq_in,
        sq_out,
        sq_bin,
        sq_vecs,
    )


def solution(mesh):
    rows, row, col = P(("rep", "fsdp"), None), P("fsdp", None), P(None, "fsdp")
    flat = P("fsdp")
    state = (row, row, row, flat, col)
    return jax.shard_map(
        functools.partial(local, mesh.shape["fsdp"], mesh.shape["rep"]),
        mesh=mesh,
        in_specs=(rows, rows, P(("rep", "fsdp"))) + state * 3,
        out_specs=(rows, rows) + state * 4,
        check_vma=False,
    )
```

```python
import functools

import jax
import jax.numpy as jnp
from jax import lax
from jax.experimental import pallas as pl
from jax.experimental.pallas import tpu as pltpu
from jax.sharding import PartitionSpec as P

D = 768
HEADS = 12
HDIM = 64
PART = D // 2
FF = 3072
SEQ = 128
STEP = 5

RANKS = 8
SHARD = D // RANKS
SHARD_FF = FF // RANKS

beta_one = 0.9
beta_two = 0.999
adam_epsilon = 1e-06
norm_epsilon = 1e-05
masked_score = -1000000000.0

bf16 = jnp.bfloat16
f32 = jnp.float32
NN = (((1,), (0,)), ((), ()))
NT = (((1,), (1,)), ((), ()))
TN = (((0,), (0,)), ((), ()))
VMEM_BYTES = 24 * 1024 * 1024
TILE = 256
LIGHT = 1000


def dot(left, right, dims):
    return lax.dot_general(left, right, dims, preferred_element_type=f32)


def call(kernel, grid, in_specs, out_specs, out_shape, scratch=(), flops=0, bytes_accessed=0, name=None):
    return pl.pallas_call(
        kernel,
        grid_spec=pltpu.PrefetchScalarGridSpec(
            num_scalar_prefetch=1,
            grid=grid,
            in_specs=in_specs,
            out_specs=out_specs,
            scratch_shapes=list(scratch),
        ),
        out_shape=out_shape,
        compiler_params=pltpu.CompilerParams(
            vmem_limit_bytes=VMEM_BYTES, dimension_semantics=("arbitrary",) * len(grid)
        ),
        cost_estimate=pl.CostEstimate(
            flops=int(flops) // LIGHT, bytes_accessed=int(bytes_accessed) // LIGHT, transcendentals=0
        ),
        name=name,
    )


def rows_of(width, tile=TILE):
    return pl.BlockSpec((tile, width), lambda i, s: (i, 0))


def whole(shape):
    return pl.BlockSpec(shape, lambda i, s: (0,) * len(shape))


ANY = pl.BlockSpec(memory_space=pl.ANY)


def in_hbm(array):
    return pltpu.with_memory_space_constraint(array, pltpu.HBM)


class Pieces:
    def __init__(self, arrays, places):
        self.arrays = [in_hbm(array) for array in arrays]
        self.places = places

    def __len__(self):
        return len(self.arrays)


def load_weight(pieces, me, refs, scratch, sem):
    copies = []
    for ref, place in zip(refs, pieces.places):
        if place is None:
            target = scratch
        else:
            mask, first, count = place
            target = scratch.at[me ^ mask, pl.ds(first, count)]
        copies.append(pltpu.make_async_copy(ref, target, sem))
    for copy in copies:
        copy.start()
    for copy in copies:
        copy.wait()


def load_halves(halves, me, refs, scratch, sem):
    rows = scratch.shape[1] // 2
    copies = []
    for number, pieces in enumerate(halves):
        for ref, place in zip(refs[number * len(pieces) :], pieces.places):
            at = pl.ds(number * rows, rows)
            if place is None:
                target = scratch.at[:, at]
            else:
                target = scratch.at[me ^ place[0], at]
            copies.append(pltpu.make_async_copy(ref, target, sem))
    for copy in copies:
        copy.start()
    for copy in copies:
        copy.wait()


def lane_sum(value):
    return jnp.sum(value, axis=-1, keepdims=True)


def normalize(residual):
    centre = residual - lane_sum(residual) * (1.0 / D)
    variance = lane_sum(centre * centre) * (1.0 / D)
    inv_std = lax.rsqrt(variance + norm_epsilon)
    return (centre * inv_std, inv_std)


def norm_back(grad_normed, normed, inv_std):
    first_mean = lane_sum(grad_normed) * (1.0 / D)
    second_mean = lane_sum(grad_normed * normed) * (1.0 / D)
    return inv_std * (grad_normed - first_mean - normed * second_mean)


def gelu_and_slope(pre_act):
    cumulative = 0.5 * (1.0 + lax.erf(pre_act * 0.7071067811865476))
    density = jnp.exp(-0.5 * pre_act * pre_act) * 0.3989422804014327
    return (pre_act * cumulative, cumulative + pre_act * density)


def project_qkv(me, tokens, weight, bias):
    rows = tokens.shape[0]
    count = len(weight)
    width = 3 * PART

    def kernel(s, x_ref, b_ref, *rest):
        refs, (out_ref, w_ref, sem) = rest[:count], rest[count:]

        @pl.when(pl.program_id(0) == 0)
        def _():
            load_weight(weight, s[0], refs, w_ref, sem)

        w = w_ref[...].reshape(D, width)
        out_ref[...] = (dot(x_ref[...], w, NN) + b_ref[...]).astype(bf16)

    return call(
        kernel,
        (rows // 512,),
        [rows_of(D, 512), whole((1, width))] + [ANY] * count,
        rows_of(width, 512),
        jax.ShapeDtypeStruct((rows, width), bf16),
        [pltpu.VMEM((RANKS, SHARD, width), bf16), pltpu.SemaphoreType.DMA],
        flops=2 * rows * D * width,
        bytes_accessed=2 * (rows * D * 4 + 3 * D * D),
        name="qkv",
    )(me, tokens, bias, *weight.arrays)


def head_masks():
    lane = lax.broadcasted_iota(jnp.int32, (SEQ, 2 * HDIM), 1)
    return lane < HDIM


def stack_heads(value, first):
    zero = jnp.zeros_like(value)
    return jnp.concatenate([jnp.where(first, value, zero), jnp.where(first, zero, value)], axis=0)


GROUP = 2


def attention(lengths, qkv):
    rows = qkv.shape[0]
    scale = HDIM ** (-0.5)
    wide = 2 * HDIM

    def kernel(s, qkv_ref, out_ref, p_ref):
        first = head_masks()
        for g in range(GROUP):
            at = slice(g * SEQ, (g + 1) * SEQ)
            length = s[pl.program_id(0) * GROUP + g]
            valid = lax.broadcasted_iota(jnp.int32, (SEQ, SEQ), 1) < length
            for h in range(PART // wide):
                lanes = slice(h * wide, (h + 1) * wide)
                q = qkv_ref[at, lanes]
                k = qkv_ref[at, PART + h * wide : PART + (h + 1) * wide]
                v = qkv_ref[at, 2 * PART + h * wide : 2 * PART + (h + 1) * wide]
                scores = dot(q, stack_heads(k, first), NT) * scale
                halves = []
                for part in range(2):
                    one = jnp.where(valid, scores[:, part * SEQ : (part + 1) * SEQ], masked_score)
                    top = jnp.max(one, axis=-1, keepdims=True)
                    raised = jnp.exp(one - top)
                    halves.append(raised / lane_sum(raised))
                weights = jnp.concatenate(halves, axis=1)
                p_ref[at, h * 2 * SEQ : (h + 1) * 2 * SEQ] = weights
                out_ref[at, lanes] = dot(weights.astype(bf16), stack_heads(v, first), NN).astype(bf16)

    width = HEADS * SEQ // 2
    return call(
        kernel,
        (rows // (GROUP * SEQ),),
        [rows_of(3 * PART, GROUP * SEQ)],
        [rows_of(PART, GROUP * SEQ), rows_of(width, GROUP * SEQ)],
        [jax.ShapeDtypeStruct((rows, PART), bf16), pltpu.HBM((rows, width), f32)],
        flops=4e9,
        bytes_accessed=rows * (PART * 8 + width * 4),
        name="attention",
    )(lengths, qkv)


def feed_in(me, attended, tokens, weight, vectors, in_bias):
    rows = tokens.shape[0]
    count = len(weight[0])
    total = 2 * count
    tile = 384
    width = (D + FF) // 2

    def kernel(s, o0_ref, o1_ref, x_ref, v_ref, b_ref, *rest):
        refs = rest[:total]
        n1_ref, inv_ref, hb_ref, f_ref, sl_ref, w0_ref, w1_ref, sem = rest[total:]

        @pl.when(pl.program_id(0) == 0)
        def _():
            load_weight(weight[0], s[0], refs[:count], w0_ref, sem)
            load_weight(weight[1], s[0], refs[count:], w1_ref, sem)

        w_proj = w0_ref[:, :, :D].reshape(D, D)
        branch = (
            dot(o0_ref[...], w_proj[:PART], NN) + dot(o1_ref[...], w_proj[PART:], NN) + v_ref[2:3, :]
        )
        normed, inv_std = normalize(x_ref[...].astype(f32) + branch)
        n1_ref[...] = normed
        inv_ref[...] = inv_std
        low = (normed * v_ref[3:4, :] + v_ref[4:5, :]).astype(bf16)
        hb_ref[...] = low
        for j, lead, end in IN_TILES:
            w = (w0_ref, w1_ref)[j][:, :, lead:end].reshape(D, end - lead)
            start = j * width + lead - D
            lanes = slice(start, start + end - lead)
            pre_act = dot(low, w, NN) + b_ref[:, lanes]
            act, slope = gelu_and_slope(pre_act)
            f_ref[:, lanes] = act.astype(bf16)
            sl_ref[:, lanes] = slope.astype(bf16)

    return call(
        kernel,
        (rows // TILE,),
        [rows_of(PART), rows_of(PART), rows_of(D), whole((8, D)), whole((1, FF))] + [ANY] * total,
        [rows_of(D), rows_of(1), rows_of(D), rows_of(FF), rows_of(FF)],
        [
            jax.ShapeDtypeStruct((rows, D), f32),
            jax.ShapeDtypeStruct((rows, 1), f32),
            jax.ShapeDtypeStruct((rows, D), bf16),
            jax.ShapeDtypeStruct((rows, FF), bf16),
            jax.ShapeDtypeStruct((rows, FF), bf16),
        ],
        [pltpu.VMEM((RANKS, SHARD, width), bf16)] * 2 + [pltpu.SemaphoreType.DMA],
        flops=2 * rows * D * (D + FF),
        bytes_accessed=rows * (D * 10 + FF * 4) + 2 * D * (D + FF),
        name="feed_in",
    )(me, *attended, tokens, vectors, in_bias, *weight[0].arrays, *weight[1].arrays)


IN_TILES = ((0, 768, 1280), (0, 1280, 1920), (1, 0, 512), (1, 512, 1024), (1, 1024, 1536), (1, 1536, 1920))


def feed_out(me, activated, normed_one, cotangent, weight, vectors):
    rows = activated.shape[0]
    count = len(weight[0])
    total = 2 * count

    def kernel(s, f_ref, n1_ref, g_ref, v_ref, *rest):
        refs = rest[:total]
        y_ref, dr_ref, dz_ref, sums_ref, w_ref, sem = rest[total:]

        @pl.when(pl.program_id(0) == 0)
        def _():
            load_halves(weight, s[0], refs, w_ref, sem)
            sums_ref[...] = jnp.zeros_like(sums_ref)

        branch = dot(f_ref[...], w_ref[...].reshape(FF, D), NN) + v_ref[5:6, :]
        hidden = n1_ref[...] * v_ref[3:4, :] + v_ref[4:5, :]
        normed, inv_std = normalize(hidden + branch)
        y_ref[...] = (normed * v_ref[6:7, :] + v_ref[7:8, :]).astype(bf16)
        grad_y = g_ref[...].astype(f32)
        sums_ref[1:2, :] += jnp.sum(grad_y * normed, axis=0, keepdims=True)
        sums_ref[2:3, :] += jnp.sum(grad_y, axis=0, keepdims=True)
        grad_res = norm_back(grad_y * v_ref[6:7, :], normed, inv_std)
        dr_ref[...] = grad_res
        low = grad_res.astype(bf16)
        dz_ref[...] = low
        sums_ref[0:1, :] += jnp.sum(low.astype(f32), axis=0, keepdims=True)

    return call(
        kernel,
        (rows // TILE,),
        [rows_of(FF), rows_of(D), rows_of(D), whole((8, D))] + [ANY] * total,
        [rows_of(D), rows_of(D), rows_of(D), whole((8, D))],
        [
            jax.ShapeDtypeStruct((rows, D), bf16),
            jax.ShapeDtypeStruct((rows, D), f32),
            jax.ShapeDtypeStruct((rows, D), bf16),
            jax.ShapeDtypeStruct((8, D), f32),
        ],
        [pltpu.VMEM((RANKS, SHARD_FF, D), bf16), pltpu.SemaphoreType.DMA],
        flops=2 * rows * D * FF,
        bytes_accessed=rows * (D * 14 + FF * 2) + 2 * D * FF,
        name="feed_out",
    )(me, activated, normed_one, cotangent, vectors, *weight[0].arrays, *weight[1].arrays)


def grad_w_out(me, activated, grad_ffn):
    rows = activated.shape[0]
    half = RANKS // 2

    def kernel(s, f_ref, dz_ref, t_ref, m_ref):
        block = dot(f_ref[...], dz_ref[...], TN).astype(bf16)
        low, high = block[:SHARD_FF], block[SHARD_FF:]
        even = (s[0] & 1) == 0
        m_ref[0] = jnp.where(even, low, high)
        t_ref[0] = jnp.where(even, high, low)

    shape = jax.ShapeDtypeStruct((half, SHARD_FF, D), bf16)
    out = pl.BlockSpec((1, SHARD_FF, D), lambda i, s: (i, 0, 0))
    return call(
        kernel,
        (half,),
        [
            pl.BlockSpec((rows, 2 * SHARD_FF), lambda i, s: (0, (s[0] >> 1) ^ i)),
            whole((rows, D)),
        ],
        [out, out],
        [shape, shape],
        flops=2 * rows * D * FF,
        bytes_accessed=rows * (D * 2 + FF * 2) + 2 * D * FF,
        name="grad_w_out",
    )(me, activated, grad_ffn)


def back_out(me, grad_ffn, slope, weight):
    rows = grad_ffn.shape[0]
    count = len(weight[0])
    total = 2 * count

    def kernel(s, dz_ref, sl_ref, *rest):
        refs = rest[:total]
        du_ref, sums_ref, w_ref, sem = rest[total:]

        @pl.when(pl.program_id(0) == 0)
        def _():
            load_halves(weight, s[0], refs, w_ref, sem)
            sums_ref[...] = jnp.zeros_like(sums_ref)

        dz = dz_ref[...]
        for r in range(RANKS // 2):
            lanes = slice(2 * r * SHARD_FF, 2 * (r + 1) * SHARD_FF)
            w = w_ref[2 * r : 2 * r + 2].reshape(2 * SHARD_FF, D)
            grad = dot(dz, w, NT) * sl_ref[:, lanes].astype(f32)
            low = grad.astype(bf16)
            du_ref[:, lanes] = low
            sums_ref[:, lanes] += jnp.sum(low.astype(f32), axis=0, keepdims=True)

    return call(
        kernel,
        (rows // TILE,),
        [rows_of(D), rows_of(FF)] + [ANY] * total,
        [rows_of(FF), whole((1, FF))],
        [jax.ShapeDtypeStruct((rows, FF), bf16), jax.ShapeDtypeStruct((1, FF), f32)],
        [pltpu.VMEM((RANKS, SHARD_FF, D), bf16), pltpu.SemaphoreType.DMA],
        flops=2 * rows * D * FF,
        bytes_accessed=rows * (D * 2 + FF * 4) + 2 * D * FF,
        name="back_out",
    )(me, grad_ffn, slope, *weight[0].arrays, *weight[1].arrays)


def back_in(me, grad_pre, grad_res_two, normed_one, inv_one, weight, vectors):
    rows = grad_pre.shape[0]
    count = len(weight[0])
    total = 2 * count
    width = (D + FF) // 2

    def kernel(s, du_ref, dr2_ref, n1_ref, inv_ref, v_ref, *rest):
        refs = rest[:total]
        dr1_ref, da_ref, do0_ref, do1_ref, sums_ref, w0_ref, w1_ref, sem = rest[total:]

        @pl.when(pl.program_id(0) == 0)
        def _():
            load_weight(weight[0], s[0], refs[:count], w0_ref, sem)
            load_weight(weight[1], s[0], refs[count:], w1_ref, sem)
            sums_ref[...] = jnp.zeros_like(sums_ref)

        cut = width - D
        grad_hidden = (
            dot(du_ref[:, :cut], w0_ref[:, :, D:].reshape(D, cut), NT)
            + dot(du_ref[:, cut:], w1_ref[...].reshape(D, width), NT)
            + dr2_ref[...]
        )
        normed = n1_ref[...]
        sums_ref[1:2, :] += jnp.sum(grad_hidden * normed, axis=0, keepdims=True)
        sums_ref[2:3, :] += jnp.sum(grad_hidden, axis=0, keepdims=True)
        grad_res = norm_back(grad_hidden * v_ref[3:4, :], normed, inv_ref[...])
        dr1_ref[...] = grad_res
        low = grad_res.astype(bf16)
        da_ref[...] = low
        sums_ref[0:1, :] += jnp.sum(low.astype(f32), axis=0, keepdims=True)
        w_proj = w0_ref[:, :, :D].reshape(D, D)
        grad_attended = dot(low, w_proj, NT).astype(bf16)
        do0_ref[...] = grad_attended[:, :PART]
        do1_ref[...] = grad_attended[:, PART:]

    return call(
        kernel,
        (rows // TILE,),
        [rows_of(FF), rows_of(D), rows_of(D), rows_of(1), whole((8, D))] + [ANY] * total,
        [rows_of(D), rows_of(D), rows_of(PART), rows_of(PART), whole((8, D))],
        [
            jax.ShapeDtypeStruct((rows, D), f32),
            jax.ShapeDtypeStruct((rows, D), bf16),
            jax.ShapeDtypeStruct((rows, PART), bf16),
            jax.ShapeDtypeStruct((rows, PART), bf16),
            jax.ShapeDtypeStruct((8, D), f32),
        ],
        [pltpu.VMEM((RANKS, SHARD, width), bf16)] * 2 + [pltpu.SemaphoreType.DMA],
        flops=2 * rows * D * (D + FF),
        bytes_accessed=rows * (D * 16 + FF * 2) + 2 * D * (D + FF),
        name="back_in",
    )(
        me,
        grad_pre,
        grad_res_two,
        normed_one,
        inv_one,
        vectors,
        *weight[0].arrays,
        *weight[1].arrays,
    )


def store_by_rank(s, block, t_ref, m_ref, first=0):
    even = (s[0] & 1) == 0
    chip = s[0] >> 1
    lanes = slice(first, first + block.shape[1])
    for k in range(RANKS // 2):
        low = block[2 * k * SHARD : (2 * k + 1) * SHARD]
        high = block[(2 * k + 1) * SHARD : (2 * k + 2) * SHARD]
        m_ref[chip ^ k, :, lanes] = jnp.where(even, low, high)
        t_ref[chip ^ k, :, lanes] = jnp.where(even, high, low)


def grad_w_in(me, hidden_low, grad_pre):
    rows = hidden_low.shape[0]
    half = RANKS // 2

    def kernel(s, h_ref, du_ref, t_ref, m_ref):
        store_by_rank(s, dot(h_ref[...], du_ref[...], TN).astype(bf16), t_ref, m_ref)

    shape = jax.ShapeDtypeStruct((half, SHARD, FF), bf16)
    out = pl.BlockSpec((half, SHARD, D), lambda i, s: (0, 0, i))
    return call(
        kernel,
        (FF // D,),
        [whole((rows, D)), pl.BlockSpec((rows, D), lambda i, s: (0, i))],
        [out, out],
        [shape, shape],
        flops=2 * rows * D * FF,
        bytes_accessed=rows * (D * 4 + FF * 2) + 2 * D * FF,
        name="grad_w_in",
    )(me, hidden_low, grad_pre)


def attention_back(lengths, qkv, weights, grad_attended):
    rows = qkv.shape[0]
    scale = HDIM ** (-0.5)
    wide = 2 * HDIM
    width = HEADS * SEQ // 2

    def kernel(s, qkv_ref, p_ref, do_ref, out_ref, sums_ref):
        @pl.when(pl.program_id(0) == 0)
        def _():
            sums_ref[...] = jnp.zeros_like(sums_ref)

        first = head_masks()
        for g in range(GROUP):
            at = slice(g * SEQ, (g + 1) * SEQ)
            for h in range(PART // wide):
                lanes = slice(h * wide, (h + 1) * wide)
                k_lanes = slice(PART + h * wide, PART + (h + 1) * wide)
                v_lanes = slice(2 * PART + h * wide, 2 * PART + (h + 1) * wide)
                q, k, v = qkv_ref[at, lanes], qkv_ref[at, k_lanes], qkv_ref[at, v_lanes]
                grad_out = do_ref[at, lanes]
                p = p_ref[at, h * 2 * SEQ : (h + 1) * 2 * SEQ]
                grad_p = dot(grad_out, stack_heads(v, first), NT)
                both = grad_p * p
                halves = []
                for part in range(2):
                    cut = slice(part * SEQ, (part + 1) * SEQ)
                    inner = grad_p[:, cut] - lane_sum(both[:, cut])
                    halves.append((p[:, cut] * inner).astype(bf16))
                grad_s = jnp.concatenate(halves, axis=1)
                grad_v = dot(p.astype(bf16), grad_out, TN)
                grad_v = jnp.where(first, grad_v[:SEQ], grad_v[SEQ:]).astype(bf16)
                grad_q = (dot(grad_s, stack_heads(k, first), NN) * scale).astype(bf16)
                grad_k = dot(grad_s, q, TN)
                grad_k = (jnp.where(first, grad_k[:SEQ], grad_k[SEQ:]) * scale).astype(bf16)
                out_ref[at, lanes] = grad_q
                out_ref[at, k_lanes] = grad_k
                out_ref[at, v_lanes] = grad_v
                sums_ref[0:1, lanes] += jnp.sum(grad_q.astype(f32), axis=0, keepdims=True)
                sums_ref[1:2, lanes] += jnp.sum(grad_v.astype(f32), axis=0, keepdims=True)

    return call(
        kernel,
        (rows // (GROUP * SEQ),),
        [rows_of(3 * PART, GROUP * SEQ), rows_of(width, GROUP * SEQ), rows_of(PART, GROUP * SEQ)],
        [rows_of(3 * PART, GROUP * SEQ), whole((8, PART))],
        [jax.ShapeDtypeStruct((rows, 3 * PART), bf16), jax.ShapeDtypeStruct((8, PART), f32)],
        flops=7e9,
        bytes_accessed=rows * (PART * 14 + width * 4),
        name="attention_back",
    )(lengths, qkv, in_hbm(weights), grad_attended)


def grad_w_qkv(me, tokens, grad_mixed):
    rows = tokens.shape[0]
    half = RANKS // 2
    width = 3 * PART

    def kernel(s, x_ref, g_ref, t_ref, m_ref):
        store_by_rank(s, dot(x_ref[...], g_ref[...], TN).astype(bf16), t_ref, m_ref)

    shape = jax.ShapeDtypeStruct((half, SHARD, width), bf16)
    out = whole((half, SHARD, width))
    return call(
        kernel,
        (1,),
        [whole((rows, D)), whole((rows, width))],
        [out, out],
        [shape, shape],
        flops=2 * rows * D * width,
        bytes_accessed=rows * (D * 8) + 2 * D * width,
        name="grad_w_qkv",
    )(me, tokens, grad_mixed)


def grad_w_mixed(me, tokens, grad_mixed, attended, grad_branch):
    rows = tokens.shape[0]
    half = RANKS // 2
    width = 3 * PART

    def kernel(s, x_ref, g_ref, o0_ref, o1_ref, da_ref, t_ref, m_ref):
        store_by_rank(s, dot(x_ref[...], g_ref[...], TN).astype(bf16), t_ref, m_ref)
        proj = jnp.concatenate(
            [
                dot(o0_ref[...], da_ref[...], TN).astype(bf16),
                dot(o1_ref[...], da_ref[...], TN).astype(bf16),
            ],
            axis=0,
        )
        store_by_rank(s, proj, t_ref, m_ref, width)

    shape = jax.ShapeDtypeStruct((half, SHARD, width + D), bf16)
    out = whole((half, SHARD, width + D))
    return call(
        kernel,
        (1,),
        [
            whole((rows, D)),
            whole((rows, width)),
            whole((rows, PART)),
            whole((rows, PART)),
            whole((rows, D)),
        ],
        [out, out],
        [shape, shape],
        flops=2 * rows * D * (width + D),
        bytes_accessed=rows * (D * 12) + 2 * D * (width + D),
        name="grad_w_mixed",
    )(me, tokens, grad_mixed, *attended, grad_branch)


def back_qkv(me, grad_mixed, grad_res_one, weight):
    rows = grad_res_one.shape[0]
    count = len(weight[0])
    total = 2 * count
    width = 3 * PART

    def kernel(s, g0_ref, g1_ref, dr_ref, *rest):
        refs = rest[:total]
        out_ref, w0_ref, w1_ref, sem = rest[total:]

        @pl.when(pl.program_id(0) == 0)
        def _():
            load_weight(weight[0], s[0], refs[:count], w0_ref, sem)
            load_weight(weight[1], s[0], refs[count:], w1_ref, sem)

        out_ref[...] = (
            dot(g0_ref[...], w0_ref[...].reshape(D, width), NT)
            + dot(g1_ref[...], w1_ref[...].reshape(D, width), NT)
            + dr_ref[...]
        ).astype(bf16)

    return call(
        kernel,
        (rows // TILE,),
        [rows_of(width), rows_of(width), rows_of(D)] + [ANY] * total,
        rows_of(D),
        jax.ShapeDtypeStruct((rows, D), bf16),
        [pltpu.VMEM((RANKS, SHARD, width), bf16)] * 2 + [pltpu.SemaphoreType.DMA],
        flops=2 * rows * D * 3 * D,
        bytes_accessed=rows * D * 12 + 2 * D * 3 * D,
        name="back_qkv",
    )(me, *grad_mixed, grad_res_one, *weight[0].arrays, *weight[1].arrays)


def adamw_math(moment, square, gradient):
    first_fix = 1.0 - beta_one**STEP
    second_fix = 1.0 - beta_two**STEP
    moment = beta_one * moment + (1.0 - beta_one) * gradient
    square = beta_two * square + (1.0 - beta_two) * gradient * gradient
    update = moment / first_fix / (jnp.sqrt(square / second_fix) + adam_epsilon)
    return (update, moment, square)


def adamw(moment, square, gradient):
    gradient = gradient.astype(f32)
    return (gradient,) + adamw_math(moment, square, gradient)


def flip(bit):
    return [(i, i ^ bit) for i in range(RANKS)]


def swap(value, bit):
    return lax.ppermute(value, "fsdp", flip(bit))


def after(value, *others):
    return lax.optimization_barrier((value,) + others)[0]


class Gather:
    def __init__(self, shard, turn):
        self.shard, self.turn = shard, turn

    def start(self, *others):
        self.shard = after(self.shard, *others) if others else self.shard
        self.x = swap(self.shard, 2)
        self.y = swap(self.shard, 4)
        return self

    def forward(self, *others):
        self.x, self.y = lax.optimization_barrier((self.x, self.y) + others)[:2]
        self.far = swap(self.x if self.turn == 4 else self.y, self.turn)
        return self

    def cross(self):
        self.mine = [self.shard, self.x, self.y, self.far]
        self.other = [swap(piece, 1) for piece in self.mine]
        return self

    def pieces(self):
        rows = self.shard.shape[0]
        masks = (0, 2, 4, 6)
        return Pieces(
            self.mine + self.other,
            [(m, 0, rows) for m in masks] + [(m ^ 1, 0, rows) for m in masks],
        )


def low_sum(*values):
    total = values[0].astype(f32)
    for value in values[1:]:
        total = total + value.astype(f32)
    return total.astype(bf16)


class Scatter:
    def __init__(self, parts):
        self.theirs, self.mine = parts
        self.half = self.mine.shape[1] // 2
        self.got = swap(self.theirs, 1)

    def one(self, *others):
        half, mine = self.half, self.mine
        self.got = after(self.got, *others)
        self.send_x = low_sum(mine[1::2, :half], self.got[1::2, :half])
        self.send_y = low_sum(mine[2:, half:], self.got[2:, half:])
        self.got_x = swap(self.send_x, 2)
        self.got_y = swap(self.send_y, 4)
        return self.send_x, self.send_y

    def two(self, *others):
        half, mine, got = self.half, self.mine, self.got
        self.got_x, self.got_y = lax.optimization_barrier((self.got_x, self.got_y) + others)[:2]
        send_y = low_sum(mine[2, :half], got[2, :half], self.got_x[1])
        send_x = low_sum(mine[1, half:], got[1, half:], self.got_y[1])
        self.last_y = swap(send_y, 4)
        self.last_x = swap(send_x, 2)
        return send_x, send_y

    def three(self, *others):
        half, mine, got = self.half, self.mine, self.got
        self.last_x, self.last_y = lax.optimization_barrier((self.last_x, self.last_y) + others)[:2]
        self.owned = jnp.concatenate(
            [
                low_sum(mine[0, :half], got[0, :half], self.got_x[0], self.last_y),
                low_sum(mine[0, half:], got[0, half:], self.got_y[0], self.last_x),
            ],
            axis=0,
        )
        self.near = lax.ppermute(self.owned, "rep", [(0, 1), (3, 2)])
        return (self.owned,)

    def four(self, *others):
        self.near = low_sum(self.owned, after(self.near, *others))
        self.across = lax.ppermute(self.near, "rep", [(1, 2), (2, 1)])
        return (self.near,)

    def five(self, *others):
        self.total = low_sum(self.near, after(self.across, *others))
        self.back = lax.ppermute(self.total, "rep", [(1, 0), (2, 3)])
        return (self.total,)

    def result(self, rep_index):
        inner = (rep_index == 1) | (rep_index == 2)
        return jnp.where(inner, self.total, self.back)


def gather_small(value, me, position, *others):
    got = after(swap(value, 1 << position), *others)
    low_first = ((me >> position) & 1) == 0
    return jnp.where(low_first, jnp.concatenate([value, got]), jnp.concatenate([got, value]))


def by_head_half(value, half):
    return [value[:, k * D + half * PART : k * D + (half + 1) * PART] for k in range(3)]


def local(
    fsdp,
    rep,
    tokens,
    cotangent,
    lengths,
    w_attn,
    w_in,
    w_out,
    b_in,
    vecs,
    m_attn,
    m_in,
    m_out,
    m_bin,
    m_vecs,
    v_attn,
    v_in,
    v_out,
    v_bin,
    v_vecs,
):
    direct = fsdp == RANKS and rep == 4
    position = lax.axis_index("fsdp")
    rep_index = lax.axis_index("rep")
    part = D // fsdp
    cut = (FF - D) // 2
    low_a = [jnp.concatenate(by_head_half(w_attn, h), axis=1).astype(bf16) for h in range(2)]
    low_b = [
        jnp.concatenate([w_attn[:, 3 * D :], w_in[:, :cut]], axis=1).astype(bf16),
        w_in[:, cut:].astype(bf16),
    ]
    middle = w_out.shape[0] // 2
    low_c = [w_out[:middle].astype(bf16), w_out[middle:].astype(bf16)]
    small = jnp.concatenate([vecs.reshape(1, -1), b_in.reshape(1, -1)], axis=1).astype(bf16)
    if direct:
        me = position.reshape(1)
        a = [Gather(low, turn) for low, turn in zip(low_a, (4, 2))]
        b = [Gather(low, turn) for low, turn in zip(low_b, (4, 2))]
        c = [Gather(low, turn) for low, turn in zip(low_c, (4, 2))]
        a[0].start()
        small_all = gather_small(small, position, 0, a[0].x, a[0].y)
        a[0].forward()
        a[1].start(a[0].x, a[0].y)
        small_all = gather_small(small_all, position, 1, a[0].far)
        a[0].cross()
        small_all = gather_small(small_all, position, 2, a[1].x, a[1].y)
        a[1].forward(a[0].far)
        for g in b:
            g.start(a[1].x, a[1].y)
        a[1].cross()
        pieces_a = [g.pieces() for g in a]
    else:
        me = jnp.zeros((1,), jnp.int32)

        def gather(shard):
            full = lax.all_gather(shard, "fsdp", axis=0, tiled=True)
            return Pieces([full.reshape(RANKS, -1, full.shape[1])], [None])

        def gather_rows(shards):
            full = lax.all_gather(jnp.concatenate(shards, axis=0), "fsdp", axis=0, tiled=True)
            full = full.reshape(RANKS, 2, -1, full.shape[1])
            return [Pieces([full[:, h]], [None]) for h in range(2)]

        pieces_a = [gather(low) for low in low_a]
        pieces_b = [gather(low) for low in low_b]
        pieces_c = gather_rows(low_c)
        small_all = lax.all_gather(small, "fsdp", axis=0, tiled=True)
    small_all = small_all.astype(f32)
    vectors = small_all[:, : 8 * part].reshape(fsdp, 8, part).transpose(1, 0, 2).reshape(8, D)
    in_bias = small_all[:, 8 * part :].reshape(1, FF)
    bias = [
        jnp.concatenate(
            [
                vectors[0:1, h * PART : (h + 1) * PART],
                jnp.zeros((1, PART), f32),
                vectors[1:2, h * PART : (h + 1) * PART],
            ],
            axis=1,
        )
        for h in range(2)
    ]

    x = after(tokens, a[1].x, a[1].y) if direct else tokens
    qkv = [project_qkv(me, x, pieces_a[0], bias[0])]
    x = after(tokens, qkv[0])
    qkv.append(project_qkv(me, x, pieces_a[1], bias[1]))
    attended, weights = [None, None], [None, None]
    attended[0], weights[0] = attention(lengths, after(qkv[0], qkv[1]))
    if direct:
        for g in b:
            g.forward(attended[0])
        for g in c:
            g.start(b[0].x, b[0].y, b[1].x, b[1].y)
        for g in b:
            g.cross()
        pieces_b = [g.pieces() for g in b]
        second = after(qkv[1], attended[0], b[0].x, b[0].y, b[1].x, b[1].y)
    else:
        second = qkv[1]
    attended[1], weights[1] = attention(lengths, second)
    normed_one, inv_one, hidden_low, activated, slope = feed_in(
        me, attended, tokens, pieces_b, vectors, in_bias
    )
    if direct:
        for g in c:
            g.forward(activated)
            g.cross()
        pieces_c = [g.pieces() for g in c]
    output, grad_res_two, grad_ffn, sums_two = feed_out(
        me, activated, normed_one, cotangent, pieces_c, vectors
    )

    def ordered(value, *others):
        return after(value, *others) if direct else value

    parts_out = grad_w_out(me, activated, grad_ffn)
    grad_pre, sums_in = back_out(me, ordered(grad_ffn, *parts_out), slope, pieces_c)
    if direct:
        r_out = Scatter(parts_out)
        sent = r_out.one(grad_pre)
    else:
        sent = ()
    parts_in = grad_w_in(me, hidden_low, ordered(grad_pre, *sent))
    grad_res_one, grad_branch, *grad_attended, sums_one = back_in(
        me,
        ordered(grad_pre, *parts_in),
        grad_res_two,
        normed_one,
        inv_one,
        pieces_b,
        vectors,
    )
    if direct:
        r_in = Scatter(parts_in)
        sent = r_out.two(grad_branch) + r_in.one(grad_branch)
    mixed0, sums_q0 = attention_back(
        lengths, qkv[0], weights[0], ordered(grad_attended[0], *sent)
    )
    if direct:
        sent = r_out.three(mixed0)
    parts_mix = grad_w_mixed(me, tokens, ordered(mixed0, *sent), attended, grad_branch)
    if direct:
        r_mix = Scatter(parts_mix)
        sent = r_in.two(*parts_mix)
    mixed1, sums_q1 = attention_back(
        lengths, qkv[1], weights[1], ordered(grad_attended[1], *sent, *parts_mix)
    )
    if direct:
        sent = r_mix.one(mixed1) + r_out.four(mixed1)
    parts_qkv = grad_w_qkv(me, tokens, ordered(mixed1, *sent))
    local_vecs = jnp.concatenate(
        [
            jnp.concatenate([sums_q0[0:2], sums_q1[0:2]], axis=1),
            sums_one[0:3],
            sums_two[0:3],
            sums_in.reshape(FF // D, D),
        ],
        axis=0,
    )
    if direct:
        r_qkv = Scatter(parts_qkv)
        sent = r_in.three(*parts_qkv)
    grad_tokens = back_qkv(
        me,
        (mixed0, ordered(mixed1, *sent, *parts_qkv)),
        grad_res_one,
        pieces_a,
    )
    if direct:
        r_qkv.one(grad_tokens)
        r_mix.two(grad_tokens)
        r_out.five(grad_tokens)
        r_in.four(grad_tokens)
        local_vecs = after(local_vecs, r_qkv.send_x)
        local_vecs = local_vecs + swap(local_vecs, 1)
        r_mix.three()
        sent = r_qkv.two()
        local_vecs = after(local_vecs, *sent)
        local_vecs = local_vecs + swap(local_vecs, 2)
        r_in.five()
        r_mix.four()
        sent = r_qkv.three()
        local_vecs = after(local_vecs, *sent)
        local_vecs = local_vecs + swap(local_vecs, 4)
        r_mix.five()
        sent = r_qkv.four()
        local_vecs = after(local_vecs, *sent)
        local_vecs = local_vecs + lax.ppermute(local_vecs, "rep", [(i, i ^ 1) for i in range(4)])
        sent = r_qkv.five()
        local_vecs = after(local_vecs, *sent)
        local_vecs = local_vecs + lax.ppermute(local_vecs, "rep", [(i, i ^ 2) for i in range(4)])
        sum_out, sum_in, sum_mix, sum_qkv = [
            r.result(rep_index) for r in (r_out, r_in, r_mix, r_qkv)
        ]
    else:
        local_vecs = lax.psum(local_vecs, ("fsdp", "rep"))

        def reduce(theirs, mine):
            full = jnp.stack([mine, theirs], axis=1)
            full = full.reshape(-1, full.shape[-1])
            owned = lax.psum_scatter(full, "fsdp", scatter_dimension=0, tiled=True)
            return lax.psum(owned, "rep")

        sum_out, sum_in, sum_mix, sum_qkv = [
            reduce(*parts) for parts in (parts_out, parts_in, parts_mix, parts_qkv)
        ]
    sum_vecs = lax.dynamic_slice(local_vecs, (0, position * part), (8, part))
    sum_bin = lax.dynamic_slice(local_vecs[8:].reshape(FF), (position * (FF // fsdp),), (FF // fsdp,))

    grad_out, step_out, mom_out, sq_out = adamw(m_out, v_out, sum_out)
    grad_in, step_in, mom_in, sq_in = adamw(m_in, v_in, sum_in)
    columns = []
    for k in range(3):
        columns += [sum_mix[:, k * PART : (k + 1) * PART], sum_qkv[:, k * PART : (k + 1) * PART]]
    sum_attn = jnp.concatenate(columns + [sum_mix[:, 3 * PART :]], axis=1)
    grad_attn, step_attn, mom_attn, sq_attn = adamw(m_attn, v_attn, sum_attn)
    grad_bin, step_bin, mom_bin, sq_bin = adamw(m_bin, v_bin, sum_bin)
    grad_vecs, step_vecs, mom_vecs, sq_vecs = adamw(m_vecs, v_vecs, sum_vecs)
    return (
        output,
        grad_tokens,
        grad_attn,
        grad_in,
        grad_out,
        grad_bin,
        grad_vecs,
        step_attn,
        step_in,
        step_out,
        step_bin,
        step_vecs,
        mom_attn,
        mom_in,
        mom_out,
        mom_bin,
        mom_vecs,
        sq_attn,
        sq_in,
        sq_out,
        sq_bin,
        sq_vecs,
    )


def solution(mesh):
    rows, row, col = P(("rep", "fsdp"), None), P("fsdp", None), P(None, "fsdp")
    flat = P("fsdp")
    state = (row, row, row, flat, col)
    return jax.shard_map(
        functools.partial(local, mesh.shape["fsdp"], mesh.shape["rep"]),
        mesh=mesh,
        in_specs=(rows, rows, P(("rep", "fsdp"))) + state * 3,
        out_specs=(rows, rows) + state * 4,
        check_vma=False,
    )
```

```python
import functools

import jax
import jax.numpy as jnp
from jax import lax
from jax.experimental import pallas as pl
from jax.experimental.pallas import tpu as pltpu
from jax.sharding import PartitionSpec as P

D = 768
HEADS = 12
HDIM = 64
PART = D // 2
FF = 3072
SEQ = 128
STEP = 5

RANKS = 8
SHARD = D // RANKS
SHARD_FF = FF // RANKS

beta_one = 0.9
beta_two = 0.999
adam_epsilon = 1e-06
norm_epsilon = 1e-05
masked_score = -1000000000.0

bf16 = jnp.bfloat16
f32 = jnp.float32
NN = (((1,), (0,)), ((), ()))
NT = (((1,), (1,)), ((), ()))
TN = (((0,), (0,)), ((), ()))
VMEM_BYTES = 20 * 1024 * 1024
TILE = 256
LIGHT = 1000


def dot(left, right, dims):
    return lax.dot_general(left, right, dims, preferred_element_type=f32)


def call(kernel, grid, in_specs, out_specs, out_shape, scratch=(), flops=0, bytes_accessed=0, name=None):
    return pl.pallas_call(
        kernel,
        grid_spec=pltpu.PrefetchScalarGridSpec(
            num_scalar_prefetch=1,
            grid=grid,
            in_specs=in_specs,
            out_specs=out_specs,
            scratch_shapes=list(scratch),
        ),
        out_shape=out_shape,
        compiler_params=pltpu.CompilerParams(
            vmem_limit_bytes=VMEM_BYTES, dimension_semantics=("arbitrary",) * len(grid)
        ),
        cost_estimate=pl.CostEstimate(
            flops=int(flops) // LIGHT, bytes_accessed=int(bytes_accessed) // LIGHT, transcendentals=0
        ),
        name=name,
    )


def rows_of(width, tile=TILE):
    return pl.BlockSpec((tile, width), lambda i, s: (i, 0))


def whole(shape):
    return pl.BlockSpec(shape, lambda i, s: (0,) * len(shape))


ANY = pl.BlockSpec(memory_space=pl.ANY)
HELD = pl.BlockSpec(memory_space=pltpu.VMEM)


def in_vmem(array):
    return pltpu.with_memory_space_constraint(array, pltpu.VMEM)


def in_hbm(array):
    return pltpu.with_memory_space_constraint(array, pltpu.HBM)


class Weight:
    def __init__(self, arrays, shape, by_rank=False):
        self.arrays = [in_hbm(array) for array in arrays]
        self.shape, self.by_rank = shape, by_rank

    def __len__(self):
        return len(self.arrays)

    def load(self, me, refs, held, sem):
        if len(refs) == 1:
            copies = [pltpu.make_async_copy(refs[0], held, sem)]
        else:
            copies = []
            for number, ref in enumerate(refs):
                owner = me if number < 4 else me ^ 1
                half = owner & 1
                along = jnp.where(half == 0, 2, 4)
                mask = (0, along, 6 - along, 6)[number % 4]
                for core in range(2):
                    rank = owner ^ mask ^ core
                    target = held.at[rank, half] if self.by_rank else held.at[half, rank]
                    copies.append(pltpu.make_async_copy(ref.at[core], target, sem))
        for copy in copies:
            copy.start()
        for copy in copies:
            copy.wait()


def lane_sum(value):
    return jnp.sum(value, axis=-1, keepdims=True)


def normalize(residual):
    centre = residual - lane_sum(residual) * (1.0 / D)
    variance = lane_sum(centre * centre) * (1.0 / D)
    inv_std = lax.rsqrt(variance + norm_epsilon)
    return (centre * inv_std, inv_std)


def norm_back(grad_normed, normed, inv_std):
    first_mean = lane_sum(grad_normed) * (1.0 / D)
    second_mean = lane_sum(grad_normed * normed) * (1.0 / D)
    return inv_std * (grad_normed - first_mean - normed * second_mean)


def gelu_and_slope(pre_act):
    cumulative = 0.5 * (1.0 + lax.erf(pre_act * 0.7071067811865476))
    density = jnp.exp(-0.5 * pre_act * pre_act) * 0.3989422804014327
    return (pre_act * cumulative, cumulative + pre_act * density)


def project_qkv(me, tokens, weight, bias):
    rows = tokens.shape[0]
    count = len(weight)
    width = 3 * PART

    def kernel(s, x_ref, b_ref, *rest):
        refs, (out0_ref, out1_ref, w_ref, sem) = rest[:count], rest[count:]

        @pl.when(pl.program_id(0) == 0)
        def _():
            weight.load(s[0], refs, w_ref, sem)

        for h, out_ref in enumerate((out0_ref, out1_ref)):
            w = w_ref[h].reshape(D, width)
            out_ref[...] = (dot(x_ref[...], w, NN) + b_ref[h : h + 1]).astype(bf16)

    return call(
        kernel,
        (rows // TILE,),
        [rows_of(D), whole((2, width))] + [ANY] * count,
        [rows_of(width), rows_of(width)],
        [
            jax.ShapeDtypeStruct((rows, width), bf16),
            jax.ShapeDtypeStruct((rows, width), bf16),
        ],
        [pltpu.VMEM(weight.shape, bf16), pltpu.SemaphoreType.DMA],
        flops=2 * rows * D * width * 2,
        bytes_accessed=2 * (rows * D * 4 + 3 * D * D),
        name="qkv",
    )(me, tokens, bias, *weight.arrays)


def head_masks():
    lane = lax.broadcasted_iota(jnp.int32, (SEQ, 2 * HDIM), 1)
    return lane < HDIM


def stack_heads(value, first):
    zero = jnp.zeros_like(value)
    return jnp.concatenate([jnp.where(first, value, zero), jnp.where(first, zero, value)], axis=0)


GROUP = 2


def attention(lengths, qkv):
    rows = qkv.shape[0]
    scale = HDIM ** (-0.5)
    wide = 2 * HDIM

    def kernel(s, qkv_ref, out_ref, p_ref):
        first = head_masks()
        for g in range(GROUP):
            at = slice(g * SEQ, (g + 1) * SEQ)
            length = s[pl.program_id(0) * GROUP + g]
            valid = lax.broadcasted_iota(jnp.int32, (SEQ, SEQ), 1) < length
            for h in range(PART // wide):
                lanes = slice(h * wide, (h + 1) * wide)
                q = qkv_ref[at, lanes]
                k = qkv_ref[at, PART + h * wide : PART + (h + 1) * wide]
                v = qkv_ref[at, 2 * PART + h * wide : 2 * PART + (h + 1) * wide]
                scores = dot(q, stack_heads(k, first), NT) * scale
                halves = []
                for part in range(2):
                    one = jnp.where(valid, scores[:, part * SEQ : (part + 1) * SEQ], masked_score)
                    top = jnp.max(one, axis=-1, keepdims=True)
                    raised = jnp.exp(one - top)
                    halves.append(raised / lane_sum(raised))
                weights = jnp.concatenate(halves, axis=1)
                p_ref[at, h * 2 * SEQ : (h + 1) * 2 * SEQ] = weights
                out_ref[at, lanes] = dot(weights.astype(bf16), stack_heads(v, first), NN).astype(bf16)

    width = HEADS * SEQ // 2
    return call(
        kernel,
        (rows // (GROUP * SEQ),),
        [rows_of(3 * PART, GROUP * SEQ)],
        [rows_of(PART, GROUP * SEQ), rows_of(width, GROUP * SEQ)],
        [jax.ShapeDtypeStruct((rows, PART), bf16), pltpu.HBM((rows, width), f32)],
        flops=4e9,
        bytes_accessed=rows * (PART * 8 + width * 4),
        name="attention",
    )(lengths, qkv)


def feed_in(me, attended, tokens, weight, vectors, in_bias):
    rows = tokens.shape[0]
    count = len(weight)
    width = (D + FF) // 2

    def kernel(s, o0_ref, o1_ref, x_ref, v_ref, b_ref, *rest):
        refs = rest[:count]
        n1_ref, inv_ref, hb_ref, f_ref, sl_ref, w_ref, sem = rest[count:]

        @pl.when(pl.program_id(0) == 0)
        def _():
            weight.load(s[0], refs, w_ref, sem)

        w_proj = w_ref[0, :, :, :D].reshape(D, D)
        branch = (
            dot(o0_ref[...], w_proj[:PART], NN) + dot(o1_ref[...], w_proj[PART:], NN) + v_ref[2:3, :]
        )
        normed, inv_std = normalize(x_ref[...].astype(f32) + branch)
        n1_ref[...] = normed
        inv_ref[...] = inv_std
        low = (normed * v_ref[3:4, :] + v_ref[4:5, :]).astype(bf16)
        hb_ref[...] = low
        for j, lead, end in IN_TILES:
            w = w_ref[j, :, :, lead:end].reshape(D, end - lead)
            start = j * width + lead - D
            lanes = slice(start, start + end - lead)
            pre_act = dot(low, w, NN) + b_ref[:, lanes]
            act, slope = gelu_and_slope(pre_act)
            f_ref[:, lanes] = act.astype(bf16)
            sl_ref[:, lanes] = slope.astype(bf16)

    return call(
        kernel,
        (rows // TILE,),
        [rows_of(PART), rows_of(PART), rows_of(D), whole((8, D)), whole((1, FF))] + [ANY] * count,
        [rows_of(D), rows_of(1), rows_of(D), rows_of(FF), rows_of(FF), HELD],
        [
            pltpu.HBM((rows, D), f32),
            pltpu.HBM((rows, 1), f32),
            jax.ShapeDtypeStruct((rows, D), bf16),
            pltpu.VMEM((rows, FF), bf16),
            pltpu.VMEM((rows, FF), bf16),
            pltpu.VMEM(weight.shape, bf16),
        ],
        [pltpu.SemaphoreType.DMA],
        flops=2 * rows * D * (D + FF),
        bytes_accessed=rows * (D * 10 + FF * 4) + 2 * D * (D + FF),
        name="feed_in",
    )(me, *attended, tokens, vectors, in_bias, *weight.arrays)


IN_TILES = ((0, 768, 1280), (0, 1280, 1920), (1, 0, 512), (1, 512, 1024), (1, 1024, 1536), (1, 1536, 1920))


def feed_out(me, activated, normed_one, cotangent, weight, vectors):
    rows = activated.shape[0]
    count = len(weight)

    def kernel(s, f_ref, n1_ref, g_ref, v_ref, *rest):
        refs = rest[:count]
        y_ref, dr_ref, dz_ref, sums_ref, w_ref, sem = rest[count:]

        @pl.when(pl.program_id(0) == 0)
        def _():
            weight.load(s[0], refs, w_ref, sem)
            sums_ref[...] = jnp.zeros_like(sums_ref)

        branch = dot(f_ref[...], w_ref[...].reshape(FF, D), NN) + v_ref[5:6, :]
        hidden = n1_ref[...] * v_ref[3:4, :] + v_ref[4:5, :]
        normed, inv_std = normalize(hidden + branch)
        y_ref[...] = (normed * v_ref[6:7, :] + v_ref[7:8, :]).astype(bf16)
        grad_y = g_ref[...].astype(f32)
        sums_ref[1:2, :] += jnp.sum(grad_y * normed, axis=0, keepdims=True)
        sums_ref[2:3, :] += jnp.sum(grad_y, axis=0, keepdims=True)
        grad_res = norm_back(grad_y * v_ref[6:7, :], normed, inv_std)
        dr_ref[...] = grad_res
        low = grad_res.astype(bf16)
        dz_ref[...] = low
        sums_ref[0:1, :] += jnp.sum(low.astype(f32), axis=0, keepdims=True)

    return call(
        kernel,
        (rows // TILE,),
        [rows_of(FF), rows_of(D), rows_of(D), whole((8, D))] + [ANY] * count,
        [rows_of(D), rows_of(D), rows_of(D), whole((8, D)), HELD],
        [
            jax.ShapeDtypeStruct((rows, D), bf16),
            pltpu.HBM((rows, D), f32),
            jax.ShapeDtypeStruct((rows, D), bf16),
            jax.ShapeDtypeStruct((8, D), f32),
            pltpu.VMEM(weight.shape, bf16),
        ],
        [pltpu.SemaphoreType.DMA],
        flops=2 * rows * D * FF,
        bytes_accessed=rows * (D * 14 + FF * 2) + 2 * D * FF,
        name="feed_out",
    )(me, in_vmem(activated), in_hbm(normed_one), cotangent, vectors, *weight.arrays)


def grad_w_out(me, activated, grad_ffn):
    rows = activated.shape[0]
    half = RANKS // 2

    def kernel(s, f_ref, dz_ref, t_ref, m_ref):
        block = dot(f_ref[...], dz_ref[...], TN).astype(bf16)
        low, high = block[:SHARD_FF], block[SHARD_FF:]
        even = (s[0] & 1) == 0
        m_ref[0] = jnp.where(even, low, high)
        t_ref[0] = jnp.where(even, high, low)

    shape = pltpu.HBM((half, SHARD_FF, D), bf16)
    out = pl.BlockSpec((1, SHARD_FF, D), lambda i, s: (i, 0, 0))
    return call(
        kernel,
        (half,),
        [
            pl.BlockSpec((rows, 2 * SHARD_FF), lambda i, s: (0, (s[0] >> 1) ^ i)),
            whole((rows, D)),
        ],
        [out, out],
        [shape, shape],
        flops=2 * rows * D * FF,
        bytes_accessed=rows * (D * 2 + FF * 2) + 2 * D * FF,
        name="grad_w_out",
    )(me, in_vmem(activated), grad_ffn)


def back_out(me, grad_ffn, slope, weight):
    rows = grad_ffn.shape[0]

    def kernel(s, dz_ref, sl_ref, w_ref, du_ref, sums_ref):
        @pl.when(pl.program_id(0) == 0)
        def _():
            sums_ref[...] = jnp.zeros_like(sums_ref)

        dz = dz_ref[...]
        for r in range(RANKS // 2):
            lanes = slice(2 * r * SHARD_FF, 2 * (r + 1) * SHARD_FF)
            w = w_ref[2 * r : 2 * r + 2].reshape(2 * SHARD_FF, D)
            grad = dot(dz, w, NT) * sl_ref[:, lanes].astype(f32)
            low = grad.astype(bf16)
            du_ref[:, lanes] = low
            sums_ref[:, lanes] += jnp.sum(low.astype(f32), axis=0, keepdims=True)

    return call(
        kernel,
        (rows // TILE,),
        [rows_of(D), rows_of(FF), HELD],
        [rows_of(FF), whole((1, FF))],
        [jax.ShapeDtypeStruct((rows, FF), bf16), jax.ShapeDtypeStruct((1, FF), f32)],
        flops=2 * rows * D * FF,
        bytes_accessed=rows * (D * 2 + FF * 4) + 2 * D * FF,
        name="back_out",
    )(me, grad_ffn, in_vmem(slope), in_vmem(weight))


def back_in(me, grad_pre, grad_res_two, normed_one, inv_one, weight, vectors):
    rows = grad_pre.shape[0]
    width = (D + FF) // 2

    def kernel(
        s, du_ref, dr2_ref, n1_ref, inv_ref, v_ref, w_ref, dr1_ref, da_ref, do0_ref, do1_ref, sums_ref
    ):
        @pl.when(pl.program_id(0) == 0)
        def _():
            sums_ref[...] = jnp.zeros_like(sums_ref)

        cut = width - D
        grad_hidden = (
            dot(du_ref[:, :cut], w_ref[0, :, :, D:].reshape(D, cut), NT)
            + dot(du_ref[:, cut:], w_ref[1].reshape(D, width), NT)
            + dr2_ref[...]
        )
        normed = n1_ref[...]
        sums_ref[1:2, :] += jnp.sum(grad_hidden * normed, axis=0, keepdims=True)
        sums_ref[2:3, :] += jnp.sum(grad_hidden, axis=0, keepdims=True)
        grad_res = norm_back(grad_hidden * v_ref[3:4, :], normed, inv_ref[...])
        dr1_ref[...] = grad_res
        low = grad_res.astype(bf16)
        da_ref[...] = low
        sums_ref[0:1, :] += jnp.sum(low.astype(f32), axis=0, keepdims=True)
        w_proj = w_ref[0, :, :, :D].reshape(D, D)
        grad_attended = dot(low, w_proj, NT).astype(bf16)
        do0_ref[...] = grad_attended[:, :PART]
        do1_ref[...] = grad_attended[:, PART:]

    return call(
        kernel,
        (rows // TILE,),
        [rows_of(FF), rows_of(D), rows_of(D), rows_of(1), whole((8, D))] + [HELD],
        [rows_of(D), rows_of(D), rows_of(PART), rows_of(PART), whole((8, D))],
        [
            pltpu.HBM((rows, D), f32),
            jax.ShapeDtypeStruct((rows, D), bf16),
            jax.ShapeDtypeStruct((rows, PART), bf16),
            jax.ShapeDtypeStruct((rows, PART), bf16),
            jax.ShapeDtypeStruct((8, D), f32),
        ],
        flops=2 * rows * D * (D + FF),
        bytes_accessed=rows * (D * 16 + FF * 2) + 2 * D * (D + FF),
        name="back_in",
    )(
        me,
        grad_pre,
        in_hbm(grad_res_two),
        in_hbm(normed_one),
        in_hbm(inv_one),
        vectors,
        in_vmem(weight),
    )


def store_by_rank(s, block, t_ref, m_ref, first=0):
    even = (s[0] & 1) == 0
    chip = s[0] >> 1
    lanes = slice(first, first + block.shape[1])
    for k in range(RANKS // 2):
        low = block[2 * k * SHARD : (2 * k + 1) * SHARD]
        high = block[(2 * k + 1) * SHARD : (2 * k + 2) * SHARD]
        m_ref[chip ^ k, :SHARD, lanes] = jnp.where(even, low, high)
        t_ref[chip ^ k, :SHARD, lanes] = jnp.where(even, high, low)


def grad_w_in(me, hidden_low, grad_pre):
    rows = hidden_low.shape[0]
    half = RANKS // 2

    def kernel(s, h_ref, du_ref, t_ref, m_ref):
        store_by_rank(s, dot(h_ref[...], du_ref[...], TN).astype(bf16), t_ref, m_ref)

    shape = pltpu.HBM((half, SHARD, FF), bf16)
    out = pl.BlockSpec((half, SHARD, D), lambda i, s: (0, 0, i))
    return call(
        kernel,
        (FF // D,),
        [whole((rows, D)), pl.BlockSpec((rows, D), lambda i, s: (0, i))],
        [out, out],
        [shape, shape],
        flops=2 * rows * D * FF,
        bytes_accessed=rows * (D * 4 + FF * 2) + 2 * D * FF,
        name="grad_w_in",
    )(me, hidden_low, grad_pre)


def attention_back(lengths, qkv, weights, grad_attended):
    rows = qkv.shape[0]
    scale = HDIM ** (-0.5)
    wide = 2 * HDIM
    width = HEADS * SEQ // 2

    def kernel(s, qkv_ref, p_ref, do_ref, out_ref, sums_ref):
        @pl.when(pl.program_id(0) == 0)
        def _():
            sums_ref[...] = jnp.zeros_like(sums_ref)

        first = head_masks()
        for g in range(GROUP):
            at = slice(g * SEQ, (g + 1) * SEQ)
            for h in range(PART // wide):
                lanes = slice(h * wide, (h + 1) * wide)
                k_lanes = slice(PART + h * wide, PART + (h + 1) * wide)
                v_lanes = slice(2 * PART + h * wide, 2 * PART + (h + 1) * wide)
                q, k, v = qkv_ref[at, lanes], qkv_ref[at, k_lanes], qkv_ref[at, v_lanes]
                grad_out = do_ref[at, lanes]
                p = p_ref[at, h * 2 * SEQ : (h + 1) * 2 * SEQ]
                grad_p = dot(grad_out, stack_heads(v, first), NT)
                both = grad_p * p
                halves = []
                for part in range(2):
                    cut = slice(part * SEQ, (part + 1) * SEQ)
                    inner = grad_p[:, cut] - lane_sum(both[:, cut])
                    halves.append((p[:, cut] * inner).astype(bf16))
                grad_s = jnp.concatenate(halves, axis=1)
                grad_v = dot(p.astype(bf16), grad_out, TN)
                grad_v = jnp.where(first, grad_v[:SEQ], grad_v[SEQ:]).astype(bf16)
                grad_q = (dot(grad_s, stack_heads(k, first), NN) * scale).astype(bf16)
                grad_k = dot(grad_s, q, TN)
                grad_k = (jnp.where(first, grad_k[:SEQ], grad_k[SEQ:]) * scale).astype(bf16)
                out_ref[at, lanes] = grad_q
                out_ref[at, k_lanes] = grad_k
                out_ref[at, v_lanes] = grad_v
                sums_ref[0:1, lanes] += jnp.sum(grad_q.astype(f32), axis=0, keepdims=True)
                sums_ref[1:2, lanes] += jnp.sum(grad_v.astype(f32), axis=0, keepdims=True)

    return call(
        kernel,
        (rows // (GROUP * SEQ),),
        [rows_of(3 * PART, GROUP * SEQ), rows_of(width, GROUP * SEQ), rows_of(PART, GROUP * SEQ)],
        [rows_of(3 * PART, GROUP * SEQ), whole((8, PART))],
        [jax.ShapeDtypeStruct((rows, 3 * PART), bf16), jax.ShapeDtypeStruct((8, PART), f32)],
        flops=7e9,
        bytes_accessed=rows * (PART * 14 + width * 4),
        name="attention_back",
    )(lengths, qkv, in_hbm(weights), grad_attended)


EXTRA = 16
IN_AT = 128


def grad_w_qkv(me, tokens, grad_mixed, sums_qkv, sums_one, sums_two, sums_in):
    rows = tokens.shape[0]
    half = RANKS // 2
    width = 3 * PART

    def kernel(s, x_ref, g_ref, q0_ref, q1_ref, one_ref, two_ref, in_ref, t_ref, m_ref):
        store_by_rank(s, dot(x_ref[...], g_ref[...], TN).astype(bf16), t_ref, m_ref)
        vectors = jnp.concatenate(
            [
                jnp.concatenate([q0_ref[0:2], q1_ref[0:2]], axis=1),
                one_ref[0:3],
                two_ref[0:3],
            ],
            axis=0,
        )
        even = (s[0] & 1) == 0
        chip = s[0] >> 1
        for k in range(half):
            blocks = []
            for rank in (2 * k, 2 * k + 1):
                vec = vectors[:, rank * SHARD : (rank + 1) * SHARD]
                vec = jnp.concatenate([vec, jnp.zeros((8, IN_AT - SHARD), f32)], axis=1)
                bias = in_ref[:, rank * SHARD_FF : (rank + 1) * SHARD_FF]
                bias = jnp.concatenate([bias, jnp.zeros((7, SHARD_FF), f32)], axis=0)
                block = jnp.concatenate([vec, bias], axis=1)
                blocks.append(jnp.concatenate([block, jnp.zeros_like(block)], axis=0).astype(bf16))
            end = IN_AT + SHARD_FF
            m_ref[chip ^ k, SHARD:, :end] = jnp.where(even, blocks[0], blocks[1])
            t_ref[chip ^ k, SHARD:, :end] = jnp.where(even, blocks[1], blocks[0])
            m_ref[chip ^ k, SHARD:, end:] = jnp.zeros((EXTRA, width - end), bf16)
            t_ref[chip ^ k, SHARD:, end:] = jnp.zeros((EXTRA, width - end), bf16)

    shape = pltpu.HBM((half, SHARD + EXTRA, width), bf16)
    out = whole((half, SHARD + EXTRA, width))
    return call(
        kernel,
        (1,),
        [
            whole((rows, D)),
            whole((rows, width)),
            whole((8, PART)),
            whole((8, PART)),
            whole((8, D)),
            whole((8, D)),
            whole((1, FF)),
        ],
        [out, out],
        [shape, shape],
        flops=2 * rows * D * width,
        bytes_accessed=rows * (D * 8) + 2 * D * width,
        name="grad_w_qkv",
    )(me, tokens, grad_mixed, *sums_qkv, sums_one, sums_two, sums_in)


def grad_w_mixed(me, tokens, grad_mixed, attended, grad_branch):
    rows = tokens.shape[0]
    half = RANKS // 2
    width = 3 * PART

    def kernel(s, x_ref, g_ref, o0_ref, o1_ref, da_ref, t_ref, m_ref):
        store_by_rank(s, dot(x_ref[...], g_ref[...], TN).astype(bf16), t_ref, m_ref)
        proj = jnp.concatenate(
            [
                dot(o0_ref[...], da_ref[...], TN).astype(bf16),
                dot(o1_ref[...], da_ref[...], TN).astype(bf16),
            ],
            axis=0,
        )
        store_by_rank(s, proj, t_ref, m_ref, width)

    shape = pltpu.HBM((half, SHARD, width + D), bf16)
    out = whole((half, SHARD, width + D))
    return call(
        kernel,
        (1,),
        [
            whole((rows, D)),
            whole((rows, width)),
            whole((rows, PART)),
            whole((rows, PART)),
            whole((rows, D)),
        ],
        [out, out],
        [shape, shape],
        flops=2 * rows * D * (width + D),
        bytes_accessed=rows * (D * 12) + 2 * D * (width + D),
        name="grad_w_mixed",
    )(me, tokens, grad_mixed, *attended, grad_branch)


def back_qkv(me, grad_mixed, grad_res_one, weight):
    rows = grad_res_one.shape[0]
    count = len(weight)
    width = 3 * PART

    def kernel(s, g0_ref, g1_ref, dr_ref, *rest):
        refs, (out_ref, w_ref, sem) = rest[:count], rest[count:]

        @pl.when(pl.program_id(0) == 0)
        def _():
            weight.load(s[0], refs, w_ref, sem)

        out_ref[...] = (
            dot(g0_ref[...], w_ref[0].reshape(D, width), NT)
            + dot(g1_ref[...], w_ref[1].reshape(D, width), NT)
            + dr_ref[...]
        ).astype(bf16)

    return call(
        kernel,
        (rows // TILE,),
        [rows_of(width), rows_of(width), rows_of(D)] + [ANY] * count,
        rows_of(D),
        jax.ShapeDtypeStruct((rows, D), bf16),
        [pltpu.VMEM(weight.shape, bf16), pltpu.SemaphoreType.DMA],
        flops=2 * rows * D * 3 * D,
        bytes_accessed=rows * D * 12 + 2 * D * 3 * D,
        name="back_qkv",
    )(me, *grad_mixed, in_hbm(grad_res_one), *weight.arrays)


def adamw_math(moment, square, gradient):
    first_fix = 1.0 - beta_one**STEP
    second_fix = 1.0 - beta_two**STEP
    moment = beta_one * moment + (1.0 - beta_one) * gradient
    square = beta_two * square + (1.0 - beta_two) * gradient * gradient
    update = moment / first_fix / (jnp.sqrt(square / second_fix) + adam_epsilon)
    return (update, moment, square)


def adamw(moment, square, gradient):
    gradient = gradient.astype(f32)
    return (gradient,) + adamw_math(moment, square, gradient)


def flip(bit):
    return [(i, i ^ bit) for i in range(RANKS)]


def swap(value, bit):
    return lax.ppermute(value, "fsdp", flip(bit))


def after(value, *others):
    return lax.optimization_barrier((value,) + others)[0]


def split_swap(value, even_bit, odd_bit):
    return lax.ppermute(
        value, "fsdp", [(i, i ^ (odd_bit if i & 1 else even_bit)) for i in range(RANKS)]
    )


class Gather:
    def __init__(self, halves, core):
        first = core == 0
        keep = jnp.where(first, halves[0], halves[1]).astype(bf16)
        send = jnp.where(first, halves[1], halves[0]).astype(bf16)
        self.pair = jnp.stack([keep, swap(send, 1)])

    def start(self, *others):
        if others:
            self.pair = after(self.pair, *others)
        self.one = split_swap(self.pair, 2, 4)
        self.two = split_swap(self.pair, 4, 2)

    def direct(self, *others):
        self.start(*others)
        self.far = swap(self.pair, 6)

    def cross(self, *others):
        self.other = [swap(after(piece, *others), 1) for piece in (self.pair, self.one, self.two)]

    def forward(self, *others):
        self.one, self.two = lax.optimization_barrier((self.one, self.two) + others)[:2]
        self.far = split_swap(self.one, 4, 2)
        self.other = [swap(piece, 1) for piece in (self.pair, self.one, self.two)]

    def finish(self, *others):
        self.far = after(self.far, *others)
        self.other.append(swap(self.far, 1))
        return [self.pair, self.one, self.two, self.far] + self.other


def low_sum(*values):
    total = values[0].astype(f32)
    for value in values[1:]:
        total = total + value.astype(f32)
    return total.astype(bf16)


class Scatter:
    def __init__(self, parts):
        self.theirs, self.mine = parts
        self.half = self.mine.shape[1] // 2
        self.got = swap(self.theirs, 1)

    def one(self, *others):
        half, mine = self.half, self.mine
        self.got = after(self.got, *others)
        self.send_x = low_sum(mine[1::2, :half], self.got[1::2, :half])
        self.send_y = low_sum(mine[2:, half:], self.got[2:, half:])
        self.got_x = swap(self.send_x, 2)
        self.got_y = swap(self.send_y, 4)
        return self.send_x, self.send_y

    def two(self, *others):
        half, mine, got = self.half, self.mine, self.got
        self.got_x, self.got_y = lax.optimization_barrier((self.got_x, self.got_y) + others)[:2]
        send_y = low_sum(mine[2, :half], got[2, :half], self.got_x[1])
        send_x = low_sum(mine[1, half:], got[1, half:], self.got_y[1])
        self.last_y = swap(send_y, 4)
        self.last_x = swap(send_x, 2)
        return send_x, send_y

    def three(self, *others):
        half, mine, got = self.half, self.mine, self.got
        self.last_x, self.last_y = lax.optimization_barrier((self.last_x, self.last_y) + others)[:2]
        self.owned = jnp.concatenate(
            [
                low_sum(mine[0, :half], got[0, :half], self.got_x[0], self.last_y),
                low_sum(mine[0, half:], got[0, half:], self.got_y[0], self.last_x),
            ],
            axis=0,
        )
        return (self.owned,)

    def line(self):
        self.near = lax.ppermute(self.owned, "rep", [(0, 1), (3, 2)])

    def four(self, *others):
        self.near = low_sum(self.owned, after(self.near, *others))
        self.across = lax.ppermute(self.near, "rep", [(1, 2), (2, 1)])
        return (self.near,)

    def five(self, *others):
        self.total = low_sum(self.near, after(self.across, *others))
        self.back = lax.ppermute(self.total, "rep", [(1, 0), (2, 3)])
        return (self.total,)

    def all_copies(self):
        near, across, far = [
            lax.ppermute(self.owned, "rep", [(i, i ^ bit) for i in range(4)]).astype(f32)
            for bit in (1, 2, 3)
        ]
        return (self.owned.astype(f32) + near) + (across + far)

    def result(self, rep_index):
        inner = (rep_index == 1) | (rep_index == 2)
        return jnp.where(inner, self.total, self.back)


def gather_small(value, me, position, *others):
    got = after(swap(value, 1 << position), *others)
    low_first = ((me >> position) & 1) == 0
    return jnp.where(low_first, jnp.concatenate([value, got]), jnp.concatenate([got, value]))


def by_head_half(value, half):
    return [value[:, k * D + half * PART : k * D + (half + 1) * PART] for k in range(3)]


def local(
    fsdp,
    rep,
    tokens,
    cotangent,
    lengths,
    w_attn,
    w_in,
    w_out,
    b_in,
    vecs,
    m_attn,
    m_in,
    m_out,
    m_bin,
    m_vecs,
    v_attn,
    v_in,
    v_out,
    v_bin,
    v_vecs,
):
    direct = fsdp == RANKS and rep == 4
    position = lax.axis_index("fsdp")
    rep_index = lax.axis_index("rep")
    part = D // fsdp
    cut = (FF - D) // 2
    middle = w_out.shape[0] // 2
    halves_a = [jnp.concatenate(by_head_half(w_attn, h), axis=1) for h in range(2)]
    halves_b = [jnp.concatenate([w_attn[:, 3 * D :], w_in[:, :cut]], axis=1), w_in[:, cut:]]
    halves_c = [w_out[:middle], w_out[middle:]]
    shape_a = (2, RANKS, SHARD, 3 * PART)
    shape_b = (2, RANKS, SHARD, (D + FF) // 2)
    shape_c = (RANKS, 2, SHARD_FF // 2, D)
    small = jnp.concatenate([vecs.reshape(1, -1), b_in.reshape(1, -1)], axis=1).astype(bf16)
    if direct:
        me = position.reshape(1)
        core = position & 1
        a = Gather(halves_a, core)
        b = Gather(halves_b, core)
        c = Gather(halves_c, core)
        small_all = gather_small(small, position, 0)
        a.start(small_all)
        small_all = gather_small(small_all, position, 1)
        a.forward(small_all)
        small_all = gather_small(small_all, position, 2, a.one, a.two)
        b.start(a.one, a.two)
        weight_a = Weight(a.finish(), shape_a)
    else:
        me = jnp.zeros((1,), jnp.int32)

        def gather(halves, shape):
            halves = [
                lax.all_gather(half.astype(bf16), "fsdp", axis=0, tiled=True) for half in halves
            ]
            return Weight([jnp.stack(halves).reshape(shape)], shape)

        weight_a = gather(halves_a, shape_a)
        weight_b = gather(halves_b, shape_b)
        full_c = lax.all_gather(w_out.astype(bf16), "fsdp", axis=0, tiled=True)
        weight_c = Weight([full_c.reshape(shape_c)], shape_c, by_rank=True)
        small_all = lax.all_gather(small, "fsdp", axis=0, tiled=True)

    def ordered(value, *others):
        return after(value, *others) if direct else value

    small_all = small_all.astype(f32)
    vectors = small_all[:, : 8 * part].reshape(fsdp, 8, part).transpose(1, 0, 2).reshape(8, D)
    in_bias = small_all[:, 8 * part :].reshape(1, FF)
    bias = jnp.stack([vectors[0], jnp.zeros((D,), f32), vectors[1]]).reshape(3, 2, PART)
    bias = bias.transpose(1, 0, 2).reshape(2, 3 * PART)

    qkv = project_qkv(me, tokens, weight_a, bias)
    attended, weights = [None, None], [None, None]
    attended[0], weights[0] = attention(lengths, qkv[0])
    second = qkv[1]
    if direct:
        b.forward(attended[0])
        c.direct(b.one, b.two)
        second = after(second, attended[0], b.one, b.two)
    attended[1], weights[1] = attention(lengths, second)
    if direct:
        weight_b = Weight(b.finish(attended[1]), shape_b)
    normed_one, inv_one, hidden_low, activated, slope, held_b = feed_in(
        me, attended, tokens, weight_b, vectors, in_bias
    )
    if direct:
        c.cross(activated)
        weight_c = Weight(c.finish(), shape_c, by_rank=True)
    output, grad_res_two, grad_ffn, sums_two, held_c = feed_out(
        me, activated, normed_one, cotangent, weight_c, vectors
    )
    held_c = held_c.reshape(RANKS, SHARD_FF, D)

    parts_out = grad_w_out(me, activated, grad_ffn)
    grad_pre, sums_in = back_out(me, ordered(grad_ffn, *parts_out), slope, held_c)
    sent = ()
    if direct:
        r_out = Scatter(parts_out)
        sent = r_out.one(grad_pre)
    parts_in = grad_w_in(me, hidden_low, ordered(grad_pre, *sent))
    grad_res_one, grad_branch, *grad_attended, sums_one = back_in(
        me, ordered(grad_pre, *parts_in), grad_res_two, normed_one, inv_one, held_b, vectors
    )
    if direct:
        r_in = Scatter(parts_in)
        sent = r_out.two(grad_branch) + r_in.one(grad_branch)
    mixed0, sums_q0 = attention_back(
        lengths, qkv[0], weights[0], ordered(grad_attended[0], *sent)
    )
    if direct:
        sent = r_out.three(mixed0)
        r_out.line()
    parts_mix = grad_w_mixed(me, tokens, ordered(mixed0, *sent), attended, grad_branch)
    if direct:
        r_mix = Scatter(parts_mix)
        sent = r_in.two(*parts_mix)
    mixed1, sums_q1 = attention_back(
        lengths, qkv[1], weights[1], ordered(grad_attended[1], *sent, *parts_mix)
    )
    parts_qkv = grad_w_qkv(me, tokens, mixed1, (sums_q0, sums_q1), sums_one, sums_two, sums_in)
    sent = ()
    if direct:
        r_qkv = Scatter(parts_qkv)
        sent = r_in.three(*parts_qkv)
        r_in.line()
        sent = r_mix.one(*sent)
        sent = r_out.four(*sent)
        sent = r_qkv.one(*sent)
    grad_tokens = back_qkv(
        me, (mixed0, ordered(mixed1, *sent, *parts_qkv)), grad_res_one, weight_a
    )
    if direct:
        sent = r_mix.two(grad_tokens)
        sent = r_qkv.two(*sent)
        sent = r_in.four(*sent)
        sent = r_out.five(*sent)
        sent = r_mix.three(*sent)
        r_mix.line()
        sent = r_qkv.three(*sent)
        r_qkv.line()
        sent = r_in.five(*sent)
        sent = r_mix.four(*sent)
        sent = r_qkv.four(*sent)
        sent = r_mix.five(*sent)
        sent = r_qkv.five(*sent)
        sum_qkv = r_qkv.result(rep_index)
        sum_out, sum_in, sum_mix = [r.result(rep_index) for r in (r_out, r_in, r_mix)]
        sum_vecs = sum_qkv[SHARD : SHARD + 8, :part]
        sum_bin = sum_qkv[SHARD, IN_AT : IN_AT + FF // fsdp]
        sum_qkv = sum_qkv[:SHARD]
    else:

        def reduce(theirs, mine):
            full = jnp.stack([mine, theirs], axis=1)
            full = full.reshape(-1, full.shape[-1])
            owned = lax.psum_scatter(full, "fsdp", scatter_dimension=0, tiled=True)
            return lax.psum(owned, "rep")

        sum_out, sum_in, sum_mix = [reduce(*parts) for parts in (parts_out, parts_in, parts_mix)]
        sum_qkv = reduce(*[parts[:, :SHARD] for parts in parts_qkv])
        extra = jnp.stack([parts_qkv[1][:, SHARD:], parts_qkv[0][:, SHARD:]], axis=1)
        extra = extra.reshape(RANKS, EXTRA, 3 * PART).astype(f32)
        extra = lax.psum(extra[:, :8], ("fsdp", "rep"))
        all_vecs = extra[:, :, :SHARD].transpose(1, 0, 2).reshape(8, D)
        all_bin = extra[:, 0, IN_AT : IN_AT + SHARD_FF].reshape(FF)
        sum_vecs = lax.dynamic_slice(all_vecs, (0, position * part), (8, part))
        sum_bin = lax.dynamic_slice(all_bin, (position * (FF // fsdp),), (FF // fsdp,))

    grad_out, step_out, mom_out, sq_out = adamw(m_out, v_out, sum_out)
    grad_in, step_in, mom_in, sq_in = adamw(m_in, v_in, sum_in)
    columns = []
    for k in range(3):
        columns += [sum_mix[:, k * PART : (k + 1) * PART].astype(f32), sum_qkv[:, k * PART : (k + 1) * PART].astype(f32)]
    sum_attn = jnp.concatenate(columns + [sum_mix[:, 3 * PART :].astype(f32)], axis=1)
    grad_attn, step_attn, mom_attn, sq_attn = adamw(m_attn, v_attn, sum_attn)
    grad_bin, step_bin, mom_bin, sq_bin = adamw(m_bin, v_bin, sum_bin)
    grad_vecs, step_vecs, mom_vecs, sq_vecs = adamw(m_vecs, v_vecs, sum_vecs)
    return (
        output,
        grad_tokens,
        grad_attn,
        grad_in,
        grad_out,
        grad_bin,
        grad_vecs,
        step_attn,
        step_in,
        step_out,
        step_bin,
        step_vecs,
        mom_attn,
        mom_in,
        mom_out,
        mom_bin,
        mom_vecs,
        sq_attn,
        sq_in,
        sq_out,
        sq_bin,
        sq_vecs,
    )


def solution(mesh):
    rows, row, col = P(("rep", "fsdp"), None), P("fsdp", None), P(None, "fsdp")
    flat = P("fsdp")
    state = (row, row, row, flat, col)
    return jax.shard_map(
        functools.partial(local, mesh.shape["fsdp"], mesh.shape["rep"]),
        mesh=mesh,
        in_specs=(rows, rows, P(("rep", "fsdp"))) + state * 3,
        out_specs=(rows, rows) + state * 4,
        check_vma=False,
    )
```

```python
import functools

import jax
import jax.numpy as jnp
from jax import lax
from jax.experimental import pallas as pl
from jax.experimental.pallas import tpu as pltpu
from jax.sharding import PartitionSpec as P

D = 768
HEADS = 12
HDIM = 64
PART = D // 2
FF = 3072
SEQ = 128
STEP = 5

RANKS = 8
SHARD = D // RANKS
SHARD_FF = FF // RANKS

beta_one = 0.9
beta_two = 0.999
adam_epsilon = 1e-06
norm_epsilon = 1e-05
masked_score = -1000000000.0

bf16 = jnp.bfloat16
f32 = jnp.float32
NN = (((1,), (0,)), ((), ()))
NT = (((1,), (1,)), ((), ()))
TN = (((0,), (0,)), ((), ()))
VMEM_BYTES = 17 * 1024 * 1024
TILE = 256
LIGHT = 1000


def dot(left, right, dims):
    return lax.dot_general(left, right, dims, preferred_element_type=f32)


def call(kernel, grid, in_specs, out_specs, out_shape, scratch=(), flops=0, bytes_accessed=0, name=None, aliases=None):
    return pl.pallas_call(
        kernel,
        grid_spec=pltpu.PrefetchScalarGridSpec(
            num_scalar_prefetch=1,
            grid=grid,
            in_specs=in_specs,
            out_specs=out_specs,
            scratch_shapes=list(scratch),
        ),
        out_shape=out_shape,
        input_output_aliases=aliases or {},
        compiler_params=pltpu.CompilerParams(
            vmem_limit_bytes=VMEM_BYTES, dimension_semantics=("arbitrary",) * len(grid)
        ),
        cost_estimate=pl.CostEstimate(
            flops=int(flops) // LIGHT, bytes_accessed=int(bytes_accessed) // LIGHT, transcendentals=0
        ),
        name=name,
    )


def rows_of(width, tile=TILE, first=0):
    return pl.BlockSpec((tile, width), lambda i, s: (i + first, 0))


def whole(shape):
    return pl.BlockSpec(shape, lambda i, s: (0,) * len(shape))


ANY = pl.BlockSpec(memory_space=pl.ANY)
HELD = pl.BlockSpec(memory_space=pltpu.VMEM)


def in_vmem(array):
    return pltpu.with_memory_space_constraint(array, pltpu.VMEM)


def in_hbm(array):
    return pltpu.with_memory_space_constraint(array, pltpu.HBM)


class Weight:
    def __init__(self, arrays):
        self.arrays = [in_hbm(array) for array in arrays]
        self.shape = (RANKS,) + self.arrays[0].shape[-2:]

    def __len__(self):
        return len(self.arrays)

    def load(self, me, refs, held, sem):
        if len(refs) == 1:
            copies = [pltpu.make_async_copy(refs[0], held, sem)]
        else:
            copies = []
            for number, ref in enumerate(refs):
                owner = me if number < 4 else me ^ 1
                first = jnp.where((owner & 1) == 0, 2, 4)
                rank = owner ^ (0, first, 6 - first, 6)[number % 4]
                copies.append(pltpu.make_async_copy(ref, held.at[rank], sem))
        for copy in copies:
            copy.start()
        for copy in copies:
            copy.wait()


def lane_sum(value):
    return jnp.sum(value, axis=-1, keepdims=True)


def normalize(residual):
    centre = residual - lane_sum(residual) * (1.0 / D)
    variance = lane_sum(centre * centre) * (1.0 / D)
    inv_std = lax.rsqrt(variance + norm_epsilon)
    return (centre * inv_std, inv_std)


def norm_back(grad_normed, normed, inv_std):
    first_mean = lane_sum(grad_normed) * (1.0 / D)
    second_mean = lane_sum(grad_normed * normed) * (1.0 / D)
    return inv_std * (grad_normed - first_mean - normed * second_mean)


def gelu_and_slope(pre_act):
    cumulative = 0.5 * (1.0 + lax.erf(pre_act * 0.7071067811865476))
    density = jnp.exp(-0.5 * pre_act * pre_act) * 0.3989422804014327
    return (pre_act * cumulative, cumulative + pre_act * density)


def project_qkv(me, tokens, weight, bias):
    rows = tokens.shape[0]
    count = len(weight)
    width = 3 * PART

    def kernel(s, x_ref, b_ref, *rest):
        refs, (out0_ref, out1_ref, w_ref, sem) = rest[:count], rest[count:]

        @pl.when(pl.program_id(0) == 0)
        def _():
            weight.load(s[0], refs, w_ref, sem)

        rounded = (dot(x_ref[...], w_ref[...].reshape(D, 2 * width), NN) + b_ref[...]).astype(bf16)
        for h, out_ref in enumerate((out0_ref, out1_ref)):
            lead = h * width
            out_ref[:, :PART] = rounded[:, lead : lead + PART] * HDIM ** (-0.5)
            out_ref[:, PART:] = rounded[:, lead + PART : lead + width]

    return call(
        kernel,
        (rows // TILE,),
        [rows_of(D), whole((1, 2 * width))] + [ANY] * count,
        [rows_of(width), rows_of(width)],
        [
            pltpu.HBM((rows, width), bf16),
            pltpu.HBM((rows, width), bf16),
        ],
        [pltpu.VMEM(weight.shape, bf16), pltpu.SemaphoreType.DMA],
        flops=2 * rows * D * width * 2,
        bytes_accessed=2 * (rows * D * 4 + 3 * D * D),
        name="qkv",
    )(me, tokens, bias, *weight.arrays)


def head_masks():
    lane = lax.broadcasted_iota(jnp.int32, (SEQ, 2 * HDIM), 1)
    return lane < HDIM


def stack_heads(value, first):
    zero = jnp.zeros_like(value)
    return jnp.concatenate([jnp.where(first, value, zero), jnp.where(first, zero, value)], axis=0)


GROUP = 2


def attention(lengths, qkv):
    rows = qkv.shape[0]
    wide = 2 * HDIM

    def kernel(s, qkv_ref, out_ref, p_ref):
        first = head_masks()
        for g in range(GROUP):
            at = slice(g * SEQ, (g + 1) * SEQ)
            length = s[pl.program_id(0) * GROUP + g]
            valid = lax.broadcasted_iota(jnp.int32, (SEQ, SEQ), 1) < length
            for h in range(PART // wide):
                lanes = slice(h * wide, (h + 1) * wide)
                q = qkv_ref[at, lanes]
                k = qkv_ref[at, PART + h * wide : PART + (h + 1) * wide]
                v = qkv_ref[at, 2 * PART + h * wide : 2 * PART + (h + 1) * wide]
                scores = dot(q, stack_heads(k, first), NT)
                halves = []
                for part in range(2):
                    one = jnp.where(valid, scores[:, part * SEQ : (part + 1) * SEQ], masked_score)
                    top = jnp.max(one, axis=-1, keepdims=True)
                    raised = jnp.exp(one - top)
                    halves.append(raised * (1.0 / lane_sum(raised)))
                weights = jnp.concatenate(halves, axis=1)
                p_ref[at, h * 2 * SEQ : (h + 1) * 2 * SEQ] = weights
                out_ref[at, lanes] = dot(weights.astype(bf16), stack_heads(v, first), NN).astype(bf16)

    width = HEADS * SEQ // 2
    return call(
        kernel,
        (rows // (GROUP * SEQ),),
        [rows_of(3 * PART, GROUP * SEQ)],
        [rows_of(PART, GROUP * SEQ), rows_of(width, GROUP * SEQ)],
        [pltpu.VMEM((rows, PART), bf16), pltpu.HBM((rows, width), f32)],
        flops=4e9,
        bytes_accessed=rows * (PART * 8 + width * 4),
        name="attention",
    )(lengths, in_hbm(qkv))


def project(me, attended, tokens, weight, vectors):
    rows = tokens.shape[0]
    count = len(weight)

    def kernel(s, o0_ref, o1_ref, x_ref, v_ref, *rest):
        refs, (n1_ref, inv_ref, hb_ref, w_ref, sem) = rest[:count], rest[count:]

        @pl.when(pl.program_id(0) == 0)
        def _():
            weight.load(s[0], refs, w_ref, sem)

        both = jnp.concatenate([o0_ref[...], o1_ref[...]], axis=1)
        branch = dot(both, w_ref[:, :, :D].reshape(D, D), NN) + v_ref[2:3, :]
        normed, inv_std = normalize(x_ref[...].astype(f32) + branch)
        n1_ref[...] = normed
        inv_ref[...] = inv_std
        hb_ref[...] = (normed * v_ref[3:4, :] + v_ref[4:5, :]).astype(bf16)

    return call(
        kernel,
        (rows // TILE,),
        [rows_of(PART), rows_of(PART), rows_of(D), whole((8, D))] + [ANY] * count,
        [rows_of(D), rows_of(1), rows_of(D), HELD],
        [
            pltpu.HBM((rows, D), f32),
            pltpu.HBM((rows, 1), f32),
            pltpu.VMEM((rows, D), bf16),
            pltpu.VMEM(weight.shape, bf16),
        ],
        [pltpu.SemaphoreType.DMA],
        flops=2 * rows * D * D,
        bytes_accessed=rows * D * 10 + 2 * D * (D + FF),
        name="project",
    )(me, *[in_vmem(half) for half in attended], tokens, vectors, *weight.arrays)


def expand(me, hidden_low, weight, in_bias):
    rows = hidden_low.shape[0]
    tile = 512

    def kernel(s, h_ref, b_ref, w_ref, f_ref, sl_ref):
        low = h_ref[...]
        for j in range(FF // tile):
            lanes = slice(j * tile, (j + 1) * tile)
            w = w_ref[:, :, D + j * tile : D + (j + 1) * tile].reshape(D, tile)
            act, slope = gelu_and_slope(dot(low, w, NN) + b_ref[:, lanes])
            f_ref[:, lanes] = act.astype(bf16)
            sl_ref[:, lanes] = slope.astype(bf16)

    return call(
        kernel,
        (rows // TILE,),
        [rows_of(D), whole((1, FF)), HELD],
        [rows_of(FF), rows_of(FF)],
        [pltpu.VMEM((rows, FF), bf16), pltpu.VMEM((rows, FF), bf16)],
        flops=2 * rows * D * FF,
        bytes_accessed=rows * (D * 2 + FF * 4) + 2 * D * FF,
        name="expand",
    )(me, in_vmem(hidden_low), in_bias, in_vmem(weight))


def feed_out(me, activated, normed_one, cotangent, weight, vectors):
    rows = activated.shape[0]
    count = len(weight)

    def kernel(s, f_ref, n1_ref, g_ref, v_ref, *rest):
        refs = rest[:count]
        y_ref, dr_ref, dz_ref, sums_ref, w_ref, sem = rest[count:]

        @pl.when(pl.program_id(0) == 0)
        def _():
            weight.load(s[0], refs, w_ref, sem)
            sums_ref[...] = jnp.zeros_like(sums_ref)

        branch = dot(f_ref[...], w_ref[...].reshape(FF, D), NN) + v_ref[5:6, :]
        hidden = n1_ref[...] * v_ref[3:4, :] + v_ref[4:5, :]
        normed, inv_std = normalize(hidden + branch)
        y_ref[...] = (normed * v_ref[6:7, :] + v_ref[7:8, :]).astype(bf16)
        grad_y = g_ref[...].astype(f32)
        sums_ref[1:2, :] += jnp.sum(grad_y * normed, axis=0, keepdims=True)
        sums_ref[2:3, :] += jnp.sum(grad_y, axis=0, keepdims=True)
        grad_res = norm_back(grad_y * v_ref[6:7, :], normed, inv_std)
        dr_ref[...] = grad_res
        low = grad_res.astype(bf16)
        dz_ref[...] = low
        sums_ref[0:1, :] += jnp.sum(low.astype(f32), axis=0, keepdims=True)

    return call(
        kernel,
        (rows // TILE,),
        [rows_of(FF), rows_of(D), rows_of(D), whole((8, D))] + [ANY] * count,
        [rows_of(D), rows_of(D), rows_of(D), whole((8, D)), HELD],
        [
            jax.ShapeDtypeStruct((rows, D), bf16),
            pltpu.HBM((rows, D), f32),
            jax.ShapeDtypeStruct((rows, D), bf16),
            jax.ShapeDtypeStruct((8, D), f32),
            pltpu.VMEM(weight.shape, bf16),
        ],
        [pltpu.SemaphoreType.DMA],
        flops=2 * rows * D * FF,
        bytes_accessed=rows * (D * 14 + FF * 2) + 2 * D * FF,
        name="feed_out",
    )(me, in_vmem(activated), in_hbm(normed_one), cotangent, vectors, *weight.arrays)


def slot(chip, core):
    return jnp.where(core == 0, chip, (chip & 1) * 2 + (chip >> 1))


def grad_w_out(me, activated, grad_ffn):
    rows = activated.shape[0]
    half = RANKS // 2

    def kernel(s, f_ref, dz_ref, t_ref, m_ref):
        block = dot(f_ref[...], dz_ref[...], TN).astype(bf16)
        low, high = block[:SHARD_FF], block[SHARD_FF:]
        even = (s[0] & 1) == 0
        m_ref[0] = jnp.where(even, low, high)
        t_ref[0] = jnp.where(even, high, low)

    shape = pltpu.HBM((half, SHARD_FF, D), bf16)

    def out(flip):
        return pl.BlockSpec((1, SHARD_FF, D), lambda i, s: (slot(i, (s[0] & 1) ^ flip), 0, 0))

    return call(
        kernel,
        (half,),
        [
            pl.BlockSpec((rows, 2 * SHARD_FF), lambda i, s: (0, (s[0] >> 1) ^ i)),
            whole((rows, D)),
        ],
        [out(1), out(0)],
        [shape, shape],
        flops=2 * rows * D * FF,
        bytes_accessed=rows * (D * 2 + FF * 2) + 2 * D * FF,
        name="grad_w_out",
    )(me, in_vmem(activated), grad_ffn)


def back_out(me, grad_ffn, slope, weight):
    rows = grad_ffn.shape[0]

    def kernel(s, dz_ref, sl_ref, w_ref, du_ref, sums_ref):
        @pl.when(pl.program_id(0) == 0)
        def _():
            sums_ref[...] = jnp.zeros_like(sums_ref)

        dz = dz_ref[...]
        for r in range(RANKS // 2):
            lanes = slice(2 * r * SHARD_FF, 2 * (r + 1) * SHARD_FF)
            w = w_ref[2 * r : 2 * r + 2].reshape(2 * SHARD_FF, D)
            grad = dot(dz, w, NT) * sl_ref[:, lanes].astype(f32)
            low = grad.astype(bf16)
            du_ref[:, lanes] = low
            sums_ref[:, lanes] += jnp.sum(low.astype(f32), axis=0, keepdims=True)

    return call(
        kernel,
        (rows // TILE,),
        [rows_of(D), rows_of(FF), HELD],
        [rows_of(FF), whole((1, FF))],
        [pltpu.VMEM((rows, FF), bf16), jax.ShapeDtypeStruct((1, FF), f32)],
        flops=2 * rows * D * FF,
        bytes_accessed=rows * (D * 2 + FF * 4) + 2 * D * FF,
        name="back_out",
    )(me, grad_ffn, in_vmem(slope), in_vmem(weight))


def back_in(me, grad_pre, grad_res_two, normed_one, inv_one, weight, vectors):
    rows = grad_pre.shape[0]

    def kernel(
        s, du_ref, dr2_ref, n1_ref, inv_ref, v_ref, w_ref, dr1_ref, da_ref, do0_ref, do1_ref, sums_ref
    ):
        @pl.when(pl.program_id(0) == 0)
        def _():
            sums_ref[...] = jnp.zeros_like(sums_ref)

        w_in = w_ref[:, :, D:].reshape(D, FF)
        grad_hidden = dot(du_ref[...], w_in, NT) + dr2_ref[...]
        normed = n1_ref[...]
        sums_ref[1:2, :] += jnp.sum(grad_hidden * normed, axis=0, keepdims=True)
        sums_ref[2:3, :] += jnp.sum(grad_hidden, axis=0, keepdims=True)
        grad_res = norm_back(grad_hidden * v_ref[3:4, :], normed, inv_ref[...])
        dr1_ref[...] = grad_res
        low = grad_res.astype(bf16)
        da_ref[...] = low
        sums_ref[0:1, :] += jnp.sum(low.astype(f32), axis=0, keepdims=True)
        w_proj = w_ref[:, :, :D].reshape(D, D)
        grad_attended = dot(low, w_proj, NT).astype(bf16)
        do0_ref[...] = grad_attended[:, :PART]
        do1_ref[...] = grad_attended[:, PART:]

    return call(
        kernel,
        (rows // TILE,),
        [rows_of(FF), rows_of(D), rows_of(D), rows_of(1), whole((8, D))] + [HELD],
        [rows_of(D), rows_of(D), rows_of(PART), rows_of(PART), whole((8, D))],
        [
            pltpu.HBM((rows, D), f32),
            pltpu.VMEM((rows, D), bf16),
            pltpu.VMEM((rows, PART), bf16),
            pltpu.VMEM((rows, PART), bf16),
            jax.ShapeDtypeStruct((8, D), f32),
        ],
        flops=2 * rows * D * (D + FF),
        bytes_accessed=rows * (D * 16 + FF * 2) + 2 * D * (D + FF),
        name="back_in",
    )(
        me,
        in_vmem(grad_pre),
        in_hbm(grad_res_two),
        in_hbm(normed_one),
        in_hbm(inv_one),
        vectors,
        in_vmem(weight),
    )


def store_by_rank(s, block, t_ref, m_ref, first=0):
    core = s[0] & 1
    lanes = slice(first, first + block.shape[1])
    for k in range(RANKS // 2):
        low = block[2 * k * SHARD : (2 * k + 1) * SHARD]
        high = block[(2 * k + 1) * SHARD : (2 * k + 2) * SHARD]
        away = (s[0] >> 1) ^ k
        m_ref[slot(away, core), :SHARD, lanes] = jnp.where(core == 0, low, high)
        t_ref[slot(away, 1 - core), :SHARD, lanes] = jnp.where(core == 0, high, low)


def grad_w_in(me, hidden_low, grad_pre):
    rows = hidden_low.shape[0]
    half = RANKS // 2

    def kernel(s, h_ref, du_ref, t_ref, m_ref):
        store_by_rank(s, dot(h_ref[...], du_ref[...], TN).astype(bf16), t_ref, m_ref)

    shape = pltpu.HBM((half, SHARD, FF), bf16)
    out = pl.BlockSpec((half, SHARD, D), lambda i, s: (0, 0, i))
    return call(
        kernel,
        (FF // D,),
        [whole((rows, D)), pl.BlockSpec((rows, D), lambda i, s: (0, i))],
        [out, out],
        [shape, shape],
        flops=2 * rows * D * FF,
        bytes_accessed=rows * (D * 4 + FF * 2) + 2 * D * FF,
        name="grad_w_in",
    )(me, in_vmem(hidden_low), in_vmem(grad_pre))


def attention_back(lengths, qkv, weights, grad_attended):
    rows = qkv.shape[0]
    scale = HDIM ** (-0.5)
    wide = 2 * HDIM
    width = HEADS * SEQ // 2

    def kernel(s, qkv_ref, p_ref, do_ref, out_ref, sums_ref):
        @pl.when(pl.program_id(0) == 0)
        def _():
            sums_ref[...] = jnp.zeros_like(sums_ref)

        first = head_masks()
        for g in range(GROUP):
            at = slice(g * SEQ, (g + 1) * SEQ)
            for h in range(PART // wide):
                lanes = slice(h * wide, (h + 1) * wide)
                k_lanes = slice(PART + h * wide, PART + (h + 1) * wide)
                v_lanes = slice(2 * PART + h * wide, 2 * PART + (h + 1) * wide)
                q, k, v = qkv_ref[at, lanes], qkv_ref[at, k_lanes], qkv_ref[at, v_lanes]
                grad_out = do_ref[at, lanes]
                p = p_ref[at, h * 2 * SEQ : (h + 1) * 2 * SEQ]
                grad_p = dot(grad_out, stack_heads(v, first), NT)
                both = grad_p * p
                halves = []
                for part in range(2):
                    cut = slice(part * SEQ, (part + 1) * SEQ)
                    inner = grad_p[:, cut] - lane_sum(both[:, cut])
                    halves.append((p[:, cut] * inner).astype(bf16))
                grad_s = jnp.concatenate(halves, axis=1)
                grad_v = dot(p.astype(bf16), grad_out, TN)
                grad_v = jnp.where(first, grad_v[:SEQ], grad_v[SEQ:]).astype(bf16)
                grad_q = (dot(grad_s, stack_heads(k, first), NN) * scale).astype(bf16)
                grad_k = dot(grad_s, q, TN)
                grad_k = jnp.where(first, grad_k[:SEQ], grad_k[SEQ:]).astype(bf16)
                out_ref[at, lanes] = grad_q
                out_ref[at, k_lanes] = grad_k
                out_ref[at, v_lanes] = grad_v
                sums_ref[0:1, lanes] += jnp.sum(grad_q.astype(f32), axis=0, keepdims=True)
                sums_ref[1:2, lanes] += jnp.sum(grad_v.astype(f32), axis=0, keepdims=True)

    return call(
        kernel,
        (rows // (GROUP * SEQ),),
        [rows_of(3 * PART, GROUP * SEQ), rows_of(width, GROUP * SEQ), rows_of(PART, GROUP * SEQ)],
        [rows_of(3 * PART, GROUP * SEQ), whole((8, PART))],
        [pltpu.VMEM((rows, 3 * PART), bf16), jax.ShapeDtypeStruct((8, PART), f32)],
        flops=7e9,
        bytes_accessed=rows * (PART * 14 + width * 4),
        name="attention_back",
    )(lengths, in_hbm(qkv), in_hbm(weights), in_vmem(grad_attended))


EXTRA = 16
IN_AT = 128


def grad_w_qkv(me, tokens, grad_mixed, sums_qkv, sums_one, sums_two, sums_in):
    rows = tokens.shape[0]
    half = RANKS // 2
    width = 3 * PART

    def kernel(s, x_ref, g_ref, q0_ref, q1_ref, one_ref, two_ref, in_ref, t_ref, m_ref):
        store_by_rank(s, dot(x_ref[...], g_ref[...], TN).astype(bf16), t_ref, m_ref)
        vectors = jnp.concatenate(
            [
                jnp.concatenate([q0_ref[0:2], q1_ref[0:2]], axis=1),
                one_ref[0:3],
                two_ref[0:3],
            ],
            axis=0,
        )
        core = s[0] & 1
        end = IN_AT + SHARD_FF
        rest = jnp.zeros((EXTRA, width - end), bf16)
        for k in range(half):
            blocks = []
            for rank in (2 * k, 2 * k + 1):
                vec = vectors[:, rank * SHARD : (rank + 1) * SHARD]
                vec = jnp.concatenate([vec, jnp.zeros((8, IN_AT - SHARD), f32)], axis=1)
                bias = in_ref[:, rank * SHARD_FF : (rank + 1) * SHARD_FF]
                bias = jnp.concatenate([bias, jnp.zeros((7, SHARD_FF), f32)], axis=0)
                block = jnp.concatenate([vec, bias], axis=1)
                blocks.append(jnp.concatenate([block, jnp.zeros_like(block)], axis=0).astype(bf16))
            away = (s[0] >> 1) ^ k
            for ref, here, block in (
                (m_ref, core, jnp.where(core == 0, blocks[0], blocks[1])),
                (t_ref, 1 - core, jnp.where(core == 0, blocks[1], blocks[0])),
            ):
                ref[slot(away, here), SHARD:, :end] = block
                ref[slot(away, here), SHARD:, end:] = rest

    shape = pltpu.HBM((half, SHARD + EXTRA, width), bf16)
    out = whole((half, SHARD + EXTRA, width))
    return call(
        kernel,
        (1,),
        [
            whole((rows, D)),
            HELD,
            whole((8, PART)),
            whole((8, PART)),
            whole((8, D)),
            whole((8, D)),
            whole((1, FF)),
        ],
        [out, out],
        [shape, shape],
        flops=2 * rows * D * width,
        bytes_accessed=rows * (D * 8) + 2 * D * width,
        name="grad_w_qkv",
    )(me, tokens, in_vmem(grad_mixed), *sums_qkv, sums_one, sums_two, sums_in)


def grad_w_mixed(me, tokens, grad_mixed, attended, grad_branch):
    rows = tokens.shape[0]
    half = RANKS // 2
    width = 3 * PART

    def kernel(s, x_ref, g_ref, o0_ref, o1_ref, da_ref, t_ref, m_ref):
        store_by_rank(s, dot(x_ref[...], g_ref[...], TN).astype(bf16), t_ref, m_ref)
        both = jnp.concatenate([o0_ref[...], o1_ref[...]], axis=1)
        proj = dot(both, da_ref[...], TN).astype(bf16)
        store_by_rank(s, proj, t_ref, m_ref, width)

    shape = pltpu.HBM((half, SHARD, width + D), bf16)
    out = whole((half, SHARD, width + D))
    return call(
        kernel,
        (1,),
        [
            whole((rows, D)),
            HELD,
            HELD,
            HELD,
            HELD,
        ],
        [out, out],
        [shape, shape],
        flops=2 * rows * D * (width + D),
        bytes_accessed=rows * (D * 12) + 2 * D * (width + D),
        name="grad_w_mixed",
    )(
        me,
        tokens,
        in_vmem(grad_mixed),
        *[in_vmem(half) for half in attended],
        in_vmem(grad_branch),
    )


def back_qkv(me, grad_mixed, grad_res_one, weight, before=None):
    rows = grad_res_one.shape[0]
    steps = rows // TILE // 2
    width = 3 * PART

    def compute(g0_ref, g1_ref, dr_ref, w_ref, out_ref):
        both = jnp.concatenate([g0_ref[...], g1_ref[...]], axis=1)
        w = w_ref[...].reshape(D, 2 * width)
        out_ref[...] = (dot(both, w, NT) + dr_ref[...]).astype(bf16)

    def kernel_one(s, g0_ref, g1_ref, dr_ref, *rest):
        refs, (out_ref, w_ref, sem) = rest[: len(weight)], rest[len(weight) :]

        @pl.when(pl.program_id(0) == 0)
        def _():
            weight.load(s[0], refs, w_ref, sem)

        compute(g0_ref, g1_ref, dr_ref, w_ref, out_ref)

    def kernel_two(s, g0_ref, g1_ref, dr_ref, w_ref, before_ref, out_ref):
        compute(g0_ref, g1_ref, dr_ref, w_ref, out_ref)

    def at(width):
        return rows_of(width, TILE, steps if before is not None else 0)

    operands = (me, *[in_vmem(half) for half in grad_mixed], in_hbm(grad_res_one))
    blocks = [at(width), at(width), at(D)]
    out = pltpu.HBM((rows, D), bf16)
    cost = dict(flops=rows * D * 3 * D, bytes_accessed=rows * D * 6 + 2 * D * 3 * D, name="back_qkv")
    if before is None:
        return call(
            kernel_one,
            (steps,),
            blocks + [ANY] * len(weight),
            [at(D), HELD],
            [out, pltpu.VMEM(weight.shape, bf16)],
            [pltpu.SemaphoreType.DMA],
            **cost,
        )(*operands, *weight.arrays)
    return call(
        kernel_two, (steps,), blocks + [HELD, ANY], at(D), out, aliases={5: 0}, **cost
    )(*operands, in_vmem(weight), in_hbm(before))


def adamw_math(moment, square, gradient):
    first_fix = 1.0 - beta_one**STEP
    second_fix = 1.0 - beta_two**STEP
    moment = beta_one * moment + (1.0 - beta_one) * gradient
    square = beta_two * square + (1.0 - beta_two) * gradient * gradient
    update = moment / first_fix / (jnp.sqrt(square / second_fix) + adam_epsilon)
    return (update, moment, square)


def adamw(moment, square, gradient):
    gradient = gradient.astype(f32)
    return (gradient,) + adamw_math(moment, square, gradient)


def flip(bit):
    return [(i, i ^ bit) for i in range(RANKS)]


def swap(value, bit):
    return lax.ppermute(value, "fsdp", flip(bit))


def after(value, *others):
    return lax.optimization_barrier((value,) + others)[0]


def split_swap(value, even_bit, odd_bit):
    return lax.ppermute(
        value, "fsdp", [(i, i ^ (odd_bit if i & 1 else even_bit)) for i in range(RANKS)]
    )


class Gather:
    def __init__(self, shard):
        self.shard = shard

    def start(self, *others):
        if others:
            self.shard = after(self.shard, *others)
        self.one = split_swap(self.shard, 2, 4)
        self.two = split_swap(self.shard, 4, 2)

    def forward(self, *others):
        self.one, self.two = lax.optimization_barrier((self.one, self.two) + others)[:2]
        self.far = split_swap(self.one, 4, 2)
        self.other = [swap(piece, 1) for piece in (self.shard, self.one, self.two)]

    def finish(self, *others):
        self.far = after(self.far, *others)
        self.other.append(swap(self.far, 1))
        return Weight([self.shard, self.one, self.two, self.far] + self.other)


def low_sum(*values):
    total = values[0].astype(f32)
    for value in values[1:]:
        total = total + value.astype(f32)
    return total.astype(bf16)


class Scatter:
    def __init__(self, parts):
        self.theirs, self.mine = parts
        self.got = swap(self.theirs, 1)

    def one(self, *others):
        self.got = after(self.got, *others)
        send = low_sum(self.mine[1::2], self.got[1::2])
        self.near_got = split_swap(send, 2, 4)
        return (send,)

    def two(self, *others):
        self.near_got = after(self.near_got, *others)
        send = low_sum(self.mine[2], self.got[2], self.near_got[1])
        self.last = split_swap(send, 4, 2)
        return (send,)

    def three(self, *others):
        last = after(self.last, *others)
        self.owned = low_sum(self.mine[0], self.got[0], self.near_got[0], last)
        return (self.owned,)

    def line(self):
        self.near = lax.ppermute(self.owned, "rep", [(0, 1), (3, 2)])

    def four(self, *others):
        self.near = low_sum(self.owned, after(self.near, *others))
        self.across = lax.ppermute(self.near, "rep", [(1, 2), (2, 1)])
        return (self.near,)

    def five(self, *others):
        self.total = low_sum(self.near, after(self.across, *others))
        self.back = lax.ppermute(self.total, "rep", [(1, 0), (2, 3)])
        return (self.total,)

    def result(self, rep_index):
        inner = (rep_index == 1) | (rep_index == 2)
        return jnp.where(inner, self.total, self.back)


def by_rank(pairs, position):
    stacked = jnp.stack(pairs)
    stacked = jnp.where((position & 2) == 0, stacked, stacked[jnp.array([1, 0, 3, 2])])
    stacked = jnp.where((position & 4) == 0, stacked, stacked[jnp.array([2, 3, 0, 1])])
    return stacked.reshape(RANKS, -1)


def by_head_half(value, half):
    return [value[:, k * D + half * PART : k * D + (half + 1) * PART] for k in range(3)]


def local(
    fsdp,
    rep,
    tokens,
    cotangent,
    lengths,
    w_attn,
    w_in,
    w_out,
    b_in,
    vecs,
    m_attn,
    m_in,
    m_out,
    m_bin,
    m_vecs,
    v_attn,
    v_in,
    v_out,
    v_bin,
    v_vecs,
):
    direct = fsdp == RANKS and rep == 4
    position = lax.axis_index("fsdp")
    rep_index = lax.axis_index("rep")
    part = D // fsdp
    heads_a = [jnp.concatenate(by_head_half(w_attn, h), axis=1) for h in range(2)]
    low_a = jnp.concatenate(heads_a, axis=1).astype(bf16)
    if direct:
        me = position.reshape(1)
        a = Gather(low_a)
        a.start()
        wait = lambda value: after(value, low_a)
    else:
        me = jnp.zeros((1,), jnp.int32)
        wait = lambda value: value
    low_b = jnp.concatenate([wait(w_attn)[:, 3 * D :], w_in], axis=1).astype(bf16)
    low_c = wait(w_out).astype(bf16)
    small = jnp.concatenate([wait(vecs).reshape(1, -1), b_in.reshape(1, -1)], axis=1).astype(bf16)
    if direct:
        b = Gather(low_b)
        c = Gather(low_c)
        got = swap(small, 1)
        first = (position & 1) == 0
        pair = jnp.concatenate([jnp.where(first, small, got), jnp.where(first, got, small)])
        pairs = [pair] + [swap(pair, bit) for bit in (2, 4, 6)]
        a.forward(*pairs)
        b.start(a.one, a.two, *pairs)
        small_all = by_rank(pairs, position)
        weight_a = a.finish()
    else:

        def gather(low):
            full = lax.all_gather(low, "fsdp", axis=0, tiled=True)
            return Weight([full.reshape(RANKS, -1, full.shape[1])])

        weight_a, weight_b, weight_c = gather(low_a), gather(low_b), gather(low_c)
        small_all = lax.all_gather(small, "fsdp", axis=0, tiled=True)

    def ordered(value, *others):
        return after(value, *others) if direct else value

    small_all = small_all.astype(f32)
    vectors = small_all[:, : 8 * part].reshape(fsdp, 8, part).transpose(1, 0, 2).reshape(8, D)
    in_bias = small_all[:, 8 * part :].reshape(1, FF)
    bias = jnp.stack([vectors[0], jnp.zeros((D,), f32), vectors[1]]).reshape(3, 2, PART)
    bias = bias.transpose(1, 0, 2).reshape(1, 6 * PART)

    qkv = project_qkv(me, tokens, weight_a, bias)
    attended, weights = [None, None], [None, None]
    first, second = qkv
    if direct:
        b.forward(*qkv)
        first = after(first, b.one, b.two)
    attended[0], weights[0] = attention(lengths, first)
    if direct:
        c.start(attended[0], *b.other)
        second = after(second, attended[0], *b.other)
        weight_b = b.finish(attended[0])
    attended[1], weights[1] = attention(lengths, second)
    normed_one, inv_one, hidden_low, held_b = project(me, attended, tokens, weight_b, vectors)
    inner = hidden_low
    if direct:
        c.forward(hidden_low)
        inner = after(hidden_low, c.one, c.two)
    activated, slope = expand(me, inner, held_b, in_bias)
    if direct:
        weight_c = c.finish(activated)
    output, grad_res_two, grad_ffn, sums_two, held_c = feed_out(
        me, activated, normed_one, cotangent, weight_c, vectors
    )

    parts_out = grad_w_out(me, activated, grad_ffn)
    grad_pre, sums_in = back_out(me, ordered(grad_ffn, *parts_out), slope, held_c)
    sent = ()
    if direct:
        r_out = Scatter(parts_out)
        sent = r_out.one(grad_pre)
    parts_in = grad_w_in(me, hidden_low, ordered(grad_pre, *sent))
    grad_res_one, grad_branch, *grad_attended, sums_one = back_in(
        me, ordered(grad_pre, *parts_in), grad_res_two, normed_one, inv_one, held_b, vectors
    )
    sent = ()
    if direct:
        r_in = Scatter(parts_in)
        sent = r_out.two(grad_branch) + r_in.one(grad_branch)
    mixed0, sums_q0 = attention_back(
        lengths, qkv[0], weights[0], ordered(grad_attended[0], *sent)
    )
    parts_mix = grad_w_mixed(me, tokens, mixed0, attended, grad_branch)
    sent = parts_mix
    if direct:
        r_mix = Scatter(parts_mix)
        sent = r_out.three(*parts_mix)
        r_out.line()
        sent = r_in.two(*sent)
    mixed1, sums_q1 = attention_back(
        lengths, qkv[1], weights[1], ordered(grad_attended[1], *sent)
    )
    parts_qkv = grad_w_qkv(me, tokens, mixed1, (sums_q0, sums_q1), sums_one, sums_two, sums_in)
    sent = ()
    if direct:
        r_qkv = Scatter(parts_qkv)
        sent = r_in.three(*parts_qkv)
        r_in.line()
        sent = r_mix.one(*sent)
        sent = r_qkv.one(*sent)
        sent = r_out.four(*sent)
    half_tokens, held_a = back_qkv(
        me, (mixed0, ordered(mixed1, *sent, *parts_qkv)), grad_res_one, weight_a
    )
    sent = ()
    if direct:
        sent = r_mix.two(half_tokens)
        sent = r_qkv.two(*sent)
        sent = r_in.four(*sent)
    grad_tokens = back_qkv(
        me, (mixed0, ordered(mixed1, *sent)), grad_res_one, held_a, half_tokens
    )
    if direct:
        sent = r_qkv.three(grad_tokens)
        r_qkv.line()
        sent = r_mix.three(*sent)
        r_mix.line()
        sent = r_out.five(*sent)
        sent = r_in.five(*sent)
        sent = r_qkv.four(*sent)
        sent = r_mix.four(*sent)
        sent = r_qkv.five(*sent)
        sent = r_mix.five(*sent)
        sum_qkv = r_qkv.result(rep_index)
        sum_out, sum_in, sum_mix = [r.result(rep_index) for r in (r_out, r_in, r_mix)]
        sum_vecs = sum_qkv[SHARD : SHARD + 8, :part]
        sum_bin = sum_qkv[SHARD, IN_AT : IN_AT + FF // fsdp]
        sum_qkv = sum_qkv[:SHARD]
    else:

        def reduce(theirs, mine):
            full = jnp.stack([mine, theirs[jnp.array([0, 2, 1, 3])]], axis=1)
            full = full.reshape(-1, full.shape[-1])
            owned = lax.psum_scatter(full, "fsdp", scatter_dimension=0, tiled=True)
            return lax.psum(owned, "rep")

        sum_out, sum_in, sum_mix = [reduce(*parts) for parts in (parts_out, parts_in, parts_mix)]
        sum_qkv = reduce(*[parts[:, :SHARD] for parts in parts_qkv])
        theirs, mine = [parts[:, SHARD:] for parts in parts_qkv]
        extra = jnp.stack([mine, theirs[jnp.array([0, 2, 1, 3])]], axis=1)
        extra = extra.reshape(RANKS, EXTRA, 3 * PART).astype(f32)
        extra = lax.psum(extra[:, :8], ("fsdp", "rep"))
        all_vecs = extra[:, :, :SHARD].transpose(1, 0, 2).reshape(8, D)
        all_bin = extra[:, 0, IN_AT : IN_AT + SHARD_FF].reshape(FF)
        sum_vecs = lax.dynamic_slice(all_vecs, (0, position * part), (8, part))
        sum_bin = lax.dynamic_slice(all_bin, (position * (FF // fsdp),), (FF // fsdp,))

    grad_out, step_out, mom_out, sq_out = adamw(m_out, v_out, sum_out)
    grad_in, step_in, mom_in, sq_in = adamw(m_in, v_in, sum_in)
    columns = []
    for k in range(3):
        columns += [sum_mix[:, k * PART : (k + 1) * PART].astype(f32), sum_qkv[:, k * PART : (k + 1) * PART].astype(f32)]
    sum_attn = jnp.concatenate(columns + [sum_mix[:, 3 * PART :].astype(f32)], axis=1)
    grad_attn, step_attn, mom_attn, sq_attn = adamw(m_attn, v_attn, sum_attn)
    grad_bin, step_bin, mom_bin, sq_bin = adamw(m_bin, v_bin, sum_bin)
    grad_vecs, step_vecs, mom_vecs, sq_vecs = adamw(m_vecs, v_vecs, sum_vecs)
    return (
        output,
        grad_tokens,
        grad_attn,
        grad_in,
        grad_out,
        grad_bin,
        grad_vecs,
        step_attn,
        step_in,
        step_out,
        step_bin,
        step_vecs,
        mom_attn,
        mom_in,
        mom_out,
        mom_bin,
        mom_vecs,
        sq_attn,
        sq_in,
        sq_out,
        sq_bin,
        sq_vecs,
    )


def solution(mesh):
    rows, row, col = P(("rep", "fsdp"), None), P("fsdp", None), P(None, "fsdp")
    flat = P("fsdp")
    state = (row, row, row, flat, col)
    return jax.shard_map(
        functools.partial(local, mesh.shape["fsdp"], mesh.shape["rep"]),
        mesh=mesh,
        in_specs=(rows, rows, P(("rep", "fsdp"))) + state * 3,
        out_specs=(rows, rows) + state * 4,
        check_vma=False,
    )
```

```python
import functools

import jax
import jax.numpy as jnp
from jax import lax
from jax.experimental import pallas as pl
from jax.experimental.pallas import tpu as pltpu
from jax.sharding import PartitionSpec as P

D = 768
HEADS = 12
HDIM = 64
PART = D // 2
FF = 3072
SEQ = 128
STEP = 5

RANKS = 8
SHARD = D // RANKS
SHARD_FF = FF // RANKS

beta_one = 0.9
beta_two = 0.999
adam_epsilon = 1e-06
norm_epsilon = 1e-05
masked_score = -1000000000.0

bf16 = jnp.bfloat16
f32 = jnp.float32
NN = (((1,), (0,)), ((), ()))
NT = (((1,), (1,)), ((), ()))
TN = (((0,), (0,)), ((), ()))
VMEM_BYTES = 17 * 1024 * 1024
TILE = 256
LIGHT = 1000


def dot(left, right, dims):
    return lax.dot_general(left, right, dims, preferred_element_type=f32)


def call(kernel, grid, in_specs, out_specs, out_shape, scratch=(), flops=0, bytes_accessed=0, name=None, aliases=None):
    return pl.pallas_call(
        kernel,
        grid_spec=pltpu.PrefetchScalarGridSpec(
            num_scalar_prefetch=1,
            grid=grid,
            in_specs=in_specs,
            out_specs=out_specs,
            scratch_shapes=list(scratch),
        ),
        out_shape=out_shape,
        input_output_aliases=aliases or {},
        compiler_params=pltpu.CompilerParams(
            vmem_limit_bytes=VMEM_BYTES, dimension_semantics=("arbitrary",) * len(grid)
        ),
        cost_estimate=pl.CostEstimate(
            flops=int(flops) // LIGHT, bytes_accessed=int(bytes_accessed) // LIGHT, transcendentals=0
        ),
        name=name,
    )


def rows_of(width, tile=TILE, first=0):
    return pl.BlockSpec((tile, width), lambda i, s: (i + first, 0))


def whole(shape):
    return pl.BlockSpec(shape, lambda i, s: (0,) * len(shape))


ANY = pl.BlockSpec(memory_space=pl.ANY)
HELD = pl.BlockSpec(memory_space=pltpu.VMEM)


def in_vmem(array):
    return pltpu.with_memory_space_constraint(array, pltpu.VMEM)


def in_hbm(array):
    return pltpu.with_memory_space_constraint(array, pltpu.HBM)


class Weight:
    def __init__(self, arrays):
        self.arrays = [in_hbm(array) for array in arrays]
        self.shape = (RANKS,) + self.arrays[0].shape[-2:]

    def __len__(self):
        return len(self.arrays)

    def load(self, me, refs, held, sem):
        if len(refs) == 1:
            copies = [pltpu.make_async_copy(refs[0], held, sem)]
        else:
            copies = []
            for number, ref in enumerate(refs):
                owner = me if number < 4 else me ^ 1
                first = jnp.where((owner & 1) == 0, 2, 4)
                rank = owner ^ (0, first, 6 - first, 6)[number % 4]
                copies.append(pltpu.make_async_copy(ref, held.at[rank], sem))
        for copy in copies:
            copy.start()
        for copy in copies:
            copy.wait()


def lane_sum(value):
    return jnp.sum(value, axis=-1, keepdims=True)


def normalize(residual):
    centre = residual - lane_sum(residual) * (1.0 / D)
    variance = lane_sum(centre * centre) * (1.0 / D)
    inv_std = lax.rsqrt(variance + norm_epsilon)
    return (centre * inv_std, inv_std)


def norm_back(grad_normed, normed, inv_std):
    first_mean = lane_sum(grad_normed) * (1.0 / D)
    second_mean = lane_sum(grad_normed * normed) * (1.0 / D)
    return inv_std * (grad_normed - first_mean - normed * second_mean)


def gelu_and_slope(pre_act):
    cumulative = 0.5 * (1.0 + lax.erf(pre_act * 0.7071067811865476))
    density = jnp.exp(-0.5 * pre_act * pre_act) * 0.3989422804014327
    return (pre_act * cumulative, cumulative + pre_act * density)


def project_qkv(me, tokens, weight, bias):
    rows = tokens.shape[0]
    count = len(weight)
    width = 3 * PART

    def kernel(s, x_ref, b_ref, *rest):
        refs, (out0_ref, out1_ref, w_ref, sem) = rest[:count], rest[count:]

        @pl.when(pl.program_id(0) == 0)
        def _():
            weight.load(s[0], refs, w_ref, sem)

        rounded = (dot(x_ref[...], w_ref[...].reshape(D, 2 * width), NN) + b_ref[...]).astype(bf16)
        for h, out_ref in enumerate((out0_ref, out1_ref)):
            lead = h * width
            out_ref[:, :PART] = rounded[:, lead : lead + PART] * HDIM ** (-0.5)
            out_ref[:, PART:] = rounded[:, lead + PART : lead + width]

    return call(
        kernel,
        (rows // TILE,),
        [rows_of(D), whole((1, 2 * width))] + [ANY] * count,
        [rows_of(width), rows_of(width)],
        [
            pltpu.HBM((rows, width), bf16),
            pltpu.HBM((rows, width), bf16),
        ],
        [pltpu.VMEM(weight.shape, bf16), pltpu.SemaphoreType.DMA],
        flops=2 * rows * D * width * 2,
        bytes_accessed=2 * (rows * D * 4 + 3 * D * D),
        name="qkv",
    )(me, tokens, bias, *weight.arrays)


def head_masks():
    lane = lax.broadcasted_iota(jnp.int32, (SEQ, 2 * HDIM), 1)
    return lane < HDIM


def stack_heads(value, first):
    zero = jnp.zeros_like(value)
    return jnp.concatenate([jnp.where(first, value, zero), jnp.where(first, zero, value)], axis=0)


GROUP = 4


def by_stages(units, stages):
    for stage in stages:
        for unit in units:
            stage(unit)


def staggered(units, stages):
    for start in range(len(units) + len(stages) - 1):
        for number in reversed(range(len(stages))):
            if 0 <= start - number < len(units):
                stages[number](units[start - number])


def place(unit, part=0):
    lead = part * PART + unit[1] * 2 * HDIM
    return slice(unit[0] * SEQ, (unit[0] + 1) * SEQ), slice(lead, lead + 2 * HDIM)


def weight_place(unit):
    return slice(unit[0] * SEQ, (unit[0] + 1) * SEQ), slice(unit[1] * 2 * SEQ, (unit[1] + 1) * 2 * SEQ)


UNITS = [(pair, heads) for pair in range(GROUP) for heads in range(PART // (2 * HDIM))]


def attention(lengths, qkv):
    rows = qkv.shape[0]

    def kernel(s, qkv_ref, out_ref, p_ref):
        first = head_masks()
        key = lax.broadcasted_iota(jnp.int32, (SEQ, SEQ), 1)
        valid = [key < s[pl.program_id(0) * GROUP + pair] for pair in range(GROUP)]
        scores, low = {}, {}

        def score(unit):
            keys = stack_heads(qkv_ref[place(unit, 1)], first)
            scores[unit] = dot(qkv_ref[place(unit)], keys, NT)

        def soften(unit):
            halves = []
            for part in range(2):
                one = scores[unit][:, part * SEQ : (part + 1) * SEQ]
                one = jnp.where(valid[unit[0]], one, masked_score)
                raised = jnp.exp(one - jnp.max(one, axis=-1, keepdims=True))
                halves.append(raised * (1.0 / lane_sum(raised)))
            weights = jnp.concatenate(halves, axis=1)
            p_ref[weight_place(unit)] = weights
            low[unit] = weights.astype(bf16)

        def attend(unit):
            values = stack_heads(qkv_ref[place(unit, 2)], first)
            out_ref[place(unit)] = dot(low[unit], values, NN).astype(bf16)

        staggered(UNITS, (score, soften, attend))

    width = HEADS * SEQ // 2
    return call(
        kernel,
        (rows // (GROUP * SEQ),),
        [rows_of(3 * PART, GROUP * SEQ)],
        [rows_of(PART, GROUP * SEQ), rows_of(width, GROUP * SEQ)],
        [pltpu.VMEM((rows, PART), bf16), pltpu.HBM((rows, width), f32)],
        flops=4e9,
        bytes_accessed=rows * (PART * 8 + width * 4),
        name="attention",
    )(lengths, in_hbm(qkv))


def project(me, attended, tokens, weight, vectors):
    rows = tokens.shape[0]
    count = len(weight)

    def kernel(s, o0_ref, o1_ref, x_ref, v_ref, *rest):
        refs, (n1_ref, inv_ref, hb_ref, w_ref, sem) = rest[:count], rest[count:]

        @pl.when(pl.program_id(0) == 0)
        def _():
            weight.load(s[0], refs, w_ref, sem)

        both = jnp.concatenate([o0_ref[...], o1_ref[...]], axis=1)
        branch = dot(both, w_ref[:, :, :D].reshape(D, D), NN) + v_ref[2:3, :]
        normed, inv_std = normalize(x_ref[...].astype(f32) + branch)
        n1_ref[...] = normed
        inv_ref[...] = inv_std
        hb_ref[...] = (normed * v_ref[3:4, :] + v_ref[4:5, :]).astype(bf16)

    return call(
        kernel,
        (rows // TILE,),
        [rows_of(PART), rows_of(PART), rows_of(D), whole((8, D))] + [ANY] * count,
        [rows_of(D), rows_of(1), rows_of(D), HELD],
        [
            pltpu.VMEM((rows, D), f32),
            pltpu.HBM((rows, 1), f32),
            pltpu.VMEM((rows, D), bf16),
            pltpu.VMEM(weight.shape, bf16),
        ],
        [pltpu.SemaphoreType.DMA],
        flops=2 * rows * D * D,
        bytes_accessed=rows * D * 10 + 2 * D * (D + FF),
        name="project",
    )(me, *[in_vmem(half) for half in attended], tokens, vectors, *weight.arrays)


def expand(me, hidden_low, weight, in_bias):
    rows = hidden_low.shape[0]
    tile = 512

    def kernel(s, h_ref, b_ref, w_ref, f_ref, sl_ref):
        low = h_ref[...]
        for j in range(FF // tile):
            lanes = slice(j * tile, (j + 1) * tile)
            w = w_ref[:, :, D + j * tile : D + (j + 1) * tile].reshape(D, tile)
            act, slope = gelu_and_slope(dot(low, w, NN) + b_ref[:, lanes])
            f_ref[:, lanes] = act.astype(bf16)
            sl_ref[:, lanes] = slope.astype(bf16)

    return call(
        kernel,
        (rows // TILE,),
        [rows_of(D), whole((1, FF)), HELD],
        [rows_of(FF), rows_of(FF)],
        [pltpu.VMEM((rows, FF), bf16), pltpu.VMEM((rows, FF), bf16)],
        flops=2 * rows * D * FF,
        bytes_accessed=rows * (D * 2 + FF * 4) + 2 * D * FF,
        name="expand",
    )(me, in_vmem(hidden_low), in_bias, in_vmem(weight))


def feed_out(me, activated, normed_one, cotangent, weight, vectors):
    rows = activated.shape[0]
    count = len(weight)

    def kernel(s, f_ref, n1_ref, g_ref, v_ref, *rest):
        refs = rest[:count]
        y_ref, dr_ref, dz_ref, sums_ref, w_ref, sem = rest[count:]

        @pl.when(pl.program_id(0) == 0)
        def _():
            weight.load(s[0], refs, w_ref, sem)
            sums_ref[...] = jnp.zeros_like(sums_ref)

        branch = dot(f_ref[...], w_ref[...].reshape(FF, D), NN) + v_ref[5:6, :]
        hidden = n1_ref[...] * v_ref[3:4, :] + v_ref[4:5, :]
        normed, inv_std = normalize(hidden + branch)
        y_ref[...] = (normed * v_ref[6:7, :] + v_ref[7:8, :]).astype(bf16)
        grad_y = g_ref[...].astype(f32)
        sums_ref[1:2, :] += jnp.sum(grad_y * normed, axis=0, keepdims=True)
        sums_ref[2:3, :] += jnp.sum(grad_y, axis=0, keepdims=True)
        grad_res = norm_back(grad_y * v_ref[6:7, :], normed, inv_std)
        dr_ref[...] = grad_res
        low = grad_res.astype(bf16)
        dz_ref[...] = low
        sums_ref[0:1, :] += jnp.sum(low.astype(f32), axis=0, keepdims=True)

    return call(
        kernel,
        (rows // TILE,),
        [rows_of(FF), rows_of(D), rows_of(D), whole((8, D))] + [ANY] * count,
        [rows_of(D), rows_of(D), rows_of(D), whole((8, D)), HELD],
        [
            jax.ShapeDtypeStruct((rows, D), bf16),
            pltpu.VMEM((rows, D), f32),
            jax.ShapeDtypeStruct((rows, D), bf16),
            jax.ShapeDtypeStruct((8, D), f32),
            pltpu.VMEM(weight.shape, bf16),
        ],
        [pltpu.SemaphoreType.DMA],
        flops=2 * rows * D * FF,
        bytes_accessed=rows * (D * 14 + FF * 2) + 2 * D * FF,
        name="feed_out",
    )(me, in_vmem(activated), in_vmem(normed_one), cotangent, vectors, *weight.arrays)


def slot(chip, core):
    return jnp.where(core == 0, chip, (chip & 1) * 2 + (chip >> 1))


def grad_w_out(me, activated, grad_ffn):
    rows = activated.shape[0]
    half = RANKS // 2

    def kernel(s, f_ref, dz_ref, t_ref, m_ref):
        block = dot(f_ref[...], dz_ref[...], TN).astype(bf16)
        low, high = block[:SHARD_FF], block[SHARD_FF:]
        even = (s[0] & 1) == 0
        m_ref[0] = jnp.where(even, low, high)
        t_ref[0] = jnp.where(even, high, low)

    shape = pltpu.HBM((half, SHARD_FF, D), bf16)

    def out(flip):
        return pl.BlockSpec((1, SHARD_FF, D), lambda i, s: (slot(i, (s[0] & 1) ^ flip), 0, 0))

    return call(
        kernel,
        (half,),
        [
            pl.BlockSpec((rows, 2 * SHARD_FF), lambda i, s: (0, (s[0] >> 1) ^ i)),
            whole((rows, D)),
        ],
        [out(1), out(0)],
        [shape, shape],
        flops=2 * rows * D * FF,
        bytes_accessed=rows * (D * 2 + FF * 2) + 2 * D * FF,
        name="grad_w_out",
    )(me, in_vmem(activated), grad_ffn)


def back_out(me, grad_ffn, slope, weight):
    rows = grad_ffn.shape[0]

    def kernel(s, dz_ref, sl_ref, w_ref, du_ref, sums_ref):
        @pl.when(pl.program_id(0) == 0)
        def _():
            sums_ref[...] = jnp.zeros_like(sums_ref)

        dz = dz_ref[...]
        for r in range(RANKS // 2):
            lanes = slice(2 * r * SHARD_FF, 2 * (r + 1) * SHARD_FF)
            w = w_ref[2 * r : 2 * r + 2].reshape(2 * SHARD_FF, D)
            grad = dot(dz, w, NT) * sl_ref[:, lanes].astype(f32)
            low = grad.astype(bf16)
            du_ref[:, lanes] = low
            sums_ref[:, lanes] += jnp.sum(low.astype(f32), axis=0, keepdims=True)

    return call(
        kernel,
        (rows // TILE,),
        [rows_of(D), rows_of(FF), HELD],
        [rows_of(FF), whole((1, FF))],
        [pltpu.VMEM((rows, FF), bf16), jax.ShapeDtypeStruct((1, FF), f32)],
        flops=2 * rows * D * FF,
        bytes_accessed=rows * (D * 2 + FF * 4) + 2 * D * FF,
        name="back_out",
    )(me, grad_ffn, in_vmem(slope), in_vmem(weight))


def back_in(me, grad_pre, grad_res_two, normed_one, inv_one, weight, vectors):
    rows = grad_pre.shape[0]

    def kernel(
        s, du_ref, dr2_ref, n1_ref, inv_ref, v_ref, w_ref, dr1_ref, da_ref, do0_ref, do1_ref, sums_ref
    ):
        @pl.when(pl.program_id(0) == 0)
        def _():
            sums_ref[...] = jnp.zeros_like(sums_ref)

        w_in = w_ref[:, :, D:].reshape(D, FF)
        grad_hidden = dot(du_ref[...], w_in, NT) + dr2_ref[...]
        normed = n1_ref[...]
        sums_ref[1:2, :] += jnp.sum(grad_hidden * normed, axis=0, keepdims=True)
        sums_ref[2:3, :] += jnp.sum(grad_hidden, axis=0, keepdims=True)
        grad_res = norm_back(grad_hidden * v_ref[3:4, :], normed, inv_ref[...])
        dr1_ref[...] = grad_res
        low = grad_res.astype(bf16)
        da_ref[...] = low
        sums_ref[0:1, :] += jnp.sum(low.astype(f32), axis=0, keepdims=True)
        w_proj = w_ref[:, :, :D].reshape(D, D)
        grad_attended = dot(low, w_proj, NT).astype(bf16)
        do0_ref[...] = grad_attended[:, :PART]
        do1_ref[...] = grad_attended[:, PART:]

    return call(
        kernel,
        (rows // TILE,),
        [rows_of(FF), rows_of(D), rows_of(D), rows_of(1), whole((8, D))] + [HELD],
        [rows_of(D), rows_of(D), rows_of(PART), rows_of(PART), whole((8, D))],
        [
            pltpu.HBM((rows, D), f32),
            pltpu.VMEM((rows, D), bf16),
            pltpu.VMEM((rows, PART), bf16),
            pltpu.VMEM((rows, PART), bf16),
            jax.ShapeDtypeStruct((8, D), f32),
        ],
        flops=2 * rows * D * (D + FF),
        bytes_accessed=rows * (D * 16 + FF * 2) + 2 * D * (D + FF),
        name="back_in",
    )(
        me,
        in_vmem(grad_pre),
        in_vmem(grad_res_two),
        in_vmem(normed_one),
        in_hbm(inv_one),
        vectors,
        in_vmem(weight),
    )


def store_by_rank(s, block, t_ref, m_ref, first=0):
    core = s[0] & 1
    lanes = slice(first, first + block.shape[1])
    for k in range(RANKS // 2):
        low = block[2 * k * SHARD : (2 * k + 1) * SHARD]
        high = block[(2 * k + 1) * SHARD : (2 * k + 2) * SHARD]
        away = (s[0] >> 1) ^ k
        m_ref[slot(away, core), :SHARD, lanes] = jnp.where(core == 0, low, high)
        t_ref[slot(away, 1 - core), :SHARD, lanes] = jnp.where(core == 0, high, low)


def grad_w_in(me, hidden_low, grad_pre):
    rows = hidden_low.shape[0]
    half = RANKS // 2

    def kernel(s, h_ref, du_ref, t_ref, m_ref):
        store_by_rank(s, dot(h_ref[...], du_ref[...], TN).astype(bf16), t_ref, m_ref)

    shape = pltpu.HBM((half, SHARD, FF), bf16)
    out = pl.BlockSpec((half, SHARD, D), lambda i, s: (0, 0, i))
    return call(
        kernel,
        (FF // D,),
        [whole((rows, D)), pl.BlockSpec((rows, D), lambda i, s: (0, i))],
        [out, out],
        [shape, shape],
        flops=2 * rows * D * FF,
        bytes_accessed=rows * (D * 4 + FF * 2) + 2 * D * FF,
        name="grad_w_in",
    )(me, in_vmem(hidden_low), in_vmem(grad_pre))


def attention_back(lengths, qkv, weights, grad_attended):
    rows = qkv.shape[0]
    scale = HDIM ** (-0.5)
    width = HEADS * SEQ // 2

    def kernel(s, qkv_ref, p_ref, do_ref, out_ref, sums_ref):
        @pl.when(pl.program_id(0) == 0)
        def _():
            sums_ref[...] = jnp.zeros_like(sums_ref)

        first = head_masks()
        grad_p, grad_s, grad_q, grad_k, grad_v = {}, {}, {}, {}, {}

        def back_weights(unit):
            values = stack_heads(qkv_ref[place(unit, 2)], first)
            grad_p[unit] = dot(do_ref[place(unit)], values, NT)

        def back_values(unit):
            both = dot(p_ref[weight_place(unit)].astype(bf16), do_ref[place(unit)], TN)
            grad_v[unit] = jnp.where(first, both[:SEQ], both[SEQ:]).astype(bf16)

        def back_softmax(unit):
            p = p_ref[weight_place(unit)]
            product = grad_p[unit] * p
            halves = []
            for part in range(2):
                cut = slice(part * SEQ, (part + 1) * SEQ)
                inner = grad_p[unit][:, cut] - lane_sum(product[:, cut])
                halves.append((p[:, cut] * inner).astype(bf16))
            grad_s[unit] = jnp.concatenate(halves, axis=1)

        def back_queries(unit):
            keys = stack_heads(qkv_ref[place(unit, 1)], first)
            grad_q[unit] = (dot(grad_s[unit], keys, NN) * scale).astype(bf16)

        def back_keys(unit):
            both = dot(grad_s[unit], qkv_ref[place(unit)], TN)
            grad_k[unit] = jnp.where(first, both[:SEQ], both[SEQ:]).astype(bf16)

        def store(unit):
            out_ref[place(unit)] = grad_q[unit]
            out_ref[place(unit, 1)] = grad_k[unit]
            out_ref[place(unit, 2)] = grad_v[unit]
            lanes = place(unit)[1]
            sums_ref[0:1, lanes] += jnp.sum(grad_q[unit].astype(f32), axis=0, keepdims=True)
            sums_ref[1:2, lanes] += jnp.sum(grad_v[unit].astype(f32), axis=0, keepdims=True)

        stages = (back_weights, back_values, back_softmax, back_queries, back_keys, store)
        by_stages(UNITS, stages)

    return call(
        kernel,
        (rows // (GROUP * SEQ),),
        [rows_of(3 * PART, GROUP * SEQ), rows_of(width, GROUP * SEQ), rows_of(PART, GROUP * SEQ)],
        [rows_of(3 * PART, GROUP * SEQ), whole((8, PART))],
        [pltpu.VMEM((rows, 3 * PART), bf16), jax.ShapeDtypeStruct((8, PART), f32)],
        flops=7e9,
        bytes_accessed=rows * (PART * 14 + width * 4),
        name="attention_back",
    )(lengths, in_hbm(qkv), in_hbm(weights), in_vmem(grad_attended))


EXTRA = 16
IN_AT = 128


def grad_w_qkv(me, tokens, grad_mixed, sums_qkv, sums_one, sums_two, sums_in):
    rows = tokens.shape[0]
    half = RANKS // 2
    width = 3 * PART

    def kernel(s, x_ref, g_ref, q0_ref, q1_ref, one_ref, two_ref, in_ref, t_ref, m_ref):
        store_by_rank(s, dot(x_ref[...], g_ref[...], TN).astype(bf16), t_ref, m_ref)
        vectors = jnp.concatenate(
            [
                jnp.concatenate([q0_ref[0:2], q1_ref[0:2]], axis=1),
                one_ref[0:3],
                two_ref[0:3],
            ],
            axis=0,
        )
        core = s[0] & 1
        end = IN_AT + SHARD_FF
        rest = jnp.zeros((EXTRA, width - end), bf16)
        for k in range(half):
            blocks = []
            for rank in (2 * k, 2 * k + 1):
                vec = vectors[:, rank * SHARD : (rank + 1) * SHARD]
                vec = jnp.concatenate([vec, jnp.zeros((8, IN_AT - SHARD), f32)], axis=1)
                bias = in_ref[:, rank * SHARD_FF : (rank + 1) * SHARD_FF]
                bias = jnp.concatenate([bias, jnp.zeros((7, SHARD_FF), f32)], axis=0)
                block = jnp.concatenate([vec, bias], axis=1)
                blocks.append(jnp.concatenate([block, jnp.zeros_like(block)], axis=0).astype(bf16))
            away = (s[0] >> 1) ^ k
            for ref, here, block in (
                (m_ref, core, jnp.where(core == 0, blocks[0], blocks[1])),
                (t_ref, 1 - core, jnp.where(core == 0, blocks[1], blocks[0])),
            ):
                ref[slot(away, here), SHARD:, :end] = block
                ref[slot(away, here), SHARD:, end:] = rest

    shape = pltpu.HBM((half, SHARD + EXTRA, width), bf16)
    out = whole((half, SHARD + EXTRA, width))
    return call(
        kernel,
        (1,),
        [
            whole((rows, D)),
            HELD,
            whole((8, PART)),
            whole((8, PART)),
            whole((8, D)),
            whole((8, D)),
            whole((1, FF)),
        ],
        [out, out],
        [shape, shape],
        flops=2 * rows * D * width,
        bytes_accessed=rows * (D * 8) + 2 * D * width,
        name="grad_w_qkv",
    )(me, tokens, in_vmem(grad_mixed), *sums_qkv, sums_one, sums_two, sums_in)


def grad_w_mixed(me, tokens, grad_mixed, attended, grad_branch):
    rows = tokens.shape[0]
    half = RANKS // 2
    width = 3 * PART

    def kernel(s, x_ref, g_ref, o0_ref, o1_ref, da_ref, t_ref, m_ref):
        store_by_rank(s, dot(x_ref[...], g_ref[...], TN).astype(bf16), t_ref, m_ref)
        both = jnp.concatenate([o0_ref[...], o1_ref[...]], axis=1)
        proj = dot(both, da_ref[...], TN).astype(bf16)
        store_by_rank(s, proj, t_ref, m_ref, width)

    shape = pltpu.HBM((half, SHARD, width + D), bf16)
    out = whole((half, SHARD, width + D))
    return call(
        kernel,
        (1,),
        [
            whole((rows, D)),
            HELD,
            HELD,
            HELD,
            HELD,
        ],
        [out, out],
        [shape, shape],
        flops=2 * rows * D * (width + D),
        bytes_accessed=rows * (D * 12) + 2 * D * (width + D),
        name="grad_w_mixed",
    )(
        me,
        tokens,
        in_vmem(grad_mixed),
        *[in_vmem(half) for half in attended],
        in_vmem(grad_branch),
    )


def back_qkv(me, grad_mixed, grad_res_one, weight, before=None):
    rows = grad_res_one.shape[0]
    steps = rows // TILE // 2
    width = 3 * PART

    def compute(g0_ref, g1_ref, dr_ref, w_ref, out_ref):
        both = jnp.concatenate([g0_ref[...], g1_ref[...]], axis=1)
        w = w_ref[...].reshape(D, 2 * width)
        out_ref[...] = (dot(both, w, NT) + dr_ref[...]).astype(bf16)

    def kernel_one(s, g0_ref, g1_ref, dr_ref, *rest):
        refs, (out_ref, w_ref, sem) = rest[: len(weight)], rest[len(weight) :]

        @pl.when(pl.program_id(0) == 0)
        def _():
            weight.load(s[0], refs, w_ref, sem)

        compute(g0_ref, g1_ref, dr_ref, w_ref, out_ref)

    def kernel_two(s, g0_ref, g1_ref, dr_ref, w_ref, before_ref, out_ref):
        compute(g0_ref, g1_ref, dr_ref, w_ref, out_ref)

    def at(width):
        return rows_of(width, TILE, steps if before is not None else 0)

    operands = (me, *[in_vmem(half) for half in grad_mixed], in_hbm(grad_res_one))
    blocks = [at(width), at(width), at(D)]
    out = pltpu.HBM((rows, D), bf16)
    cost = dict(flops=rows * D * 3 * D, bytes_accessed=rows * D * 6 + 2 * D * 3 * D, name="back_qkv")
    if before is None:
        return call(
            kernel_one,
            (steps,),
            blocks + [ANY] * len(weight),
            [at(D), HELD],
            [out, pltpu.VMEM(weight.shape, bf16)],
            [pltpu.SemaphoreType.DMA],
            **cost,
        )(*operands, *weight.arrays)
    return call(
        kernel_two, (steps,), blocks + [HELD, ANY], at(D), out, aliases={5: 0}, **cost
    )(*operands, in_vmem(weight), in_hbm(before))


def adamw_math(moment, square, gradient):
    first_fix = 1.0 - beta_one**STEP
    second_fix = 1.0 - beta_two**STEP
    moment = beta_one * moment + (1.0 - beta_one) * gradient
    square = beta_two * square + (1.0 - beta_two) * gradient * gradient
    update = moment / first_fix / (jnp.sqrt(square / second_fix) + adam_epsilon)
    return (update, moment, square)


def adamw(moment, square, gradient):
    gradient = gradient.astype(f32)
    return (gradient,) + adamw_math(moment, square, gradient)


def flip(bit):
    return [(i, i ^ bit) for i in range(RANKS)]


def swap(value, bit):
    return lax.ppermute(value, "fsdp", flip(bit))


def after(value, *others):
    return lax.optimization_barrier((value,) + others)[0]


def split_swap(value, even_bit, odd_bit):
    return lax.ppermute(
        value, "fsdp", [(i, i ^ (odd_bit if i & 1 else even_bit)) for i in range(RANKS)]
    )


class Gather:
    def __init__(self, shard):
        self.shard = shard

    def start(self, *others):
        if others:
            self.shard = after(self.shard, *others)
        self.one = split_swap(self.shard, 2, 4)
        self.two = split_swap(self.shard, 4, 2)

    def forward(self, *others):
        self.one, self.two = lax.optimization_barrier((self.one, self.two) + others)[:2]
        self.far = split_swap(self.one, 4, 2)
        self.other = [swap(piece, 1) for piece in (self.shard, self.one, self.two)]

    def finish(self, *others):
        self.far = after(self.far, *others)
        self.other.append(swap(self.far, 1))
        return Weight([self.shard, self.one, self.two, self.far] + self.other)


def low_sum(*values):
    total = values[0].astype(f32)
    for value in values[1:]:
        total = total + value.astype(f32)
    return total.astype(bf16)


class Scatter:
    def __init__(self, parts):
        self.theirs, self.mine = parts
        self.got = swap(self.theirs, 1)

    def one(self, *others):
        self.got = after(self.got, *others)
        send = low_sum(self.mine[1::2], self.got[1::2])
        self.near_got = split_swap(send, 2, 4)
        return (send,)

    def two(self, *others):
        self.near_got = after(self.near_got, *others)
        send = low_sum(self.mine[2], self.got[2], self.near_got[1])
        self.last = split_swap(send, 4, 2)
        return (send,)

    def three(self, *others):
        last = after(self.last, *others)
        self.owned = low_sum(self.mine[0], self.got[0], self.near_got[0], last)
        return (self.owned,)

    def line(self):
        self.near = lax.ppermute(self.owned, "rep", [(0, 1), (3, 2)])

    def four(self, *others):
        self.near = low_sum(self.owned, after(self.near, *others))
        self.across = lax.ppermute(self.near, "rep", [(1, 2), (2, 1)])
        return (self.near,)

    def five(self, *others):
        self.total = low_sum(self.near, after(self.across, *others))
        self.back = lax.ppermute(self.total, "rep", [(1, 0), (2, 3)])
        return (self.total,)

    def result(self, rep_index):
        inner = (rep_index == 1) | (rep_index == 2)
        return jnp.where(inner, self.total, self.back)


def by_rank(pairs, position):
    stacked = jnp.stack(pairs)
    stacked = jnp.where((position & 2) == 0, stacked, stacked[jnp.array([1, 0, 3, 2])])
    stacked = jnp.where((position & 4) == 0, stacked, stacked[jnp.array([2, 3, 0, 1])])
    return stacked.reshape(RANKS, -1)


def by_head_half(value, half):
    return [value[:, k * D + half * PART : k * D + (half + 1) * PART] for k in range(3)]


def local(
    fsdp,
    rep,
    tokens,
    cotangent,
    lengths,
    w_attn,
    w_in,
    w_out,
    b_in,
    vecs,
    m_attn,
    m_in,
    m_out,
    m_bin,
    m_vecs,
    v_attn,
    v_in,
    v_out,
    v_bin,
    v_vecs,
):
    direct = fsdp == RANKS and rep == 4
    position = lax.axis_index("fsdp")
    rep_index = lax.axis_index("rep")
    part = D // fsdp
    heads_a = [jnp.concatenate(by_head_half(w_attn, h), axis=1) for h in range(2)]
    low_a = jnp.concatenate(heads_a, axis=1).astype(bf16)
    if direct:
        me = position.reshape(1)
        a = Gather(low_a)
        a.start()
        wait = lambda value: after(value, low_a)
    else:
        me = jnp.zeros((1,), jnp.int32)
        wait = lambda value: value
    low_b = jnp.concatenate([wait(w_attn)[:, 3 * D :], w_in], axis=1).astype(bf16)
    low_c = wait(w_out).astype(bf16)
    small = jnp.concatenate([wait(vecs).reshape(1, -1), b_in.reshape(1, -1)], axis=1).astype(bf16)
    if direct:
        b = Gather(low_b)
        c = Gather(low_c)
        got = swap(small, 1)
        first = (position & 1) == 0
        pair = jnp.concatenate([jnp.where(first, small, got), jnp.where(first, got, small)])
        pairs = [pair] + [swap(pair, bit) for bit in (2, 4, 6)]
        a.forward(*pairs)
        b.start(a.one, a.two, *pairs)
        small_all = by_rank(pairs, position)
        weight_a = a.finish()
    else:

        def gather(low):
            full = lax.all_gather(low, "fsdp", axis=0, tiled=True)
            return Weight([full.reshape(RANKS, -1, full.shape[1])])

        weight_a, weight_b, weight_c = gather(low_a), gather(low_b), gather(low_c)
        small_all = lax.all_gather(small, "fsdp", axis=0, tiled=True)

    def ordered(value, *others):
        return after(value, *others) if direct else value

    small_all = small_all.astype(f32)
    vectors = small_all[:, : 8 * part].reshape(fsdp, 8, part).transpose(1, 0, 2).reshape(8, D)
    in_bias = small_all[:, 8 * part :].reshape(1, FF)
    bias = jnp.stack([vectors[0], jnp.zeros((D,), f32), vectors[1]]).reshape(3, 2, PART)
    bias = bias.transpose(1, 0, 2).reshape(1, 6 * PART)

    qkv = project_qkv(me, tokens, weight_a, bias)
    attended, weights = [None, None], [None, None]
    first, second = qkv
    if direct:
        b.forward(*qkv)
        first = after(first, b.one, b.two)
    attended[0], weights[0] = attention(lengths, first)
    if direct:
        c.start(attended[0], *b.other)
        second = after(second, attended[0], *b.other)
        weight_b = b.finish(attended[0])
    attended[1], weights[1] = attention(lengths, second)
    normed_one, inv_one, hidden_low, held_b = project(me, attended, tokens, weight_b, vectors)
    inner = hidden_low
    if direct:
        c.forward(hidden_low)
        inner = after(hidden_low, c.one, c.two)
    activated, slope = expand(me, inner, held_b, in_bias)
    if direct:
        weight_c = c.finish(activated)
    output, grad_res_two, grad_ffn, sums_two, held_c = feed_out(
        me, activated, normed_one, cotangent, weight_c, vectors
    )

    parts_out = grad_w_out(me, activated, grad_ffn)
    grad_pre, sums_in = back_out(me, ordered(grad_ffn, *parts_out), slope, held_c)
    sent = ()
    if direct:
        r_out = Scatter(parts_out)
        sent = r_out.one(grad_pre)
    parts_in = grad_w_in(me, hidden_low, ordered(grad_pre, *sent))
    grad_res_one, grad_branch, *grad_attended, sums_one = back_in(
        me, ordered(grad_pre, *parts_in), grad_res_two, normed_one, inv_one, held_b, vectors
    )
    sent = ()
    if direct:
        r_in = Scatter(parts_in)
        sent = r_out.two(grad_branch) + r_in.one(grad_branch)
    mixed0, sums_q0 = attention_back(
        lengths, qkv[0], weights[0], ordered(grad_attended[0], *sent)
    )
    parts_mix = grad_w_mixed(me, tokens, mixed0, attended, grad_branch)
    sent = parts_mix
    if direct:
        r_mix = Scatter(parts_mix)
        sent = r_out.three(*parts_mix)
        r_out.line()
        sent = r_in.two(*sent)
    mixed1, sums_q1 = attention_back(
        lengths, qkv[1], weights[1], ordered(grad_attended[1], *sent)
    )
    parts_qkv = grad_w_qkv(me, tokens, mixed1, (sums_q0, sums_q1), sums_one, sums_two, sums_in)
    sent = ()
    if direct:
        r_qkv = Scatter(parts_qkv)
        sent = r_in.three(*parts_qkv)
        r_in.line()
        sent = r_mix.one(*sent)
        sent = r_qkv.one(*sent)
        sent = r_out.four(*sent)
    half_tokens, held_a = back_qkv(
        me, (mixed0, ordered(mixed1, *sent, *parts_qkv)), grad_res_one, weight_a
    )
    sent = ()
    if direct:
        sent = r_mix.two(half_tokens)
        sent = r_qkv.two(*sent)
        sent = r_in.four(*sent)
    grad_tokens = back_qkv(
        me, (mixed0, ordered(mixed1, *sent)), grad_res_one, held_a, half_tokens
    )
    if direct:
        sent = r_qkv.three(grad_tokens)
        r_qkv.line()
        sent = r_mix.three(*sent)
        r_mix.line()
        sent = r_out.five(*sent)
        sent = r_in.five(*sent)
        sent = r_qkv.four(*sent)
        sent = r_mix.four(*sent)
        sent = r_qkv.five(*sent)
        sent = r_mix.five(*sent)
        sum_qkv = r_qkv.result(rep_index)
        sum_out, sum_in, sum_mix = [r.result(rep_index) for r in (r_out, r_in, r_mix)]
        sum_vecs = sum_qkv[SHARD : SHARD + 8, :part]
        sum_bin = sum_qkv[SHARD, IN_AT : IN_AT + FF // fsdp]
        sum_qkv = sum_qkv[:SHARD]
    else:

        def reduce(theirs, mine):
            full = jnp.stack([mine, theirs[jnp.array([0, 2, 1, 3])]], axis=1)
            full = full.reshape(-1, full.shape[-1])
            owned = lax.psum_scatter(full, "fsdp", scatter_dimension=0, tiled=True)
            return lax.psum(owned, "rep")

        sum_out, sum_in, sum_mix = [reduce(*parts) for parts in (parts_out, parts_in, parts_mix)]
        sum_qkv = reduce(*[parts[:, :SHARD] for parts in parts_qkv])
        theirs, mine = [parts[:, SHARD:] for parts in parts_qkv]
        extra = jnp.stack([mine, theirs[jnp.array([0, 2, 1, 3])]], axis=1)
        extra = extra.reshape(RANKS, EXTRA, 3 * PART).astype(f32)
        extra = lax.psum(extra[:, :8], ("fsdp", "rep"))
        all_vecs = extra[:, :, :SHARD].transpose(1, 0, 2).reshape(8, D)
        all_bin = extra[:, 0, IN_AT : IN_AT + SHARD_FF].reshape(FF)
        sum_vecs = lax.dynamic_slice(all_vecs, (0, position * part), (8, part))
        sum_bin = lax.dynamic_slice(all_bin, (position * (FF // fsdp),), (FF // fsdp,))

    grad_out, step_out, mom_out, sq_out = adamw(m_out, v_out, sum_out)
    grad_in, step_in, mom_in, sq_in = adamw(m_in, v_in, sum_in)
    columns = []
    for k in range(3):
        columns += [sum_mix[:, k * PART : (k + 1) * PART].astype(f32), sum_qkv[:, k * PART : (k + 1) * PART].astype(f32)]
    sum_attn = jnp.concatenate(columns + [sum_mix[:, 3 * PART :].astype(f32)], axis=1)
    grad_attn, step_attn, mom_attn, sq_attn = adamw(m_attn, v_attn, sum_attn)
    grad_bin, step_bin, mom_bin, sq_bin = adamw(m_bin, v_bin, sum_bin)
    grad_vecs, step_vecs, mom_vecs, sq_vecs = adamw(m_vecs, v_vecs, sum_vecs)
    return (
        output,
        grad_tokens,
        grad_attn,
        grad_in,
        grad_out,
        grad_bin,
        grad_vecs,
        step_attn,
        step_in,
        step_out,
        step_bin,
        step_vecs,
        mom_attn,
        mom_in,
        mom_out,
        mom_bin,
        mom_vecs,
        sq_attn,
        sq_in,
        sq_out,
        sq_bin,
        sq_vecs,
    )


def solution(mesh):
    rows, row, col = P(("rep", "fsdp"), None), P("fsdp", None), P(None, "fsdp")
    flat = P("fsdp")
    state = (row, row, row, flat, col)
    return jax.shard_map(
        functools.partial(local, mesh.shape["fsdp"], mesh.shape["rep"]),
        mesh=mesh,
        in_specs=(rows, rows, P(("rep", "fsdp"))) + state * 3,
        out_specs=(rows, rows) + state * 4,
        check_vma=False,
    )
```

```python
import functools

import jax
import jax.numpy as jnp
from jax import lax
from jax.experimental import pallas as pl
from jax.experimental.pallas import tpu as pltpu
from jax.sharding import PartitionSpec as P

D = 768
HEADS = 12
HDIM = 64
PART = D // 2
FF = 3072
SEQ = 128
STEP = 5

RANKS = 8
SHARD = D // RANKS
SHARD_FF = FF // RANKS

beta_one = 0.9
beta_two = 0.999
adam_epsilon = 1e-06
norm_epsilon = 1e-05
masked_score = -1000000000.0

bf16 = jnp.bfloat16
f32 = jnp.float32
NN = (((1,), (0,)), ((), ()))
NT = (((1,), (1,)), ((), ()))
TN = (((0,), (0,)), ((), ()))
VMEM_BYTES = 17 * 1024 * 1024
TILE = 256
LIGHT = 1000


def dot(left, right, dims):
    return lax.dot_general(left, right, dims, preferred_element_type=f32)


def call(kernel, grid, in_specs, out_specs, out_shape, scratch=(), flops=0, bytes_accessed=0, name=None, aliases=None):
    return pl.pallas_call(
        kernel,
        grid_spec=pltpu.PrefetchScalarGridSpec(
            num_scalar_prefetch=1,
            grid=grid,
            in_specs=in_specs,
            out_specs=out_specs,
            scratch_shapes=list(scratch),
        ),
        out_shape=out_shape,
        input_output_aliases=aliases or {},
        compiler_params=pltpu.CompilerParams(
            vmem_limit_bytes=VMEM_BYTES, dimension_semantics=("arbitrary",) * len(grid)
        ),
        cost_estimate=pl.CostEstimate(
            flops=int(flops) // LIGHT, bytes_accessed=int(bytes_accessed) // LIGHT, transcendentals=0
        ),
        name=name,
    )


def rows_of(width, tile=TILE, first=0):
    return pl.BlockSpec((tile, width), lambda i, s: (i + first, 0))


def whole(shape):
    return pl.BlockSpec(shape, lambda i, s: (0,) * len(shape))


ANY = pl.BlockSpec(memory_space=pl.ANY)
HELD = pl.BlockSpec(memory_space=pltpu.VMEM)


def in_vmem(array):
    return pltpu.with_memory_space_constraint(array, pltpu.VMEM)


def in_hbm(array):
    return pltpu.with_memory_space_constraint(array, pltpu.HBM)


class Weight:
    def __init__(self, arrays):
        self.arrays = [in_hbm(array) for array in arrays]
        self.shape = (RANKS,) + self.arrays[0].shape[-2:]

    def __len__(self):
        return len(self.arrays)

    def load(self, me, refs, held, sem):
        if len(refs) == 1:
            copies = [pltpu.make_async_copy(refs[0], held, sem)]
        else:
            copies = []
            for number, ref in enumerate(refs):
                owner = me if number < 4 else me ^ 1
                first = jnp.where((owner & 1) == 0, 2, 4)
                rank = owner ^ (0, first, 6 - first, 6)[number % 4]
                copies.append(pltpu.make_async_copy(ref, held.at[rank], sem))
        for copy in copies:
            copy.start()
        for copy in copies:
            copy.wait()


def lane_sum(value):
    return jnp.sum(value, axis=-1, keepdims=True)


def normalize(residual):
    centre = residual - lane_sum(residual) * (1.0 / D)
    variance = lane_sum(centre * centre) * (1.0 / D)
    inv_std = lax.rsqrt(variance + norm_epsilon)
    return (centre * inv_std, inv_std)


def norm_back(grad_normed, normed, inv_std):
    first_mean = lane_sum(grad_normed) * (1.0 / D)
    second_mean = lane_sum(grad_normed * normed) * (1.0 / D)
    return inv_std * (grad_normed - first_mean - normed * second_mean)


def gelu_and_slope(pre_act):
    cumulative = 0.5 * (1.0 + lax.erf(pre_act * 0.7071067811865476))
    density = jnp.exp(-0.5 * pre_act * pre_act) * 0.3989422804014327
    return (pre_act * cumulative, cumulative + pre_act * density)


def project_qkv(me, tokens, weight, bias):
    rows = tokens.shape[0]
    count = len(weight)
    width = 3 * PART

    def kernel(s, x_ref, b_ref, *rest):
        refs, (out0_ref, out1_ref, w_ref, sem) = rest[:count], rest[count:]

        @pl.when(pl.program_id(0) == 0)
        def _():
            weight.load(s[0], refs, w_ref, sem)

        rounded = (dot(x_ref[...], w_ref[...].reshape(D, 2 * width), NN) + b_ref[...]).astype(bf16)
        for h, out_ref in enumerate((out0_ref, out1_ref)):
            lead = h * width
            out_ref[:, :PART] = rounded[:, lead : lead + PART] * HDIM ** (-0.5)
            out_ref[:, PART:] = rounded[:, lead + PART : lead + width]

    return call(
        kernel,
        (rows // TILE,),
        [rows_of(D), whole((1, 2 * width))] + [ANY] * count,
        [rows_of(width), rows_of(width)],
        [
            pltpu.HBM((rows, width), bf16),
            pltpu.HBM((rows, width), bf16),
        ],
        [pltpu.VMEM(weight.shape, bf16), pltpu.SemaphoreType.DMA],
        flops=2 * rows * D * width * 2,
        bytes_accessed=2 * (rows * D * 4 + 3 * D * D),
        name="qkv",
    )(me, tokens, bias, *weight.arrays)


def head_masks():
    lane = lax.broadcasted_iota(jnp.int32, (SEQ, 2 * HDIM), 1)
    return lane < HDIM


def stack_heads(value, first):
    zero = jnp.zeros_like(value)
    return jnp.concatenate([jnp.where(first, value, zero), jnp.where(first, zero, value)], axis=0)


GROUP = 4


def by_stages(units, stages):
    for stage in stages:
        for unit in units:
            stage(unit)


def staggered(units, stages):
    for start in range(len(units) + len(stages) - 1):
        for number in reversed(range(len(stages))):
            if 0 <= start - number < len(units):
                stages[number](units[start - number])


def place(unit, part=0):
    lead = part * PART + unit[1] * 2 * HDIM
    return slice(unit[0] * SEQ, (unit[0] + 1) * SEQ), slice(lead, lead + 2 * HDIM)


def weight_place(unit):
    return slice(unit[0] * SEQ, (unit[0] + 1) * SEQ), slice(unit[1] * 2 * SEQ, (unit[1] + 1) * 2 * SEQ)


UNITS = [(pair, heads) for pair in range(GROUP) for heads in range(PART // (2 * HDIM))]


def attention(lengths, qkv):
    rows = qkv.shape[0]

    def kernel(s, qkv_ref, out_ref, p_ref):
        first = head_masks()
        key = lax.broadcasted_iota(jnp.int32, (SEQ, SEQ), 1)
        valid = [key < s[pl.program_id(0) * GROUP + pair] for pair in range(GROUP)]
        scores, low = {}, {}

        def score(unit):
            keys = stack_heads(qkv_ref[place(unit, 1)], first)
            scores[unit] = dot(qkv_ref[place(unit)], keys, NT)

        def soften(unit):
            halves = []
            for part in range(2):
                one = scores[unit][:, part * SEQ : (part + 1) * SEQ]
                one = jnp.where(valid[unit[0]], one, masked_score)
                raised = jnp.exp(one - jnp.max(one, axis=-1, keepdims=True))
                halves.append(raised * (1.0 / lane_sum(raised)))
            weights = jnp.concatenate(halves, axis=1)
            p_ref[weight_place(unit)] = weights
            low[unit] = weights.astype(bf16)

        def attend(unit):
            values = stack_heads(qkv_ref[place(unit, 2)], first)
            out_ref[place(unit)] = dot(low[unit], values, NN).astype(bf16)

        staggered(UNITS, (score, soften, attend))

    width = HEADS * SEQ // 2
    return call(
        kernel,
        (rows // (GROUP * SEQ),),
        [rows_of(3 * PART, GROUP * SEQ)],
        [rows_of(PART, GROUP * SEQ), rows_of(width, GROUP * SEQ)],
        [pltpu.VMEM((rows, PART), bf16), pltpu.HBM((rows, width), f32)],
        flops=4e9,
        bytes_accessed=rows * (PART * 8 + width * 4),
        name="attention",
    )(lengths, in_hbm(qkv))


def project(me, attended, tokens, weight, vectors):
    rows = tokens.shape[0]
    count = len(weight)

    def kernel(s, o0_ref, o1_ref, x_ref, v_ref, *rest):
        refs, (n1_ref, inv_ref, hb_ref, w_ref, sem) = rest[:count], rest[count:]

        @pl.when(pl.program_id(0) == 0)
        def _():
            weight.load(s[0], refs, w_ref, sem)

        both = jnp.concatenate([o0_ref[...], o1_ref[...]], axis=1)
        branch = dot(both, w_ref[:, :, :D].reshape(D, D), NN) + v_ref[2:3, :]
        normed, inv_std = normalize(x_ref[...].astype(f32) + branch)
        n1_ref[...] = normed
        inv_ref[...] = inv_std
        hb_ref[...] = (normed * v_ref[3:4, :] + v_ref[4:5, :]).astype(bf16)

    return call(
        kernel,
        (rows // TILE,),
        [rows_of(PART), rows_of(PART), rows_of(D), whole((8, D))] + [ANY] * count,
        [rows_of(D), rows_of(1), rows_of(D), HELD],
        [
            pltpu.VMEM((rows, D), f32),
            pltpu.HBM((rows, 1), f32),
            pltpu.VMEM((rows, D), bf16),
            pltpu.VMEM(weight.shape, bf16),
        ],
        [pltpu.SemaphoreType.DMA],
        flops=2 * rows * D * D,
        bytes_accessed=rows * D * 10 + 2 * D * (D + FF),
        name="project",
    )(me, *[in_vmem(half) for half in attended], tokens, vectors, *weight.arrays)


def expand(me, hidden_low, weight, in_bias):
    rows = hidden_low.shape[0]
    tile = 512

    def kernel(s, h_ref, b_ref, w_ref, f_ref, sl_ref):
        low = h_ref[...]
        for j in range(FF // tile):
            lanes = slice(j * tile, (j + 1) * tile)
            w = w_ref[:, :, D + j * tile : D + (j + 1) * tile].reshape(D, tile)
            act, slope = gelu_and_slope(dot(low, w, NN) + b_ref[:, lanes])
            f_ref[:, lanes] = act.astype(bf16)
            sl_ref[:, lanes] = slope.astype(bf16)

    return call(
        kernel,
        (rows // TILE,),
        [rows_of(D), whole((1, FF)), HELD],
        [rows_of(FF), rows_of(FF)],
        [pltpu.VMEM((rows, FF), bf16), pltpu.VMEM((rows, FF), bf16)],
        flops=2 * rows * D * FF,
        bytes_accessed=rows * (D * 2 + FF * 4) + 2 * D * FF,
        name="expand",
    )(me, in_vmem(hidden_low), in_bias, in_vmem(weight))


def feed_out(me, activated, normed_one, cotangent, weight, vectors):
    rows = activated.shape[0]
    count = len(weight)

    def kernel(s, f_ref, n1_ref, g_ref, v_ref, *rest):
        refs = rest[:count]
        y_ref, dr_ref, dz_ref, sums_ref, w_ref, sem = rest[count:]

        @pl.when(pl.program_id(0) == 0)
        def _():
            weight.load(s[0], refs, w_ref, sem)
            sums_ref[...] = jnp.zeros_like(sums_ref)

        branch = dot(f_ref[...], w_ref[...].reshape(FF, D), NN) + v_ref[5:6, :]
        hidden = n1_ref[...] * v_ref[3:4, :] + v_ref[4:5, :]
        normed, inv_std = normalize(hidden + branch)
        y_ref[...] = (normed * v_ref[6:7, :] + v_ref[7:8, :]).astype(bf16)
        grad_y = g_ref[...].astype(f32)
        sums_ref[1:2, :] += jnp.sum(grad_y * normed, axis=0, keepdims=True)
        sums_ref[2:3, :] += jnp.sum(grad_y, axis=0, keepdims=True)
        grad_res = norm_back(grad_y * v_ref[6:7, :], normed, inv_std)
        dr_ref[...] = grad_res
        low = grad_res.astype(bf16)
        dz_ref[...] = low
        sums_ref[0:1, :] += jnp.sum(low.astype(f32), axis=0, keepdims=True)

    return call(
        kernel,
        (rows // TILE,),
        [rows_of(FF), rows_of(D), rows_of(D), whole((8, D))] + [ANY] * count,
        [rows_of(D), rows_of(D), rows_of(D), whole((8, D)), HELD],
        [
            jax.ShapeDtypeStruct((rows, D), bf16),
            pltpu.VMEM((rows, D), f32),
            pltpu.VMEM((rows, D), bf16),
            jax.ShapeDtypeStruct((8, D), f32),
            pltpu.VMEM(weight.shape, bf16),
        ],
        [pltpu.SemaphoreType.DMA],
        flops=2 * rows * D * FF,
        bytes_accessed=rows * (D * 14 + FF * 2) + 2 * D * FF,
        name="feed_out",
    )(me, in_vmem(activated), in_vmem(normed_one), cotangent, vectors, *weight.arrays)


def slot(chip, core):
    return jnp.where(core == 0, chip, (chip & 1) * 2 + (chip >> 1))


def grad_w_out(me, activated, grad_ffn):
    rows = activated.shape[0]
    half = RANKS // 2

    def kernel(s, f_ref, dz_ref, t_ref, m_ref):
        block = dot(f_ref[...], dz_ref[...], TN).astype(bf16)
        low, high = block[:SHARD_FF], block[SHARD_FF:]
        even = (s[0] & 1) == 0
        m_ref[0] = jnp.where(even, low, high)
        t_ref[0] = jnp.where(even, high, low)

    shape = pltpu.HBM((half, SHARD_FF, D), bf16)

    def out(flip):
        return pl.BlockSpec((1, SHARD_FF, D), lambda i, s: (slot(i, (s[0] & 1) ^ flip), 0, 0))

    return call(
        kernel,
        (half,),
        [
            pl.BlockSpec((rows, 2 * SHARD_FF), lambda i, s: (0, (s[0] >> 1) ^ i)),
            HELD,
        ],
        [out(1), out(0)],
        [shape, shape],
        flops=2 * rows * D * FF,
        bytes_accessed=rows * (D * 2 + FF * 2) + 2 * D * FF,
        name="grad_w_out",
    )(me, in_vmem(activated), in_vmem(grad_ffn))


def back_out(me, grad_ffn, slope, weight):
    rows = grad_ffn.shape[0]

    def kernel(s, dz_ref, sl_ref, w_ref, du_ref, sums_ref):
        dz = dz_ref[...]
        for r in range(RANKS // 2):
            lanes = slice(2 * r * SHARD_FF, 2 * (r + 1) * SHARD_FF)
            w = w_ref[2 * r : 2 * r + 2].reshape(2 * SHARD_FF, D)
            grad = dot(dz, w, NT) * sl_ref[:, lanes].astype(f32)
            low = grad.astype(bf16)
            du_ref[:, lanes] = low
            sums_ref[:, lanes] = jnp.sum(low.astype(f32), axis=0, keepdims=True)

    return call(
        kernel,
        (1,),
        [HELD, HELD, HELD],
        [HELD, whole((1, FF))],
        [pltpu.VMEM((rows, FF), bf16), jax.ShapeDtypeStruct((1, FF), f32)],
        flops=2 * rows * D * FF,
        bytes_accessed=rows * (D * 2 + FF * 4) + 2 * D * FF,
        name="back_out",
    )(me, in_vmem(grad_ffn), in_vmem(slope), in_vmem(weight))


def back_in(me, grad_pre, grad_res_two, normed_one, inv_one, weight, vectors):
    rows = grad_pre.shape[0]

    def kernel(
        s, du_ref, dr2_ref, n1_ref, inv_ref, v_ref, w_ref, dr1_ref, da_ref, do0_ref, do1_ref, sums_ref
    ):
        @pl.when(pl.program_id(0) == 0)
        def _():
            sums_ref[...] = jnp.zeros_like(sums_ref)

        w_in = w_ref[:, :, D:].reshape(D, FF)
        grad_hidden = dot(du_ref[...], w_in, NT) + dr2_ref[...]
        normed = n1_ref[...]
        sums_ref[1:2, :] += jnp.sum(grad_hidden * normed, axis=0, keepdims=True)
        sums_ref[2:3, :] += jnp.sum(grad_hidden, axis=0, keepdims=True)
        grad_res = norm_back(grad_hidden * v_ref[3:4, :], normed, inv_ref[...])
        dr1_ref[...] = grad_res
        low = grad_res.astype(bf16)
        da_ref[...] = low
        sums_ref[0:1, :] += jnp.sum(low.astype(f32), axis=0, keepdims=True)
        w_proj = w_ref[:, :, :D].reshape(D, D)
        grad_attended = dot(low, w_proj, NT).astype(bf16)
        do0_ref[...] = grad_attended[:, :PART]
        do1_ref[...] = grad_attended[:, PART:]

    return call(
        kernel,
        (rows // TILE,),
        [rows_of(FF), rows_of(D), rows_of(D), rows_of(1), whole((8, D))] + [HELD],
        [rows_of(D), rows_of(D), rows_of(PART), rows_of(PART), whole((8, D))],
        [
            pltpu.HBM((rows, D), f32),
            pltpu.VMEM((rows, D), bf16),
            pltpu.VMEM((rows, PART), bf16),
            pltpu.VMEM((rows, PART), bf16),
            jax.ShapeDtypeStruct((8, D), f32),
        ],
        flops=2 * rows * D * (D + FF),
        bytes_accessed=rows * (D * 16 + FF * 2) + 2 * D * (D + FF),
        name="back_in",
    )(
        me,
        in_vmem(grad_pre),
        in_vmem(grad_res_two),
        in_vmem(normed_one),
        in_hbm(inv_one),
        vectors,
        in_vmem(weight),
    )


def store_by_rank(s, block, t_ref, m_ref, first=0):
    core = s[0] & 1
    lanes = slice(first, first + block.shape[1])
    for k in range(RANKS // 2):
        low = block[2 * k * SHARD : (2 * k + 1) * SHARD]
        high = block[(2 * k + 1) * SHARD : (2 * k + 2) * SHARD]
        away = (s[0] >> 1) ^ k
        m_ref[slot(away, core), :SHARD, lanes] = jnp.where(core == 0, low, high)
        t_ref[slot(away, 1 - core), :SHARD, lanes] = jnp.where(core == 0, high, low)


def grad_w_in(me, hidden_low, grad_pre):
    rows = hidden_low.shape[0]
    half = RANKS // 2

    def kernel(s, h_ref, du_ref, t_ref, m_ref):
        lanes = pl.ds(pl.multiple_of(pl.program_id(0) * D, D), D)
        store_by_rank(s, dot(h_ref[...], du_ref[:, lanes], TN).astype(bf16), t_ref, m_ref)

    shape = pltpu.HBM((half, SHARD, FF), bf16)
    out = pl.BlockSpec((half, SHARD, D), lambda i, s: (0, 0, i))
    return call(
        kernel,
        (FF // D,),
        [HELD, HELD],
        [out, out],
        [shape, shape],
        flops=2 * rows * D * FF,
        bytes_accessed=rows * (D * 4 + FF * 2) + 2 * D * FF,
        name="grad_w_in",
    )(me, in_vmem(hidden_low), in_vmem(grad_pre))


def attention_back(lengths, qkv, weights, grad_attended):
    rows = qkv.shape[0]
    scale = HDIM ** (-0.5)
    width = HEADS * SEQ // 2

    def kernel(s, qkv_ref, p_ref, do_ref, out_ref, sums_ref):
        @pl.when(pl.program_id(0) == 0)
        def _():
            sums_ref[...] = jnp.zeros_like(sums_ref)

        first = head_masks()
        grad_p, grad_s, grad_q, grad_k, grad_v = {}, {}, {}, {}, {}

        def back_weights(unit):
            values = stack_heads(qkv_ref[place(unit, 2)], first)
            grad_p[unit] = dot(do_ref[place(unit)], values, NT)

        def back_values(unit):
            both = dot(p_ref[weight_place(unit)].astype(bf16), do_ref[place(unit)], TN)
            grad_v[unit] = jnp.where(first, both[:SEQ], both[SEQ:]).astype(bf16)

        def back_softmax(unit):
            p = p_ref[weight_place(unit)]
            product = grad_p[unit] * p
            halves = []
            for part in range(2):
                cut = slice(part * SEQ, (part + 1) * SEQ)
                inner = grad_p[unit][:, cut] - lane_sum(product[:, cut])
                halves.append((p[:, cut] * inner).astype(bf16))
            grad_s[unit] = jnp.concatenate(halves, axis=1)

        def back_queries(unit):
            keys = stack_heads(qkv_ref[place(unit, 1)], first)
            grad_q[unit] = (dot(grad_s[unit], keys, NN) * scale).astype(bf16)

        def back_keys(unit):
            both = dot(grad_s[unit], qkv_ref[place(unit)], TN)
            grad_k[unit] = jnp.where(first, both[:SEQ], both[SEQ:]).astype(bf16)

        def store(unit):
            out_ref[place(unit)] = grad_q[unit]
            out_ref[place(unit, 1)] = grad_k[unit]
            out_ref[place(unit, 2)] = grad_v[unit]
            lanes = place(unit)[1]
            sums_ref[0:1, lanes] += jnp.sum(grad_q[unit].astype(f32), axis=0, keepdims=True)
            sums_ref[1:2, lanes] += jnp.sum(grad_v[unit].astype(f32), axis=0, keepdims=True)

        stages = (back_weights, back_values, back_softmax, back_queries, back_keys, store)
        by_stages(UNITS, stages)

    return call(
        kernel,
        (rows // (GROUP * SEQ),),
        [rows_of(3 * PART, GROUP * SEQ), rows_of(width, GROUP * SEQ), rows_of(PART, GROUP * SEQ)],
        [rows_of(3 * PART, GROUP * SEQ), whole((8, PART))],
        [pltpu.VMEM((rows, 3 * PART), bf16), jax.ShapeDtypeStruct((8, PART), f32)],
        flops=7e9,
        bytes_accessed=rows * (PART * 14 + width * 4),
        name="attention_back",
    )(lengths, in_hbm(qkv), in_hbm(weights), in_vmem(grad_attended))


EXTRA = 16
IN_AT = 128


def grad_w_qkv(me, tokens, grad_mixed, sums_qkv, sums_one, sums_two, sums_in):
    rows = tokens.shape[0]
    half = RANKS // 2
    width = 3 * PART

    def kernel(s, x_ref, g_ref, q0_ref, q1_ref, one_ref, two_ref, in_ref, t_ref, m_ref):
        store_by_rank(s, dot(x_ref[...], g_ref[...], TN).astype(bf16), t_ref, m_ref)
        vectors = jnp.concatenate(
            [
                jnp.concatenate([q0_ref[0:2], q1_ref[0:2]], axis=1),
                one_ref[0:3],
                two_ref[0:3],
            ],
            axis=0,
        )
        core = s[0] & 1
        end = IN_AT + SHARD_FF
        rest = jnp.zeros((EXTRA, width - end), bf16)
        for k in range(half):
            blocks = []
            for rank in (2 * k, 2 * k + 1):
                vec = vectors[:, rank * SHARD : (rank + 1) * SHARD]
                vec = jnp.concatenate([vec, jnp.zeros((8, IN_AT - SHARD), f32)], axis=1)
                bias = in_ref[:, rank * SHARD_FF : (rank + 1) * SHARD_FF]
                bias = jnp.concatenate([bias, jnp.zeros((7, SHARD_FF), f32)], axis=0)
                block = jnp.concatenate([vec, bias], axis=1)
                blocks.append(jnp.concatenate([block, jnp.zeros_like(block)], axis=0).astype(bf16))
            away = (s[0] >> 1) ^ k
            for ref, here, block in (
                (m_ref, core, jnp.where(core == 0, blocks[0], blocks[1])),
                (t_ref, 1 - core, jnp.where(core == 0, blocks[1], blocks[0])),
            ):
                ref[slot(away, here), SHARD:, :end] = block
                ref[slot(away, here), SHARD:, end:] = rest

    shape = pltpu.HBM((half, SHARD + EXTRA, width), bf16)
    out = whole((half, SHARD + EXTRA, width))
    return call(
        kernel,
        (1,),
        [
            whole((rows, D)),
            HELD,
            whole((8, PART)),
            whole((8, PART)),
            whole((8, D)),
            whole((8, D)),
            whole((1, FF)),
        ],
        [out, out],
        [shape, shape],
        flops=2 * rows * D * width,
        bytes_accessed=rows * (D * 8) + 2 * D * width,
        name="grad_w_qkv",
    )(me, tokens, in_vmem(grad_mixed), *sums_qkv, sums_one, sums_two, sums_in)


def grad_w_mixed(me, tokens, grad_mixed, attended, grad_branch):
    rows = tokens.shape[0]
    half = RANKS // 2
    width = 3 * PART

    def kernel(s, x_ref, g_ref, o0_ref, o1_ref, da_ref, t_ref, m_ref):
        store_by_rank(s, dot(x_ref[...], g_ref[...], TN).astype(bf16), t_ref, m_ref)
        both = jnp.concatenate([o0_ref[...], o1_ref[...]], axis=1)
        proj = dot(both, da_ref[...], TN).astype(bf16)
        store_by_rank(s, proj, t_ref, m_ref, width)

    shape = pltpu.HBM((half, SHARD, width + D), bf16)
    out = whole((half, SHARD, width + D))
    return call(
        kernel,
        (1,),
        [
            whole((rows, D)),
            HELD,
            HELD,
            HELD,
            HELD,
        ],
        [out, out],
        [shape, shape],
        flops=2 * rows * D * (width + D),
        bytes_accessed=rows * (D * 12) + 2 * D * (width + D),
        name="grad_w_mixed",
    )(
        me,
        tokens,
        in_vmem(grad_mixed),
        *[in_vmem(half) for half in attended],
        in_vmem(grad_branch),
    )


def back_qkv(me, grad_mixed, grad_res_one, weight, before=None):
    rows = grad_res_one.shape[0]
    steps = rows // TILE // 2
    width = 3 * PART

    def compute(g0_ref, g1_ref, dr_ref, w_ref, out_ref):
        both = jnp.concatenate([g0_ref[...], g1_ref[...]], axis=1)
        w = w_ref[...].reshape(D, 2 * width)
        out_ref[...] = (dot(both, w, NT) + dr_ref[...]).astype(bf16)

    def kernel_one(s, g0_ref, g1_ref, dr_ref, *rest):
        refs, (out_ref, w_ref, sem) = rest[: len(weight)], rest[len(weight) :]

        @pl.when(pl.program_id(0) == 0)
        def _():
            weight.load(s[0], refs, w_ref, sem)

        compute(g0_ref, g1_ref, dr_ref, w_ref, out_ref)

    def kernel_two(s, g0_ref, g1_ref, dr_ref, w_ref, before_ref, out_ref):
        compute(g0_ref, g1_ref, dr_ref, w_ref, out_ref)

    def at(width):
        return rows_of(width, TILE, steps if before is not None else 0)

    operands = (me, *[in_vmem(half) for half in grad_mixed], in_hbm(grad_res_one))
    blocks = [at(width), at(width), at(D)]
    out = pltpu.HBM((rows, D), bf16)
    cost = dict(flops=rows * D * 3 * D, bytes_accessed=rows * D * 6 + 2 * D * 3 * D, name="back_qkv")
    if before is None:
        return call(
            kernel_one,
            (steps,),
            blocks + [ANY] * len(weight),
            [at(D), HELD],
            [out, pltpu.VMEM(weight.shape, bf16)],
            [pltpu.SemaphoreType.DMA],
            **cost,
        )(*operands, *weight.arrays)
    return call(
        kernel_two, (steps,), blocks + [HELD, ANY], at(D), out, aliases={5: 0}, **cost
    )(*operands, in_vmem(weight), in_hbm(before))


def adamw_math(moment, square, gradient):
    first_fix = 1.0 - beta_one**STEP
    second_fix = 1.0 - beta_two**STEP
    moment = beta_one * moment + (1.0 - beta_one) * gradient
    square = beta_two * square + (1.0 - beta_two) * gradient * gradient
    update = moment / first_fix / (jnp.sqrt(square / second_fix) + adam_epsilon)
    return (update, moment, square)


def adamw(moment, square, gradient):
    gradient = gradient.astype(f32)
    return (gradient,) + adamw_math(moment, square, gradient)


def flip(bit):
    return [(i, i ^ bit) for i in range(RANKS)]


def swap(value, bit):
    return lax.ppermute(value, "fsdp", flip(bit))


def after(value, *others):
    return lax.optimization_barrier((value,) + others)[0]


def split_swap(value, even_bit, odd_bit):
    return lax.ppermute(
        value, "fsdp", [(i, i ^ (odd_bit if i & 1 else even_bit)) for i in range(RANKS)]
    )


class Gather:
    def __init__(self, shard):
        self.shard = shard

    def start(self, *others):
        if others:
            self.shard = after(self.shard, *others)
        self.one = split_swap(self.shard, 2, 4)
        self.two = split_swap(self.shard, 4, 2)

    def forward(self, *others):
        self.one, self.two = lax.optimization_barrier((self.one, self.two) + others)[:2]
        self.far = split_swap(self.one, 4, 2)
        self.other = [swap(piece, 1) for piece in (self.shard, self.one, self.two)]

    def finish(self, *others):
        self.far = after(self.far, *others)
        self.other.append(swap(self.far, 1))
        return Weight([self.shard, self.one, self.two, self.far] + self.other)


def low_sum(*values):
    total = values[0].astype(f32)
    for value in values[1:]:
        total = total + value.astype(f32)
    return total.astype(bf16)


class Scatter:
    def __init__(self, parts):
        self.theirs, self.mine = parts
        self.got = swap(self.theirs, 1)
        self.by_pairs = False

    def one(self, *others):
        self.got = after(self.got, *others)
        send = low_sum(self.mine[1::2], self.got[1::2])
        self.near_got = split_swap(send, 2, 4)
        return (send,)

    def two(self, *others):
        self.near_got = after(self.near_got, *others)
        send = low_sum(self.mine[2], self.got[2], self.near_got[1])
        self.last = split_swap(send, 4, 2)
        return (send,)

    def three(self, *others):
        last = after(self.last, *others)
        self.owned = low_sum(self.mine[0], self.got[0], self.near_got[0], last)
        return (self.owned,)

    def line(self):
        self.near = lax.ppermute(self.owned, "rep", [(0, 1), (3, 2)])

    def pairs(self):
        self.near = lax.ppermute(self.owned, "rep", [(i, i ^ 1) for i in range(4)])
        self.by_pairs = True

    def four(self, *others):
        self.near = low_sum(self.owned, after(self.near, *others))
        if self.by_pairs:
            self.across = lax.ppermute(self.near, "rep", [(i, i ^ 2) for i in range(4)])
        else:
            self.across = lax.ppermute(self.near, "rep", [(1, 2), (2, 1)])
        return (self.near,)

    def five(self, *others):
        self.total = low_sum(self.near, after(self.across, *others))
        self.back = lax.ppermute(self.total, "rep", [(1, 0), (2, 3)])
        return (self.total,)

    def result(self, rep_index):
        if self.by_pairs:
            return self.near.astype(f32) + self.across.astype(f32)
        inner = (rep_index == 1) | (rep_index == 2)
        return jnp.where(inner, self.total, self.back)


def by_rank(pairs, position):
    stacked = jnp.stack(pairs)
    stacked = jnp.where((position & 2) == 0, stacked, stacked[jnp.array([1, 0, 3, 2])])
    stacked = jnp.where((position & 4) == 0, stacked, stacked[jnp.array([2, 3, 0, 1])])
    return stacked.reshape(RANKS, -1)


def by_head_half(value, half):
    return [value[:, k * D + half * PART : k * D + (half + 1) * PART] for k in range(3)]


def local(
    fsdp,
    rep,
    tokens,
    cotangent,
    lengths,
    w_attn,
    w_in,
    w_out,
    b_in,
    vecs,
    m_attn,
    m_in,
    m_out,
    m_bin,
    m_vecs,
    v_attn,
    v_in,
    v_out,
    v_bin,
    v_vecs,
):
    direct = fsdp == RANKS and rep == 4
    position = lax.axis_index("fsdp")
    rep_index = lax.axis_index("rep")
    part = D // fsdp
    heads_a = [jnp.concatenate(by_head_half(w_attn, h), axis=1) for h in range(2)]
    low_a = jnp.concatenate(heads_a, axis=1).astype(bf16)
    if direct:
        me = position.reshape(1)
        a = Gather(low_a)
        a.start()
        wait = lambda value: after(value, low_a)
    else:
        me = jnp.zeros((1,), jnp.int32)
        wait = lambda value: value
    low_b = jnp.concatenate([wait(w_attn)[:, 3 * D :], w_in], axis=1).astype(bf16)
    low_c = wait(w_out).astype(bf16)
    small = jnp.concatenate([wait(vecs).reshape(1, -1), b_in.reshape(1, -1)], axis=1).astype(bf16)
    if direct:
        b = Gather(low_b)
        c = Gather(low_c)
        got = swap(small, 1)
        first = (position & 1) == 0
        pair = jnp.concatenate([jnp.where(first, small, got), jnp.where(first, got, small)])
        pairs = [pair] + [swap(pair, bit) for bit in (2, 4, 6)]
        a.forward(*pairs)
        b.start(a.one, a.two, *pairs)
        small_all = by_rank(pairs, position)
        weight_a = a.finish()
    else:

        def gather(low):
            full = lax.all_gather(low, "fsdp", axis=0, tiled=True)
            return Weight([full.reshape(RANKS, -1, full.shape[1])])

        weight_a, weight_b, weight_c = gather(low_a), gather(low_b), gather(low_c)
        small_all = lax.all_gather(small, "fsdp", axis=0, tiled=True)

    def ordered(value, *others):
        return after(value, *others) if direct else value

    small_all = small_all.astype(f32)
    vectors = small_all[:, : 8 * part].reshape(fsdp, 8, part).transpose(1, 0, 2).reshape(8, D)
    in_bias = small_all[:, 8 * part :].reshape(1, FF)
    bias = jnp.stack([vectors[0], jnp.zeros((D,), f32), vectors[1]]).reshape(3, 2, PART)
    bias = bias.transpose(1, 0, 2).reshape(1, 6 * PART)

    qkv = project_qkv(me, tokens, weight_a, bias)
    attended, weights = [None, None], [None, None]
    first, second = qkv
    if direct:
        b.forward(*qkv)
        first = after(first, b.one, b.two)
    attended[0], weights[0] = attention(lengths, first)
    if direct:
        c.start(attended[0], *b.other)
        second = after(second, attended[0], *b.other)
        weight_b = b.finish(attended[0])
    attended[1], weights[1] = attention(lengths, second)
    normed_one, inv_one, hidden_low, held_b = project(me, attended, tokens, weight_b, vectors)
    inner = hidden_low
    if direct:
        c.forward(hidden_low)
        inner = after(hidden_low, c.one, c.two)
    activated, slope = expand(me, inner, held_b, in_bias)
    if direct:
        weight_c = c.finish(activated)
    output, grad_res_two, grad_ffn, sums_two, held_c = feed_out(
        me, activated, normed_one, cotangent, weight_c, vectors
    )

    parts_out = grad_w_out(me, activated, grad_ffn)
    grad_pre, sums_in = back_out(me, ordered(grad_ffn, *parts_out), slope, held_c)
    sent = ()
    if direct:
        r_out = Scatter(parts_out)
        sent = r_out.one(grad_pre)
    parts_in = grad_w_in(me, hidden_low, ordered(grad_pre, *sent))
    grad_res_one, grad_branch, *grad_attended, sums_one = back_in(
        me, ordered(grad_pre, *parts_in), grad_res_two, normed_one, inv_one, held_b, vectors
    )
    sent = ()
    if direct:
        r_in = Scatter(parts_in)
        sent = r_out.two(grad_branch) + r_in.one(grad_branch)
    mixed0, sums_q0 = attention_back(
        lengths, qkv[0], weights[0], ordered(grad_attended[0], *sent)
    )
    parts_mix = grad_w_mixed(me, tokens, mixed0, attended, grad_branch)
    sent = parts_mix
    if direct:
        r_mix = Scatter(parts_mix)
        sent = r_out.three(*parts_mix)
        r_out.pairs()
        sent = r_in.two(*sent)
    mixed1, sums_q1 = attention_back(
        lengths, qkv[1], weights[1], ordered(grad_attended[1], *sent)
    )
    parts_qkv = grad_w_qkv(me, tokens, mixed1, (sums_q0, sums_q1), sums_one, sums_two, sums_in)
    sent = ()
    if direct:
        r_qkv = Scatter(parts_qkv)
        sent = r_in.three(*parts_qkv)
        r_in.line()
        sent = r_mix.one(*sent)
        sent = r_qkv.one(*sent)
        sent = r_out.four(*sent)
    half_tokens, held_a = back_qkv(
        me, (mixed0, ordered(mixed1, *sent, *parts_qkv)), grad_res_one, weight_a
    )
    sent = ()
    if direct:
        sent = r_mix.two(half_tokens)
        sent = r_qkv.two(*sent)
        sent = r_in.four(*sent)
    grad_tokens = back_qkv(
        me, (mixed0, ordered(mixed1, *sent)), grad_res_one, held_a, half_tokens
    )
    if direct:
        sent = r_qkv.three(grad_tokens)
        r_qkv.line()
        sent = r_mix.three(*sent)
        r_mix.line()
        r_out.across = after(r_out.across, *sent)
        sent = r_in.five(*sent)
        sent = r_qkv.four(*sent)
        sent = r_mix.four(*sent)
        sent = r_qkv.five(*sent)
        sent = r_mix.five(*sent)
        sum_qkv = r_qkv.result(rep_index)
        sum_out, sum_in, sum_mix = [r.result(rep_index) for r in (r_out, r_in, r_mix)]
        sum_vecs = sum_qkv[SHARD : SHARD + 8, :part]
        sum_bin = sum_qkv[SHARD, IN_AT : IN_AT + FF // fsdp]
        sum_qkv = sum_qkv[:SHARD]
    else:

        def reduce(theirs, mine):
            full = jnp.stack([mine, theirs[jnp.array([0, 2, 1, 3])]], axis=1)
            full = full.reshape(-1, full.shape[-1])
            owned = lax.psum_scatter(full, "fsdp", scatter_dimension=0, tiled=True)
            return lax.psum(owned, "rep")

        sum_out, sum_in, sum_mix = [reduce(*parts) for parts in (parts_out, parts_in, parts_mix)]
        sum_qkv = reduce(*[parts[:, :SHARD] for parts in parts_qkv])
        theirs, mine = [parts[:, SHARD:] for parts in parts_qkv]
        extra = jnp.stack([mine, theirs[jnp.array([0, 2, 1, 3])]], axis=1)
        extra = extra.reshape(RANKS, EXTRA, 3 * PART).astype(f32)
        extra = lax.psum(extra[:, :8], ("fsdp", "rep"))
        all_vecs = extra[:, :, :SHARD].transpose(1, 0, 2).reshape(8, D)
        all_bin = extra[:, 0, IN_AT : IN_AT + SHARD_FF].reshape(FF)
        sum_vecs = lax.dynamic_slice(all_vecs, (0, position * part), (8, part))
        sum_bin = lax.dynamic_slice(all_bin, (position * (FF // fsdp),), (FF // fsdp,))

    grad_out, step_out, mom_out, sq_out = adamw(m_out, v_out, sum_out)
    grad_in, step_in, mom_in, sq_in = adamw(m_in, v_in, sum_in)
    columns = []
    for k in range(3):
        columns += [sum_mix[:, k * PART : (k + 1) * PART].astype(f32), sum_qkv[:, k * PART : (k + 1) * PART].astype(f32)]
    sum_attn = jnp.concatenate(columns + [sum_mix[:, 3 * PART :].astype(f32)], axis=1)
    grad_attn, step_attn, mom_attn, sq_attn = adamw(m_attn, v_attn, sum_attn)
    grad_bin, step_bin, mom_bin, sq_bin = adamw(m_bin, v_bin, sum_bin)
    grad_vecs, step_vecs, mom_vecs, sq_vecs = adamw(m_vecs, v_vecs, sum_vecs)
    return (
        output,
        grad_tokens,
        grad_attn,
        grad_in,
        grad_out,
        grad_bin,
        grad_vecs,
        step_attn,
        step_in,
        step_out,
        step_bin,
        step_vecs,
        mom_attn,
        mom_in,
        mom_out,
        mom_bin,
        mom_vecs,
        sq_attn,
        sq_in,
        sq_out,
        sq_bin,
        sq_vecs,
    )


def solution(mesh):
    rows, row, col = P(("rep", "fsdp"), None), P("fsdp", None), P(None, "fsdp")
    flat = P("fsdp")
    state = (row, row, row, flat, col)
    return jax.shard_map(
        functools.partial(local, mesh.shape["fsdp"], mesh.shape["rep"]),
        mesh=mesh,
        in_specs=(rows, rows, P(("rep", "fsdp"))) + state * 3,
        out_specs=(rows, rows) + state * 4,
        check_vma=False,
    )
```

```python
import functools

import jax
import jax.numpy as jnp
from jax import lax
from jax.experimental import pallas as pl
from jax.experimental.pallas import tpu as pltpu
from jax.sharding import PartitionSpec as P

D = 768
HEADS = 12
HDIM = 64
PART = D // 2
FF = 3072
SEQ = 128
STEP = 5

RANKS = 8
SHARD = D // RANKS
SHARD_FF = FF // RANKS

beta_one = 0.9
beta_two = 0.999
adam_epsilon = 1e-06
norm_epsilon = 1e-05
masked_score = -1000000000.0

bf16 = jnp.bfloat16
f32 = jnp.float32
NN = (((1,), (0,)), ((), ()))
NT = (((1,), (1,)), ((), ()))
TN = (((0,), (0,)), ((), ()))
VMEM_BYTES = 17 * 1024 * 1024
TILE = 256
LIGHT = 1000


def dot(left, right, dims):
    return lax.dot_general(left, right, dims, preferred_element_type=f32)


def call(kernel, grid, in_specs, out_specs, out_shape, scratch=(), flops=0, bytes_accessed=0, name=None, aliases=None):
    return pl.pallas_call(
        kernel,
        grid_spec=pltpu.PrefetchScalarGridSpec(
            num_scalar_prefetch=1,
            grid=grid,
            in_specs=in_specs,
            out_specs=out_specs,
            scratch_shapes=list(scratch),
        ),
        out_shape=out_shape,
        input_output_aliases=aliases or {},
        compiler_params=pltpu.CompilerParams(
            vmem_limit_bytes=VMEM_BYTES, dimension_semantics=("arbitrary",) * len(grid)
        ),
        cost_estimate=pl.CostEstimate(
            flops=int(flops) // LIGHT, bytes_accessed=int(bytes_accessed) // LIGHT, transcendentals=0
        ),
        name=name,
    )


def rows_of(width, tile=TILE, first=0):
    return pl.BlockSpec((tile, width), lambda i, s: (i + first, 0))


def whole(shape):
    return pl.BlockSpec(shape, lambda i, s: (0,) * len(shape))


ANY = pl.BlockSpec(memory_space=pl.ANY)
HELD = pl.BlockSpec(memory_space=pltpu.VMEM)


def in_vmem(array):
    return pltpu.with_memory_space_constraint(array, pltpu.VMEM)


def in_hbm(array):
    return pltpu.with_memory_space_constraint(array, pltpu.HBM)


class Weight:
    def __init__(self, arrays):
        self.arrays = [in_hbm(array) for array in arrays]
        self.shape = (RANKS,) + self.arrays[0].shape[-2:]

    def __len__(self):
        return len(self.arrays)

    def load(self, me, refs, held, sem):
        if len(refs) == 1:
            copies = [pltpu.make_async_copy(refs[0], held, sem)]
        else:
            copies = []
            for number, ref in enumerate(refs):
                owner = me if number < 4 else me ^ 1
                first = jnp.where((owner & 1) == 0, 2, 4)
                rank = owner ^ (0, first, 6 - first, 6)[number % 4]
                copies.append(pltpu.make_async_copy(ref, held.at[rank], sem))
        for copy in copies:
            copy.start()
        for copy in copies:
            copy.wait()


def lane_sum(value):
    return jnp.sum(value, axis=-1, keepdims=True)


def normalize(residual):
    centre = residual - lane_sum(residual) * (1.0 / D)
    variance = lane_sum(centre * centre) * (1.0 / D)
    inv_std = lax.rsqrt(variance + norm_epsilon)
    return (centre * inv_std, inv_std)


def norm_back(grad_normed, normed, inv_std):
    first_mean = lane_sum(grad_normed) * (1.0 / D)
    second_mean = lane_sum(grad_normed * normed) * (1.0 / D)
    return inv_std * (grad_normed - first_mean - normed * second_mean)


def gelu_and_slope(pre_act):
    cumulative = 0.5 * (1.0 + lax.erf(pre_act * 0.7071067811865476))
    density = jnp.exp(-0.5 * pre_act * pre_act) * 0.3989422804014327
    return (pre_act * cumulative, cumulative + pre_act * density)


def project_qkv(me, tokens, weight, bias):
    rows = tokens.shape[0]
    count = len(weight)
    width = 3 * PART

    def kernel(s, x_ref, b_ref, *rest):
        refs, (out0_ref, out1_ref, w_ref, sem) = rest[:count], rest[count:]

        @pl.when(pl.program_id(0) == 0)
        def _():
            weight.load(s[0], refs, w_ref, sem)

        rounded = (dot(x_ref[...], w_ref[...].reshape(D, 2 * width), NN) + b_ref[...]).astype(bf16)
        for h, out_ref in enumerate((out0_ref, out1_ref)):
            lead = h * width
            out_ref[:, :PART] = rounded[:, lead : lead + PART] * HDIM ** (-0.5)
            out_ref[:, PART:] = rounded[:, lead + PART : lead + width]

    return call(
        kernel,
        (rows // TILE,),
        [rows_of(D), whole((1, 2 * width))] + [ANY] * count,
        [rows_of(width), rows_of(width)],
        [
            pltpu.HBM((rows, width), bf16),
            pltpu.HBM((rows, width), bf16),
        ],
        [pltpu.VMEM(weight.shape, bf16), pltpu.SemaphoreType.DMA],
        flops=2 * rows * D * width * 2,
        bytes_accessed=2 * (rows * D * 4 + 3 * D * D),
        name="qkv",
    )(me, tokens, bias, *weight.arrays)


def head_masks():
    lane = lax.broadcasted_iota(jnp.int32, (SEQ, 2 * HDIM), 1)
    return lane < HDIM


def stack_heads(value, first):
    zero = jnp.zeros_like(value)
    return jnp.concatenate([jnp.where(first, value, zero), jnp.where(first, zero, value)], axis=0)


GROUP = 4


def by_stages(units, stages):
    for stage in stages:
        for unit in units:
            stage(unit)


def staggered(units, stages):
    for start in range(len(units) + len(stages) - 1):
        for number in reversed(range(len(stages))):
            if 0 <= start - number < len(units):
                stages[number](units[start - number])


def place(unit, part=0):
    lead = part * PART + unit[1] * 2 * HDIM
    return slice(unit[0] * SEQ, (unit[0] + 1) * SEQ), slice(lead, lead + 2 * HDIM)


def weight_place(unit):
    return slice(unit[0] * SEQ, (unit[0] + 1) * SEQ), slice(unit[1] * 2 * SEQ, (unit[1] + 1) * 2 * SEQ)


UNITS = [(pair, heads) for pair in range(GROUP) for heads in range(PART // (2 * HDIM))]


def attention(lengths, qkv):
    rows = qkv.shape[0]

    def kernel(s, qkv_ref, out_ref, p_ref):
        first = head_masks()
        key = lax.broadcasted_iota(jnp.int32, (SEQ, SEQ), 1)
        valid = [key < s[pl.program_id(0) * GROUP + pair] for pair in range(GROUP)]
        scores, low = {}, {}

        def score(unit):
            keys = stack_heads(qkv_ref[place(unit, 1)], first)
            scores[unit] = dot(qkv_ref[place(unit)], keys, NT)

        def soften(unit):
            halves = []
            for part in range(2):
                one = scores[unit][:, part * SEQ : (part + 1) * SEQ]
                one = jnp.where(valid[unit[0]], one, masked_score)
                raised = jnp.exp(one - jnp.max(one, axis=-1, keepdims=True))
                halves.append(raised * (1.0 / lane_sum(raised)))
            weights = jnp.concatenate(halves, axis=1)
            p_ref[weight_place(unit)] = weights
            low[unit] = weights.astype(bf16)

        def attend(unit):
            values = stack_heads(qkv_ref[place(unit, 2)], first)
            out_ref[place(unit)] = dot(low[unit], values, NN).astype(bf16)

        staggered(UNITS, (score, soften, attend))

    width = HEADS * SEQ // 2
    return call(
        kernel,
        (rows // (GROUP * SEQ),),
        [rows_of(3 * PART, GROUP * SEQ)],
        [rows_of(PART, GROUP * SEQ), rows_of(width, GROUP * SEQ)],
        [pltpu.VMEM((rows, PART), bf16), pltpu.HBM((rows, width), f32)],
        flops=4e9,
        bytes_accessed=rows * (PART * 8 + width * 4),
        name="attention",
    )(lengths, in_hbm(qkv))


def project(me, attended, tokens, weight, vectors):
    rows = tokens.shape[0]
    count = len(weight)

    def kernel(s, o0_ref, o1_ref, x_ref, v_ref, *rest):
        refs, (n1_ref, inv_ref, hb_ref, w_ref, sem) = rest[:count], rest[count:]

        @pl.when(pl.program_id(0) == 0)
        def _():
            weight.load(s[0], refs, w_ref, sem)

        both = jnp.concatenate([o0_ref[...], o1_ref[...]], axis=1)
        branch = dot(both, w_ref[:, :, :D].reshape(D, D), NN) + v_ref[2:3, :]
        normed, inv_std = normalize(x_ref[...].astype(f32) + branch)
        n1_ref[...] = normed
        inv_ref[...] = inv_std
        hb_ref[...] = (normed * v_ref[3:4, :] + v_ref[4:5, :]).astype(bf16)

    return call(
        kernel,
        (rows // TILE,),
        [rows_of(PART), rows_of(PART), rows_of(D), whole((8, D))] + [ANY] * count,
        [rows_of(D), rows_of(1), rows_of(D), HELD],
        [
            pltpu.VMEM((rows, D), f32),
            pltpu.HBM((rows, 1), f32),
            pltpu.VMEM((rows, D), bf16),
            pltpu.VMEM(weight.shape, bf16),
        ],
        [pltpu.SemaphoreType.DMA],
        flops=2 * rows * D * D,
        bytes_accessed=rows * D * 10 + 2 * D * (D + FF),
        name="project",
    )(me, *[in_vmem(half) for half in attended], tokens, vectors, *weight.arrays)


def expand(me, hidden_low, weight, in_bias):
    rows = hidden_low.shape[0]
    tile = 512

    def kernel(s, h_ref, b_ref, w_ref, f_ref, sl_ref):
        low = h_ref[...]
        for j in range(FF // tile):
            lanes = slice(j * tile, (j + 1) * tile)
            w = w_ref[:, :, D + j * tile : D + (j + 1) * tile].reshape(D, tile)
            act, slope = gelu_and_slope(dot(low, w, NN) + b_ref[:, lanes])
            f_ref[:, lanes] = act.astype(bf16)
            sl_ref[:, lanes] = slope.astype(bf16)

    return call(
        kernel,
        (rows // TILE,),
        [rows_of(D), whole((1, FF)), HELD],
        [rows_of(FF), rows_of(FF)],
        [pltpu.VMEM((rows, FF), bf16), pltpu.VMEM((rows, FF), bf16)],
        flops=2 * rows * D * FF,
        bytes_accessed=rows * (D * 2 + FF * 4) + 2 * D * FF,
        name="expand",
    )(me, in_vmem(hidden_low), in_bias, in_vmem(weight))


def feed_out(me, activated, normed_one, cotangent, weight, vectors):
    rows = activated.shape[0]
    count = len(weight)

    def kernel(s, f_ref, n1_ref, g_ref, v_ref, *rest):
        refs = rest[:count]
        y_ref, dr_ref, dz_ref, sums_ref, w_ref, sem = rest[count:]

        @pl.when(pl.program_id(0) == 0)
        def _():
            weight.load(s[0], refs, w_ref, sem)
            sums_ref[...] = jnp.zeros_like(sums_ref)

        branch = dot(f_ref[...], w_ref[...].reshape(FF, D), NN) + v_ref[5:6, :]
        hidden = n1_ref[...] * v_ref[3:4, :] + v_ref[4:5, :]
        normed, inv_std = normalize(hidden + branch)
        y_ref[...] = (normed * v_ref[6:7, :] + v_ref[7:8, :]).astype(bf16)
        grad_y = g_ref[...].astype(f32)
        sums_ref[1:2, :] += jnp.sum(grad_y * normed, axis=0, keepdims=True)
        sums_ref[2:3, :] += jnp.sum(grad_y, axis=0, keepdims=True)
        grad_res = norm_back(grad_y * v_ref[6:7, :], normed, inv_std)
        dr_ref[...] = grad_res
        low = grad_res.astype(bf16)
        dz_ref[...] = low
        sums_ref[0:1, :] += jnp.sum(low.astype(f32), axis=0, keepdims=True)

    return call(
        kernel,
        (rows // TILE,),
        [rows_of(FF), rows_of(D), rows_of(D), whole((8, D))] + [ANY] * count,
        [rows_of(D), rows_of(D), rows_of(D), whole((8, D)), HELD],
        [
            jax.ShapeDtypeStruct((rows, D), bf16),
            pltpu.VMEM((rows, D), f32),
            jax.ShapeDtypeStruct((rows, D), bf16),
            jax.ShapeDtypeStruct((8, D), f32),
            pltpu.VMEM(weight.shape, bf16),
        ],
        [pltpu.SemaphoreType.DMA],
        flops=2 * rows * D * FF,
        bytes_accessed=rows * (D * 14 + FF * 2) + 2 * D * FF,
        name="feed_out",
    )(me, in_vmem(activated), in_vmem(normed_one), cotangent, vectors, *weight.arrays)


def slot(chip, core):
    return jnp.where(core == 0, chip, (chip & 1) * 2 + (chip >> 1))


def grad_w_out(me, activated, grad_ffn):
    rows = activated.shape[0]
    half = RANKS // 2

    def kernel(s, f_ref, dz_ref, t_ref, m_ref):
        block = dot(f_ref[...], dz_ref[...], TN).astype(bf16)
        low, high = block[:SHARD_FF], block[SHARD_FF:]
        even = (s[0] & 1) == 0
        m_ref[0] = jnp.where(even, low, high)
        t_ref[0] = jnp.where(even, high, low)

    shape = pltpu.HBM((half, SHARD_FF, D), bf16)

    def out(flip):
        return pl.BlockSpec((1, SHARD_FF, D), lambda i, s: (slot(i, (s[0] & 1) ^ flip), 0, 0))

    return call(
        kernel,
        (half,),
        [
            pl.BlockSpec((rows, 2 * SHARD_FF), lambda i, s: (0, (s[0] >> 1) ^ i)),
            whole((rows, D)),
        ],
        [out(1), out(0)],
        [shape, shape],
        flops=2 * rows * D * FF,
        bytes_accessed=rows * (D * 2 + FF * 2) + 2 * D * FF,
        name="grad_w_out",
    )(me, in_vmem(activated), grad_ffn)


def back_out(me, grad_ffn, slope, weight):
    rows = grad_ffn.shape[0]

    def kernel(s, dz_ref, sl_ref, w_ref, du_ref, sums_ref):
        @pl.when(pl.program_id(0) == 0)
        def _():
            sums_ref[...] = jnp.zeros_like(sums_ref)

        dz = dz_ref[...]
        for r in range(RANKS // 2):
            lanes = slice(2 * r * SHARD_FF, 2 * (r + 1) * SHARD_FF)
            w = w_ref[2 * r : 2 * r + 2].reshape(2 * SHARD_FF, D)
            grad = dot(dz, w, NT) * sl_ref[:, lanes].astype(f32)
            low = grad.astype(bf16)
            du_ref[:, lanes] = low
            sums_ref[:, lanes] += jnp.sum(low.astype(f32), axis=0, keepdims=True)

    return call(
        kernel,
        (rows // TILE,),
        [rows_of(D), rows_of(FF), HELD],
        [rows_of(FF), whole((1, FF))],
        [pltpu.VMEM((rows, FF), bf16), jax.ShapeDtypeStruct((1, FF), f32)],
        flops=2 * rows * D * FF,
        bytes_accessed=rows * (D * 2 + FF * 4) + 2 * D * FF,
        name="back_out",
    )(me, grad_ffn, in_vmem(slope), in_vmem(weight))


def back_in(me, grad_pre, grad_res_two, normed_one, inv_one, weight, vectors):
    rows = grad_pre.shape[0]

    def kernel(
        s, du_ref, dr2_ref, n1_ref, inv_ref, v_ref, w_ref, dr1_ref, da_ref, do0_ref, do1_ref, sums_ref
    ):
        @pl.when(pl.program_id(0) == 0)
        def _():
            sums_ref[...] = jnp.zeros_like(sums_ref)

        w_in = w_ref[:, :, D:].reshape(D, FF)
        grad_hidden = dot(du_ref[...], w_in, NT) + dr2_ref[...]
        normed = n1_ref[...]
        sums_ref[1:2, :] += jnp.sum(grad_hidden * normed, axis=0, keepdims=True)
        sums_ref[2:3, :] += jnp.sum(grad_hidden, axis=0, keepdims=True)
        grad_res = norm_back(grad_hidden * v_ref[3:4, :], normed, inv_ref[...])
        dr1_ref[...] = grad_res
        low = grad_res.astype(bf16)
        da_ref[...] = low
        sums_ref[0:1, :] += jnp.sum(low.astype(f32), axis=0, keepdims=True)
        w_proj = w_ref[:, :, :D].reshape(D, D)
        grad_attended = dot(low, w_proj, NT).astype(bf16)
        do0_ref[...] = grad_attended[:, :PART]
        do1_ref[...] = grad_attended[:, PART:]

    return call(
        kernel,
        (rows // TILE,),
        [rows_of(FF), rows_of(D), rows_of(D), rows_of(1), whole((8, D))] + [HELD],
        [rows_of(D), rows_of(D), rows_of(PART), rows_of(PART), whole((8, D))],
        [
            pltpu.HBM((rows, D), f32),
            pltpu.VMEM((rows, D), bf16),
            pltpu.VMEM((rows, PART), bf16),
            pltpu.VMEM((rows, PART), bf16),
            jax.ShapeDtypeStruct((8, D), f32),
        ],
        flops=2 * rows * D * (D + FF),
        bytes_accessed=rows * (D * 16 + FF * 2) + 2 * D * (D + FF),
        name="back_in",
    )(
        me,
        in_vmem(grad_pre),
        in_vmem(grad_res_two),
        in_vmem(normed_one),
        in_hbm(inv_one),
        vectors,
        in_vmem(weight),
    )


def store_by_rank(s, block, t_ref, m_ref, first=0):
    core = s[0] & 1
    lanes = slice(first, first + block.shape[1])
    for k in range(RANKS // 2):
        low = block[2 * k * SHARD : (2 * k + 1) * SHARD]
        high = block[(2 * k + 1) * SHARD : (2 * k + 2) * SHARD]
        away = (s[0] >> 1) ^ k
        m_ref[slot(away, core), :SHARD, lanes] = jnp.where(core == 0, low, high)
        t_ref[slot(away, 1 - core), :SHARD, lanes] = jnp.where(core == 0, high, low)


def grad_w_in(me, hidden_low, grad_pre):
    rows = hidden_low.shape[0]
    half = RANKS // 2

    def kernel(s, h_ref, du_ref, t_ref, m_ref):
        store_by_rank(s, dot(h_ref[...], du_ref[...], TN).astype(bf16), t_ref, m_ref)

    shape = pltpu.HBM((half, SHARD, FF), bf16)
    out = pl.BlockSpec((half, SHARD, D), lambda i, s: (0, 0, i))
    return call(
        kernel,
        (FF // D,),
        [whole((rows, D)), pl.BlockSpec((rows, D), lambda i, s: (0, i))],
        [out, out],
        [shape, shape],
        flops=2 * rows * D * FF,
        bytes_accessed=rows * (D * 4 + FF * 2) + 2 * D * FF,
        name="grad_w_in",
    )(me, in_vmem(hidden_low), in_vmem(grad_pre))


def attention_back(lengths, qkv, weights, grad_attended):
    rows = qkv.shape[0]
    scale = HDIM ** (-0.5)
    width = HEADS * SEQ // 2

    def kernel(s, qkv_ref, p_ref, do_ref, out_ref, sums_ref):
        @pl.when(pl.program_id(0) == 0)
        def _():
            sums_ref[...] = jnp.zeros_like(sums_ref)

        first = head_masks()
        grad_p, grad_s, grad_q, grad_k, grad_v = {}, {}, {}, {}, {}

        def back_weights(unit):
            values = stack_heads(qkv_ref[place(unit, 2)], first)
            grad_p[unit] = dot(do_ref[place(unit)], values, NT)

        def back_values(unit):
            both = dot(p_ref[weight_place(unit)].astype(bf16), do_ref[place(unit)], TN)
            grad_v[unit] = jnp.where(first, both[:SEQ], both[SEQ:]).astype(bf16)

        def back_softmax(unit):
            p = p_ref[weight_place(unit)]
            product = grad_p[unit] * p
            halves = []
            for part in range(2):
                cut = slice(part * SEQ, (part + 1) * SEQ)
                inner = grad_p[unit][:, cut] - lane_sum(product[:, cut])
                halves.append((p[:, cut] * inner).astype(bf16))
            grad_s[unit] = jnp.concatenate(halves, axis=1)

        def back_queries(unit):
            keys = stack_heads(qkv_ref[place(unit, 1)], first)
            grad_q[unit] = (dot(grad_s[unit], keys, NN) * scale).astype(bf16)

        def back_keys(unit):
            both = dot(grad_s[unit], qkv_ref[place(unit)], TN)
            grad_k[unit] = jnp.where(first, both[:SEQ], both[SEQ:]).astype(bf16)

        def store(unit):
            out_ref[place(unit)] = grad_q[unit]
            out_ref[place(unit, 1)] = grad_k[unit]
            out_ref[place(unit, 2)] = grad_v[unit]
            lanes = place(unit)[1]
            sums_ref[0:1, lanes] += jnp.sum(grad_q[unit].astype(f32), axis=0, keepdims=True)
            sums_ref[1:2, lanes] += jnp.sum(grad_v[unit].astype(f32), axis=0, keepdims=True)

        stages = (back_weights, back_values, back_softmax, back_queries, back_keys, store)
        by_stages(UNITS, stages)

    return call(
        kernel,
        (rows // (GROUP * SEQ),),
        [rows_of(3 * PART, GROUP * SEQ), rows_of(width, GROUP * SEQ), rows_of(PART, GROUP * SEQ)],
        [rows_of(3 * PART, GROUP * SEQ), whole((8, PART))],
        [pltpu.VMEM((rows, 3 * PART), bf16), jax.ShapeDtypeStruct((8, PART), f32)],
        flops=7e9,
        bytes_accessed=rows * (PART * 14 + width * 4),
        name="attention_back",
    )(lengths, in_hbm(qkv), in_hbm(weights), in_vmem(grad_attended))


EXTRA = 16
IN_AT = 128


def grad_w_qkv(me, tokens, grad_mixed, sums_qkv, sums_one, sums_two, sums_in):
    rows = tokens.shape[0]
    half = RANKS // 2
    width = 3 * PART

    def kernel(s, x_ref, g_ref, q0_ref, q1_ref, one_ref, two_ref, in_ref, t_ref, m_ref):
        store_by_rank(s, dot(x_ref[...], g_ref[...], TN).astype(bf16), t_ref, m_ref)
        vectors = jnp.concatenate(
            [
                jnp.concatenate([q0_ref[0:2], q1_ref[0:2]], axis=1),
                one_ref[0:3],
                two_ref[0:3],
            ],
            axis=0,
        )
        core = s[0] & 1
        end = IN_AT + SHARD_FF
        rest = jnp.zeros((EXTRA, width - end), bf16)
        for k in range(half):
            blocks = []
            for rank in (2 * k, 2 * k + 1):
                vec = vectors[:, rank * SHARD : (rank + 1) * SHARD]
                vec = jnp.concatenate([vec, jnp.zeros((8, IN_AT - SHARD), f32)], axis=1)
                bias = in_ref[:, rank * SHARD_FF : (rank + 1) * SHARD_FF]
                bias = jnp.concatenate([bias, jnp.zeros((7, SHARD_FF), f32)], axis=0)
                block = jnp.concatenate([vec, bias], axis=1)
                blocks.append(jnp.concatenate([block, jnp.zeros_like(block)], axis=0).astype(bf16))
            away = (s[0] >> 1) ^ k
            for ref, here, block in (
                (m_ref, core, jnp.where(core == 0, blocks[0], blocks[1])),
                (t_ref, 1 - core, jnp.where(core == 0, blocks[1], blocks[0])),
            ):
                ref[slot(away, here), SHARD:, :end] = block
                ref[slot(away, here), SHARD:, end:] = rest

    shape = pltpu.HBM((half, SHARD + EXTRA, width), bf16)
    out = whole((half, SHARD + EXTRA, width))
    return call(
        kernel,
        (1,),
        [
            whole((rows, D)),
            HELD,
            whole((8, PART)),
            whole((8, PART)),
            whole((8, D)),
            whole((8, D)),
            whole((1, FF)),
        ],
        [out, out],
        [shape, shape],
        flops=2 * rows * D * width,
        bytes_accessed=rows * (D * 8) + 2 * D * width,
        name="grad_w_qkv",
    )(me, tokens, in_vmem(grad_mixed), *sums_qkv, sums_one, sums_two, sums_in)


def grad_w_mixed(me, tokens, grad_mixed, attended, grad_branch):
    rows = tokens.shape[0]
    half = RANKS // 2
    width = 3 * PART

    def kernel(s, x_ref, g_ref, o0_ref, o1_ref, da_ref, t_ref, m_ref):
        store_by_rank(s, dot(x_ref[...], g_ref[...], TN).astype(bf16), t_ref, m_ref)
        both = jnp.concatenate([o0_ref[...], o1_ref[...]], axis=1)
        proj = dot(both, da_ref[...], TN).astype(bf16)
        store_by_rank(s, proj, t_ref, m_ref, width)

    shape = pltpu.HBM((half, SHARD, width + D), bf16)
    out = whole((half, SHARD, width + D))
    return call(
        kernel,
        (1,),
        [
            whole((rows, D)),
            HELD,
            HELD,
            HELD,
            HELD,
        ],
        [out, out],
        [shape, shape],
        flops=2 * rows * D * (width + D),
        bytes_accessed=rows * (D * 12) + 2 * D * (width + D),
        name="grad_w_mixed",
    )(
        me,
        tokens,
        in_vmem(grad_mixed),
        *[in_vmem(half) for half in attended],
        in_vmem(grad_branch),
    )


def back_qkv(me, grad_mixed, grad_res_one, weight, before=None):
    rows = grad_res_one.shape[0]
    steps = rows // TILE // 2
    width = 3 * PART

    def compute(g0_ref, g1_ref, dr_ref, w_ref, out_ref):
        both = jnp.concatenate([g0_ref[...], g1_ref[...]], axis=1)
        w = w_ref[...].reshape(D, 2 * width)
        out_ref[...] = (dot(both, w, NT) + dr_ref[...]).astype(bf16)

    def kernel_one(s, g0_ref, g1_ref, dr_ref, *rest):
        refs, (out_ref, w_ref, sem) = rest[: len(weight)], rest[len(weight) :]

        @pl.when(pl.program_id(0) == 0)
        def _():
            weight.load(s[0], refs, w_ref, sem)

        compute(g0_ref, g1_ref, dr_ref, w_ref, out_ref)

    def kernel_two(s, g0_ref, g1_ref, dr_ref, w_ref, before_ref, out_ref):
        compute(g0_ref, g1_ref, dr_ref, w_ref, out_ref)

    def at(width):
        return rows_of(width, TILE, steps if before is not None else 0)

    operands = (me, *[in_vmem(half) for half in grad_mixed], in_hbm(grad_res_one))
    blocks = [at(width), at(width), at(D)]
    out = pltpu.HBM((rows, D), bf16)
    cost = dict(flops=rows * D * 3 * D, bytes_accessed=rows * D * 6 + 2 * D * 3 * D, name="back_qkv")
    if before is None:
        return call(
            kernel_one,
            (steps,),
            blocks + [ANY] * len(weight),
            [at(D), HELD],
            [out, pltpu.VMEM(weight.shape, bf16)],
            [pltpu.SemaphoreType.DMA],
            **cost,
        )(*operands, *weight.arrays)
    return call(
        kernel_two, (steps,), blocks + [HELD, ANY], at(D), out, aliases={5: 0}, **cost
    )(*operands, in_vmem(weight), in_hbm(before))


def adamw_math(moment, square, gradient):
    first_fix = 1.0 - beta_one**STEP
    second_fix = 1.0 - beta_two**STEP
    moment = beta_one * moment + (1.0 - beta_one) * gradient
    square = beta_two * square + (1.0 - beta_two) * gradient * gradient
    update = moment / first_fix / (jnp.sqrt(square / second_fix) + adam_epsilon)
    return (update, moment, square)


def adamw(moment, square, gradient):
    gradient = gradient.astype(f32)
    return (gradient,) + adamw_math(moment, square, gradient)


def flip(bit):
    return [(i, i ^ bit) for i in range(RANKS)]


def swap(value, bit):
    return lax.ppermute(value, "fsdp", flip(bit))


def after(value, *others):
    return lax.optimization_barrier((value,) + others)[0]


def split_swap(value, even_bit, odd_bit):
    return lax.ppermute(
        value, "fsdp", [(i, i ^ (odd_bit if i & 1 else even_bit)) for i in range(RANKS)]
    )


class Gather:
    def __init__(self, shard):
        self.shard = shard

    def start(self, *others):
        if others:
            self.shard = after(self.shard, *others)
        self.one = split_swap(self.shard, 2, 4)
        self.two = split_swap(self.shard, 4, 2)

    def forward(self, *others):
        self.one, self.two = lax.optimization_barrier((self.one, self.two) + others)[:2]
        self.far = split_swap(self.one, 4, 2)
        self.other = [swap(piece, 1) for piece in (self.shard, self.one, self.two)]

    def finish(self, *others):
        self.far = after(self.far, *others)
        self.other.append(swap(self.far, 1))
        return Weight([self.shard, self.one, self.two, self.far] + self.other)


def low_sum(*values):
    total = values[0].astype(f32)
    for value in values[1:]:
        total = total + value.astype(f32)
    return total.astype(bf16)


class Scatter:
    def __init__(self, parts):
        self.theirs, self.mine = parts
        self.got = swap(self.theirs, 1)
        self.by_pairs = False

    def one(self, *others):
        self.got = after(self.got, *others)
        send = low_sum(self.mine[1::2], self.got[1::2])
        self.near_got = split_swap(send, 2, 4)
        return (send,)

    def two(self, *others):
        self.near_got = after(self.near_got, *others)
        send = low_sum(self.mine[2], self.got[2], self.near_got[1])
        self.last = split_swap(send, 4, 2)
        return (send,)

    def three(self, *others):
        last = after(self.last, *others)
        self.owned = low_sum(self.mine[0], self.got[0], self.near_got[0], last)
        return (self.owned,)

    def line(self):
        self.near = lax.ppermute(self.owned, "rep", [(0, 1), (3, 2)])

    def pairs(self):
        self.near = lax.ppermute(self.owned, "rep", [(i, i ^ 1) for i in range(4)])
        self.by_pairs = True

    def four(self, *others):
        self.near = low_sum(self.owned, after(self.near, *others))
        if self.by_pairs:
            self.across = lax.ppermute(self.near, "rep", [(i, i ^ 2) for i in range(4)])
        else:
            self.across = lax.ppermute(self.near, "rep", [(1, 2), (2, 1)])
        return (self.near,)

    def five(self, *others):
        self.total = low_sum(self.near, after(self.across, *others))
        self.back = lax.ppermute(self.total, "rep", [(1, 0), (2, 3)])
        return (self.total,)

    def result(self, rep_index):
        if self.by_pairs:
            return self.near.astype(f32) + self.across.astype(f32)
        inner = (rep_index == 1) | (rep_index == 2)
        return jnp.where(inner, self.total, self.back)


def by_rank(pairs, position):
    stacked = jnp.stack(pairs)
    stacked = jnp.where((position & 2) == 0, stacked, stacked[jnp.array([1, 0, 3, 2])])
    stacked = jnp.where((position & 4) == 0, stacked, stacked[jnp.array([2, 3, 0, 1])])
    return stacked.reshape(RANKS, -1)


def by_head_half(value, half):
    return [value[:, k * D + half * PART : k * D + (half + 1) * PART] for k in range(3)]


def local(
    fsdp,
    rep,
    tokens,
    cotangent,
    lengths,
    w_attn,
    w_in,
    w_out,
    b_in,
    vecs,
    m_attn,
    m_in,
    m_out,
    m_bin,
    m_vecs,
    v_attn,
    v_in,
    v_out,
    v_bin,
    v_vecs,
):
    direct = fsdp == RANKS and rep == 4
    position = lax.axis_index("fsdp")
    rep_index = lax.axis_index("rep")
    part = D // fsdp
    heads_a = [jnp.concatenate(by_head_half(w_attn, h), axis=1) for h in range(2)]
    low_a = jnp.concatenate(heads_a, axis=1).astype(bf16)
    if direct:
        me = position.reshape(1)
        a = Gather(low_a)
        a.start()
        wait = lambda value: after(value, low_a)
    else:
        me = jnp.zeros((1,), jnp.int32)
        wait = lambda value: value
    low_b = jnp.concatenate([wait(w_attn)[:, 3 * D :], w_in], axis=1).astype(bf16)
    low_c = wait(w_out).astype(bf16)
    small = jnp.concatenate([wait(vecs).reshape(1, -1), b_in.reshape(1, -1)], axis=1).astype(bf16)
    if direct:
        b = Gather(low_b)
        c = Gather(low_c)
        got = swap(small, 1)
        first = (position & 1) == 0
        pair = jnp.concatenate([jnp.where(first, small, got), jnp.where(first, got, small)])
        pairs = [pair] + [swap(pair, bit) for bit in (2, 4, 6)]
        a.forward(*pairs)
        b.start(a.one, a.two, *pairs)
        small_all = by_rank(pairs, position)
        weight_a = a.finish()
    else:

        def gather(low):
            full = lax.all_gather(low, "fsdp", axis=0, tiled=True)
            return Weight([full.reshape(RANKS, -1, full.shape[1])])

        weight_a, weight_b, weight_c = gather(low_a), gather(low_b), gather(low_c)
        small_all = lax.all_gather(small, "fsdp", axis=0, tiled=True)

    def ordered(value, *others):
        return after(value, *others) if direct else value

    small_all = small_all.astype(f32)
    vectors = small_all[:, : 8 * part].reshape(fsdp, 8, part).transpose(1, 0, 2).reshape(8, D)
    in_bias = small_all[:, 8 * part :].reshape(1, FF)
    bias = jnp.stack([vectors[0], jnp.zeros((D,), f32), vectors[1]]).reshape(3, 2, PART)
    bias = bias.transpose(1, 0, 2).reshape(1, 6 * PART)

    qkv = project_qkv(me, tokens, weight_a, bias)
    attended, weights = [None, None], [None, None]
    first, second = qkv
    if direct:
        b.forward(*qkv)
        first = after(first, b.one, b.two)
    attended[0], weights[0] = attention(lengths, first)
    if direct:
        c.start(attended[0], *b.other)
        second = after(second, attended[0], *b.other)
        weight_b = b.finish(attended[0])
    attended[1], weights[1] = attention(lengths, second)
    normed_one, inv_one, hidden_low, held_b = project(me, attended, tokens, weight_b, vectors)
    inner = hidden_low
    if direct:
        c.forward(hidden_low)
        inner = after(hidden_low, c.one, c.two)
    activated, slope = expand(me, inner, held_b, in_bias)
    if direct:
        weight_c = c.finish(activated)
    output, grad_res_two, grad_ffn, sums_two, held_c = feed_out(
        me, activated, normed_one, cotangent, weight_c, vectors
    )

    parts_out = grad_w_out(me, activated, grad_ffn)
    grad_pre, sums_in = back_out(me, ordered(grad_ffn, *parts_out), slope, held_c)
    sent = ()
    if direct:
        r_out = Scatter(parts_out)
        sent = r_out.one(grad_pre)
    parts_in = grad_w_in(me, hidden_low, ordered(grad_pre, *sent))
    grad_res_one, grad_branch, *grad_attended, sums_one = back_in(
        me, ordered(grad_pre, *parts_in), grad_res_two, normed_one, inv_one, held_b, vectors
    )
    sent = ()
    if direct:
        r_in = Scatter(parts_in)
        sent = r_out.two(grad_branch) + r_in.one(grad_branch)
    mixed0, sums_q0 = attention_back(
        lengths, qkv[0], weights[0], ordered(grad_attended[0], *sent)
    )
    parts_mix = grad_w_mixed(me, tokens, mixed0, attended, grad_branch)
    sent = parts_mix
    if direct:
        r_mix = Scatter(parts_mix)
        sent = r_out.three(*parts_mix)
        r_out.pairs()
        sent = r_in.two(*sent)
    mixed1, sums_q1 = attention_back(
        lengths, qkv[1], weights[1], ordered(grad_attended[1], *sent)
    )
    parts_qkv = grad_w_qkv(me, tokens, mixed1, (sums_q0, sums_q1), sums_one, sums_two, sums_in)
    sent = ()
    if direct:
        r_qkv = Scatter(parts_qkv)
        sent = r_in.three(*parts_qkv)
        r_in.line()
        sent = r_mix.one(*sent)
        sent = r_qkv.one(*sent)
        sent = r_out.four(*sent)
    half_tokens, held_a = back_qkv(
        me, (mixed0, ordered(mixed1, *sent, *parts_qkv)), grad_res_one, weight_a
    )
    sent = ()
    if direct:
        sent = r_mix.two(half_tokens)
        sent = r_qkv.two(*sent)
        sent = r_in.four(*sent)
    grad_tokens = back_qkv(
        me, (mixed0, ordered(mixed1, *sent)), grad_res_one, held_a, half_tokens
    )
    if direct:
        sent = r_qkv.three(grad_tokens)
        r_qkv.line()
        sent = r_mix.three(*sent)
        r_mix.line()
        r_out.across = after(r_out.across, *sent)
        sent = r_in.five(*sent)
        sent = r_qkv.four(*sent)
        sent = r_mix.four(*sent)
        sent = r_qkv.five(*sent)
        sent = r_mix.five(*sent)
        sum_qkv = r_qkv.result(rep_index)
        sum_out, sum_in, sum_mix = [r.result(rep_index) for r in (r_out, r_in, r_mix)]
        sum_vecs = sum_qkv[SHARD : SHARD + 8, :part]
        sum_bin = sum_qkv[SHARD, IN_AT : IN_AT + FF // fsdp]
        sum_qkv = sum_qkv[:SHARD]
    else:

        def reduce(theirs, mine):
            full = jnp.stack([mine, theirs[jnp.array([0, 2, 1, 3])]], axis=1)
            full = full.reshape(-1, full.shape[-1])
            owned = lax.psum_scatter(full, "fsdp", scatter_dimension=0, tiled=True)
            return lax.psum(owned, "rep")

        sum_out, sum_in, sum_mix = [reduce(*parts) for parts in (parts_out, parts_in, parts_mix)]
        sum_qkv = reduce(*[parts[:, :SHARD] for parts in parts_qkv])
        theirs, mine = [parts[:, SHARD:] for parts in parts_qkv]
        extra = jnp.stack([mine, theirs[jnp.array([0, 2, 1, 3])]], axis=1)
        extra = extra.reshape(RANKS, EXTRA, 3 * PART).astype(f32)
        extra = lax.psum(extra[:, :8], ("fsdp", "rep"))
        all_vecs = extra[:, :, :SHARD].transpose(1, 0, 2).reshape(8, D)
        all_bin = extra[:, 0, IN_AT : IN_AT + SHARD_FF].reshape(FF)
        sum_vecs = lax.dynamic_slice(all_vecs, (0, position * part), (8, part))
        sum_bin = lax.dynamic_slice(all_bin, (position * (FF // fsdp),), (FF // fsdp,))

    grad_out, step_out, mom_out, sq_out = adamw(m_out, v_out, sum_out)
    grad_in, step_in, mom_in, sq_in = adamw(m_in, v_in, sum_in)
    columns = []
    for k in range(3):
        columns += [sum_mix[:, k * PART : (k + 1) * PART].astype(f32), sum_qkv[:, k * PART : (k + 1) * PART].astype(f32)]
    sum_attn = jnp.concatenate(columns + [sum_mix[:, 3 * PART :].astype(f32)], axis=1)
    grad_attn, step_attn, mom_attn, sq_attn = adamw(m_attn, v_attn, sum_attn)
    grad_bin, step_bin, mom_bin, sq_bin = adamw(m_bin, v_bin, sum_bin)
    grad_vecs, step_vecs, mom_vecs, sq_vecs = adamw(m_vecs, v_vecs, sum_vecs)
    return (
        output,
        grad_tokens,
        grad_attn,
        grad_in,
        grad_out,
        grad_bin,
        grad_vecs,
        step_attn,
        step_in,
        step_out,
        step_bin,
        step_vecs,
        mom_attn,
        mom_in,
        mom_out,
        mom_bin,
        mom_vecs,
        sq_attn,
        sq_in,
        sq_out,
        sq_bin,
        sq_vecs,
    )


def solution(mesh):
    rows, row, col = P(("rep", "fsdp"), None), P("fsdp", None), P(None, "fsdp")
    flat = P("fsdp")
    state = (row, row, row, flat, col)
    return jax.shard_map(
        functools.partial(local, mesh.shape["fsdp"], mesh.shape["rep"]),
        mesh=mesh,
        in_specs=(rows, rows, P(("rep", "fsdp"))) + state * 3,
        out_specs=(rows, rows) + state * 4,
        check_vma=False,
    )
```
